32 devices in a mesh: head: 4 (over y, core), seq: 8 (over z, x).
Axes of the slice: x: 2, y: 2, z: 4, core: 2. Of those that a mesh axis runs over, the one named last changes fastest.
Arguments:
- layer_input: bfloat16 [1024, 4096], P('seq', 'head'), may hold values from -6 to 6
- receptance: bfloat16 [1024, 4096], P('seq', 'head'), may hold values from -6 to 6
- key_act: bfloat16 [1024, 4096], P('seq', 'head'), may hold values from -0.75 to 0.75
- value_act: bfloat16 [1024, 4096], P('seq', 'head'), may hold values from -6 to 6
- attention_result_sensitivity: bfloat16 [1024, 4096], P('seq', 'head'), may hold values from -0.625 to 0.625
- time_first: float32 [64, 64], P('head'), may hold values from -1 to 1
- decay_exponent_base: float32 [4096], P('head'), may hold values from -9 to -3.4
- decay_shift_mix: float32 [4096], P('head'), may hold values from 0 to 1
- mix_rkv: float32 [3, 4096], replicated, may hold values from 0 to 1
- decay_adapter_down: float32 [4096, 128], P('head'), may hold values from -0.09375 to 0.09375
- decay_adapter_up: float32 [128, 4096], P(None, 'head'), may hold values from -1 to 1
- proj_weights: bfloat16 [3, 4096, 4096], P(None, 'seq', 'head'), may hold values from -0.09375 to 0.09375
Outputs:
- stratum_source_sensitivity: bfloat16 [1024, 4096], P('seq', 'head')
- decay_down_grad: float32 [4096, 128], P('head')
- decay_up_grad: float32 [128, 4096], P(None, 'head')
- decay_base_grad: float32 [4096], P('head')
- time_first_grad: float32 [64, 64], P('head')
The draws below stay inside these ranges and needn't reach their ends.
All inputs are finite; a program needn't handle non-finite values.
Results may differ from the reference program's by a relative error of at most 0.018.
Values may be sent and summed in bfloat16 or wider, within the bound.
No kernel may reach another device: no remote copies, remote signals or barrier semaphores. Data moves between devices by JAX's collectives and lax.ppermute only.
A program may use at most 128 MiB of HBM per device.

```python
import jax
import jax.numpy as jnp
from jax import lax

MODEL_WIDTH = 4096
HEADS = 64
HS = 64
ADAPTER_RANK = 128
TOK_DEV = 128
TOKENS = 1024
N_HEAD = 4


def steps_of(key, extent, split, smallest, largest):
    def one(dim, blocks):
        heights = jax.random.uniform(jax.random.fold_in(jax.random.fold_in(key, 6), dim), (blocks,), jnp.float32, smallest / len(split), largest / len(split))
        return jnp.repeat(jnp.exp(heights), extent[dim] // blocks).reshape((-1,) + (1,) * (len(extent) - dim - 1))

    factor_of = one(*split[0])
    for cut in split[1:]:
        factor_of = factor_of * one(*cut)
    return factor_of


def gaussian(stream_key, extent, deviation, reach, cuts=(), held_as=jnp.bfloat16):
    gain = steps_of(stream_key, extent, cuts, -0.22, 0.18) if cuts else 1.0
    entries = jax.random.normal(stream_key, extent, jnp.float32) * deviation * gain
    return jnp.minimum(jnp.maximum(entries, -reach), reach).astype(held_as)


def setup_inputs(seed: int = 0) -> dict:
    key_of = jax.random.split(jax.random.key(seed), 13)
    return {
        "layer_input": gaussian(key_of[0], (TOKENS, MODEL_WIDTH), 1.0, 6.0, ((0, 8), (1, 4))),
        "receptance": gaussian(key_of[1], (TOKENS, MODEL_WIDTH), 1.0, 6.0, ((0, 8), (1, 4))),
        "key_act": gaussian(key_of[2], (TOKENS, MODEL_WIDTH), 0.125, 0.75, ((0, 8), (1, 4))),
        "value_act": gaussian(key_of[3], (TOKENS, MODEL_WIDTH), 1.0, 6.0, ((0, 8), (1, 4))),
        "attention_result_sensitivity": gaussian(key_of[4], (TOKENS, MODEL_WIDTH), 0.1, 0.625, ((0, 8), (1, 4))),
        "time_first": jnp.clip(jax.random.uniform(key_of[5], (HEADS, HS), jnp.float32, -1.0, 1.0) * steps_of(key_of[5], (HEADS, HS), ((0, 4),), -0.4, 0.0), -1.0, 1.0),
        "decay_exponent_base": jnp.clip(-9.0 + 5.6 * jax.random.uniform(key_of[6], (MODEL_WIDTH,), jnp.float32) ** steps_of(key_of[6], (MODEL_WIDTH,), ((0, 4),), -0.2, 0.2), -9.0, -3.4),
        "decay_shift_mix": jnp.clip(1.0 * jax.random.uniform(key_of[7], (MODEL_WIDTH,), jnp.float32) ** steps_of(key_of[7], (MODEL_WIDTH,), ((0, 4),), -0.2, 0.2), 0.0, 1.0),
        "mix_rkv": jnp.clip(jax.random.uniform(key_of[8], (3, MODEL_WIDTH), jnp.float32, 0.0, 1.0), 0.0, 1.0),
        "decay_adapter_down": gaussian(key_of[9], (MODEL_WIDTH, ADAPTER_RANK), MODEL_WIDTH ** -0.5, 0.09375, ((0, 4),), jnp.float32),
        "decay_adapter_up": gaussian(key_of[10], (ADAPTER_RANK, MODEL_WIDTH), 0.18, 1.0, ((1, 4),), jnp.float32),
        "proj_weights": gaussian(key_of[11], (3, MODEL_WIDTH, MODEL_WIDTH), MODEL_WIDTH ** -0.5, 0.09375, ((1, 8), (2, 4))),
    }


EXACT_ARITHMETIC = lax.Precision.HIGHEST

def onward_scan_loop(gate_matrix, lookup_matrix, payload_matrix, fading_natural_scale, initial_reward):

    def advance(memory_matrix_handed, sequence_entries):
        present_gate_vector, key_now, val_now, logd_now = sequence_entries
        lookup_payload_product = key_now[:, :, None] * val_now[:, None, :]
        attention_result = jnp.einsum('uk,ukv->uv', present_gate_vector, memory_matrix_handed + initial_reward[:, :, None] * lookup_payload_product, precision=EXACT_ARITHMETIC)
        memory_matrix_handed = jnp.exp(logd_now)[:, :, None] * memory_matrix_handed + lookup_payload_product
        return (memory_matrix_handed, attention_result)

    def segment(memory_matrix_handed, sequence_entries):
        return lax.scan(advance, memory_matrix_handed, sequence_entries)
    length_all, head_count, head_size = gate_matrix.shape
    pieces = length_all // TOK_DEV

    def to_blocks(array):
        return array.reshape(pieces, TOK_DEV, head_count, head_size)
    initial = jnp.zeros((head_count, head_size, head_size), gate_matrix.dtype)
    unused, outputs = lax.scan(jax.checkpoint(segment), initial, (to_blocks(gate_matrix), to_blocks(lookup_matrix), to_blocks(payload_matrix), to_blocks(fading_natural_scale)))
    return outputs.reshape(length_all, head_count, head_size)

def reference(layer_input, receptance, key_act, value_act, attention_result_sensitivity, time_first, decay_exponent_base, decay_shift_mix, mix_rkv, decay_adapter_down, decay_adapter_up, proj_weights):
    features = layer_input.astype(jnp.float32)
    length_all = features.shape[0]
    previous = jnp.concatenate([jnp.zeros((1, MODEL_WIDTH), jnp.float32), features[:-1]], 0)
    decay_input = features + decay_shift_mix * (previous - features)
    adapter_middle = jnp.tanh(jnp.dot(decay_input, decay_adapter_down, precision=EXACT_ARITHMETIC))
    fading_natural_scale = -jnp.exp(decay_exponent_base + jnp.dot(adapter_middle, decay_adapter_up, precision=EXACT_ARITHMETIC))

    def attention_partition(array):
        return array.astype(jnp.float32).reshape(length_all, HEADS, HS)
    unused_out, reverse_mode_map = jax.vjp(onward_scan_loop, attention_partition(receptance), attention_partition(key_act), attention_partition(value_act), fading_natural_scale.reshape(length_all, HEADS, HS), time_first)
    gate_sensitivity, lookup_sensitivity, payload_sensitivity, fading_scale_sensitivity, reward_sensitivity = reverse_mode_map(attention_partition(attention_result_sensitivity))
    preactivation_gradient = fading_scale_sensitivity.reshape(length_all, MODEL_WIDTH) * fading_natural_scale
    raising_matrix_sensitivity = jnp.dot(adapter_middle.T, preactivation_gradient, precision=EXACT_ARITHMETIC)
    floor_rate_sensitivity = lax.optimization_barrier(jnp.sum(preactivation_gradient, 0))
    middle_gradient = jnp.dot(preactivation_gradient, decay_adapter_up.T, precision=EXACT_ARITHMETIC) * (1.0 - adapter_middle * adapter_middle)
    lowering_matrix_sensitivity = jnp.dot(decay_input.T, middle_gradient, precision=EXACT_ARITHMETIC)
    decay_input_gradient = jnp.dot(middle_gradient, decay_adapter_down.T, precision=EXACT_ARITHMETIC)
    projected = jnp.stack([gate_sensitivity.reshape(length_all, MODEL_WIDTH), lookup_sensitivity.reshape(length_all, MODEL_WIDTH), payload_sensitivity.reshape(length_all, MODEL_WIDTH)]).astype(jnp.bfloat16)
    group_columns = MODEL_WIDTH // N_HEAD

    def add_group(index, accum):
        token_offset = (index * group_columns).astype(jnp.int32)
        own_portion = jnp.zeros((length_all, MODEL_WIDTH), jnp.float32)
        previous_portion = jnp.zeros((length_all, MODEL_WIDTH), jnp.float32)
        for member in range(3):
            piece_grad = lax.dynamic_slice_in_dim(projected[member], token_offset, group_columns, 1).astype(jnp.float32)
            piece_weight = lax.dynamic_slice_in_dim(proj_weights[member], token_offset, group_columns, 1).astype(jnp.float32)
            term = jnp.dot(piece_grad, piece_weight.T, precision=EXACT_ARITHMETIC)
            own_portion = own_portion + (1.0 - mix_rkv[member]) * term
            previous_portion = previous_portion + mix_rkv[member] * term
        adapter_columns = lax.dynamic_slice_in_dim(decay_input_gradient, token_offset, group_columns, 1)
        mixed_columns = lax.dynamic_slice_in_dim(decay_shift_mix, token_offset, group_columns, 0)
        own_columns = lax.dynamic_slice_in_dim(own_portion, token_offset, group_columns, 1) + (1.0 - mixed_columns) * adapter_columns
        own_portion = lax.dynamic_update_slice_in_dim(own_portion, own_columns, token_offset, 1)
        previous_columns = lax.dynamic_slice_in_dim(previous_portion, token_offset, group_columns, 1) + mixed_columns * adapter_columns
        previous_portion = lax.dynamic_update_slice_in_dim(previous_portion, previous_columns, token_offset, 1)
        group_term = own_portion + jnp.concatenate([previous_portion[1:], jnp.zeros((1, MODEL_WIDTH), jnp.float32)], 0)
        rounded = lax.optimization_barrier(group_term.astype(jnp.bfloat16))
        return accum + rounded.astype(jnp.float32)
    accumulated_contributions = lax.fori_loop(0, N_HEAD, add_group, jnp.zeros((length_all, MODEL_WIDTH), jnp.float32))
    return (accumulated_contributions.astype(jnp.bfloat16), lowering_matrix_sensitivity, raising_matrix_sensitivity, floor_rate_sensitivity, reward_sensitivity)
```

```python
import jax
import jax.numpy as jnp
import numpy as np
from jax import lax
from jax.experimental import pallas as pl
from jax.experimental.pallas import tpu as pltpu
from jax.sharding import PartitionSpec as P

F32 = jnp.float32
BF16 = jnp.bfloat16
EXACT = lax.Precision.HIGHEST
PAIR = 128
NN = (((1,), (0,)), ((), ()))
NT = (((1,), (1,)), ((), ()))
TN = (((0,), (0,)), ((), ()))


def mm(a, b, dims=NN):
    return lax.dot_general(a, b, dims, preferred_element_type=F32)


def halves(a):
    hi = a.astype(BF16)
    return hi, (a - hi.astype(F32)).astype(BF16)


def low_lanes(shape, half):
    return lax.broadcasted_iota(jnp.int32, shape, len(shape) - 1) < half


def block_rows(a, half):
    low = low_lanes(a.shape, half)
    zero = jnp.zeros_like(a)
    return jnp.concatenate([jnp.where(low, a, zero), jnp.where(low, zero, a)], 0)


def fold(a, half):
    rows = a.shape[0] // 2
    return jnp.where(low_lanes((rows, a.shape[1]), half), a[:rows], a[rows:])


def sum_matrix(rows):
    t = np.arange(rows)
    both = np.concatenate([t[:, None] > t[None, :], t[:, None] < t[None, :]], 0)
    return np.concatenate([both, both], 1).astype(np.float32)


def level_matrix(rows):
    t = np.arange(rows)
    parts = []
    m = 1
    while m < rows:
        mid = (t // (2 * m)) * 2 * m + m
        right = t >= mid
        u = t[None, :]
        take_right = (u >= mid[:, None]) & (u < t[:, None])
        take_left = (u > t[:, None]) & (u < mid[:, None])
        parts.append(np.where(right[:, None], take_right, take_left))
        m *= 2
    both = np.concatenate(parts, 0)
    return np.concatenate([both, both], 1).astype(np.float32)


def cumulative_matrix(rows):
    t = np.arange(rows)
    strict = (t[:, None] < t[None, :]).astype(np.float32)
    full = (t[:, None] <= t[None, :]).astype(np.float32)
    return np.concatenate([strict, strict, -full, -full], 1)


def decay_kernel(head, count, *refs):
    pres = refs[:count]
    base, up, r, k, v, dy, sums, lora, lora_t, w_out, end, st, gt = refs[count:]
    rows = r.shape[0]
    total = pres[0][...]
    for pre in pres[1:]:
        total = total + pre[...]
    mid = jnp.tanh(total)
    lora[...] = mid
    lora_t[...] = mid.T.astype(BF16)
    w = -jnp.exp(
        base[...] + lax.dot_general(mid, up[...], NN, precision=EXACT, preferred_element_type=F32)
    )
    w_out[...] = w
    hi, lo = halves(w)
    args = mm(sums[...], jnp.concatenate([hi, lo], 0))
    before, after = args[:rows], args[rows:]
    end[...] = before[rows - 1 :] + w[rows - 1 :]
    kf = (k[...].astype(F32) * jnp.exp(after)).astype(BF16)
    rb = (r[...].astype(F32) * jnp.exp(before)).astype(BF16)
    for p in range(r.shape[1] // PAIR):
        cols = slice(p * PAIR, (p + 1) * PAIR)
        st[:, cols] = fold(mm(v[:, cols], kf[:, cols], TN), head)
        gt[:, cols] = fold(mm(dy[:, cols], rb[:, cols], TN), head)


def inner_kernel(head, r, k, v, dy, w, u, levels, gr_out, gk_out, gv_out, self_out, du_out):
    rows = r.shape[0]
    rf, kf = r[...].astype(F32), k[...].astype(F32)
    vf, dyf = v[...].astype(F32), dy[...].astype(F32)
    hi, lo = halves(w[...])
    decay = jnp.exp(mm(levels[...], jnp.concatenate([hi, lo], 0)))
    row = lax.broadcasted_iota(jnp.int32, (rows, PAIR), 0)
    row2 = lax.broadcasted_iota(jnp.int32, (rows, 2 * rows), 0)
    col2 = lax.broadcasted_iota(jnp.int32, (rows, 2 * rows), 1)
    apart = row2 ^ (col2 & (rows - 1))
    dydy = block_rows(dy[...], head)
    pairs = mm(dy[...], block_rows(v[...], head), NT)
    pairs_t = mm(v[...], dydy, NT)
    gr = jnp.zeros((rows, PAIR), F32)
    gk = jnp.zeros((rows, PAIR), F32)
    scores_t = jnp.zeros((rows, 2 * rows), F32)
    m, level = 1, 0
    while m < rows:
        d = decay[level * rows : (level + 1) * rows]
        right = (row & m) != 0
        rd = jnp.where(right, rf * d, 0.0).astype(BF16)
        kd = jnp.where(right, 0.0, kf * d).astype(BF16)
        kk, rr = block_rows(kd, head), block_rows(rd, head)
        near = apart < 2 * m
        a = mm(kd, rr, NT)
        scores_t = scores_t + jnp.where(near, a, 0.0)
        here = jnp.where(near, pairs, 0.0).astype(BF16)
        here_t = jnp.where(near, pairs_t, 0.0).astype(BF16)
        gr = gr + jnp.where(right, d * mm(here, kk), 0.0)
        gk = gk + jnp.where(right, 0.0, d * mm(here_t, rr))
        m, level = 2 * m, level + 1
    lane_r = lax.broadcasted_iota(jnp.int32, (2 * PAIR, PAIR), 0) & (PAIR - 1)
    lane_c = lax.broadcasted_iota(jnp.int32, (2 * PAIR, PAIR), 1)
    ones = jnp.where((lane_r < head) == (lane_c < head), 1.0, 0.0).astype(BF16)
    sh, sl = halves(dyf * vf)
    own = mm(jnp.concatenate([sh, sl], 1), ones)
    bh, bl = halves(rf * u[...] * kf)
    bonus = mm(jnp.concatenate([bh, bl], 1), ones)
    gr_out[...] = gr
    gk_out[...] = gk
    gv_out[...] = mm(scores_t.astype(BF16), dydy) + bonus * dyf
    self_out[...] = own
    du_out[...] = jnp.sum(rf * kf * own, 0, keepdims=True)


def outer_kernel(
    head, r, k, v, dy, w, u, gr0, gk0, gv0, own, st_in, gt_in, st, end, up, lora_t, sums, cums,
    proj, up_grad, base_grad, mid_grad,
):
    rows = r.shape[0]
    rf, kf = r[...].astype(F32), k[...].astype(F32)
    wv = w[...]
    hi, lo = halves(wv)
    decay = jnp.exp(mm(sums[...], jnp.concatenate([hi, lo], 0)))
    eb, ee = decay[:rows], decay[rows:]
    sb = block_rows(st_in[...].astype(BF16), head)
    gb = block_rows(gt_in[...].astype(BF16), head)
    gr = gr0[...] + eb * mm(dy[...], sb)
    gk = gk0[...] + ee * mm(v[...], gb)
    gv = gv0[...] + mm((kf * ee).astype(BF16), gb, NT)
    at_end = jnp.sum(gt_in[...] * (jnp.exp(end[...]) * st_in[...] + st[...]), 0, keepdims=True)
    ah, al = halves(rf * gr)
    bh, bl = halves(kf * gk)
    gl = mm(cums[...], jnp.concatenate([ah, al, bh, bl], 0)) + at_end
    gp = gl * wv
    s = own[...] * u[...]
    proj[0] = (gr + kf * s).astype(BF16)
    proj[1] = (gk + rf * s).astype(BF16)
    proj[2] = gv.astype(BF16)
    gpb = gp.astype(BF16)
    up_grad[...] = mm(lora_t[...], gpb)
    base_grad[...] = jnp.sum(gp, 0, keepdims=True)

    @pl.when(pl.program_id(0) == 0)
    def _():
        mid_grad[...] = jnp.zeros_like(mid_grad)

    mid_grad[...] += mm(gpb, up[...].astype(BF16), NT)


def project_kernel(ring, tiles, place, *refs):
    blocks = refs[:ring]
    edge, w_own, w_far, mix, out = refs[ring:]
    rows = blocks[0].shape[1]
    step = pl.program_id(0)

    def product(weights):
        ms = [mix[m : m + 1, :] for m in range(3)]
        tail = sum(ms[m] * mm(edge[m], weights[m], NT) for m in range(3))
        for q in range(ring):
            own = prior = None
            for m in range(3):
                term = mm(blocks[q][m], weights[m], NT)
                later = ms[m] * term
                own = term - later if m == 0 else own + (term - later)
                prior = later if m == 0 else prior + later
            last = lax.broadcasted_iota(jnp.int32, prior.shape, 0) == rows - 1
            moved = jnp.where(last, tail[q : q + 1], pltpu.roll(prior, rows - 1, 0))
            slot = lax.rem(place[1] - q - place[2] + 2 * ring, ring)
            out[slot] = (own + moved).astype(BF16)

    @pl.when(step < tiles)
    def _():
        product(w_own)

    @pl.when(step >= tiles)
    def _():
        product(w_far)


def per_device(
    layer_input, receptance, key_act, value_act, attention_result_sensitivity, time_first,
    decay_exponent_base, decay_shift_mix, mix_rkv, decay_adapter_down, decay_adapter_up, proj_weights,
):
    rows, cols = layer_input.shape
    heads, head = time_first.shape
    rank = decay_adapter_down.shape[1]
    n_seq, n_head = lax.axis_size("seq"), lax.axis_size("head")
    inner = n_seq // n_head
    ring = n_seq // inner
    pairs = cols // PAIR
    seq, hd = lax.axis_index("seq"), lax.axis_index("head")
    r, k, v, dy = receptance, key_act, value_act, attention_result_sensitivity

    def shift(a, distance):
        return lax.ppermute(
            a, "seq", [(i - distance, i) for i in range(n_seq) if 0 <= i - distance < n_seq]
        )

    def head_parts(a):
        return [a] + [
            lax.ppermute(a, "head", [(i, (i + d) % n_head) for i in range(n_head)])
            for d in range(1, n_head)
        ]

    weights_far = lax.ppermute(proj_weights, "seq", [(i, i ^ 1) for i in range(n_seq)])

    carried = shift(layer_input[rows - 1 :], 1).astype(F32)
    features = layer_input.astype(F32)
    previous = jnp.concatenate([carried, features[:-1]], 0)
    decay_input = features + decay_shift_mix * (previous - features)
    pres = head_parts(jnp.dot(decay_input, decay_adapter_down, precision=EXACT))

    sums = jnp.asarray(sum_matrix(rows), BF16)
    levels = jnp.asarray(level_matrix(rows), BF16)
    cums = jnp.asarray(cumulative_matrix(rows), BF16)
    u = time_first.reshape(1, cols)

    def shape(s, t=F32):
        return jax.ShapeDtypeStruct(s, t)

    lora, lora_t, w, end, st, gt = pl.pallas_call(
        lambda *refs: decay_kernel(head, n_head, *refs),
        out_shape=[
            shape((rows, rank)), shape((rank, rows), BF16), shape((rows, cols)), shape((1, cols)),
            shape((head, cols)), shape((head, cols)),
        ],
        compiler_params=pltpu.CompilerParams(vmem_limit_bytes=32 * 2**20),
        name="decay_and_states",
    )(*pres, decay_exponent_base.reshape(1, cols), decay_adapter_up, r, k, v, dy, sums)

    def col_block(n):
        return pl.BlockSpec((n, PAIR), lambda p: (0, p))

    def whole(s):
        return pl.BlockSpec(s, lambda p: (0,) * len(s))

    tok = col_block(rows)
    gr0, gk0, gv0, own, du = pl.pallas_call(
        lambda *refs: inner_kernel(head, *refs),
        grid=(pairs,),
        in_specs=[tok] * 5 + [col_block(1), whole(levels.shape)],
        out_specs=[tok] * 4 + [col_block(1)],
        out_shape=[shape((rows, cols))] * 4 + [shape((1, cols))],
        compiler_params=pltpu.CompilerParams(vmem_limit_bytes=32 * 2**20),
        name="inside_chunk",
    )(r, k, v, dy, w, u, levels)

    def pack(state, decay):
        hi, lo = halves(decay)
        eight = (8, cols)
        return jnp.concatenate(
            [state.astype(BF16), jnp.broadcast_to(hi, eight), jnp.broadcast_to(lo, eight)], 0
        )

    def scan(state, sign):
        entry, entry_decay = jnp.zeros_like(state), jnp.zeros_like(end)
        run, run_decay = state, end
        d = 1
        while d < n_seq:
            got = shift(pack(run, run_decay), sign * d).astype(F32)
            got_state, got_decay = got[:head], got[head : head + 1] + got[head + 8 : head + 9]
            entry = got_state * jnp.exp(entry_decay) + entry
            entry_decay = entry_decay + got_decay
            run = entry * jnp.exp(end) + state
            run_decay = entry_decay + end
            d *= 2
        return entry

    st_in = scan(st, 1)
    gt_in = scan(gt, -1)

    proj, up_grad, base_grad, mid_grad = pl.pallas_call(
        lambda *refs: outer_kernel(head, *refs),
        grid=(pairs,),
        in_specs=[tok] * 5 + [col_block(1)] + [tok] * 4 + [col_block(head)] * 3
        + [col_block(1), col_block(rank), whole((rank, rows)), whole(sums.shape), whole(cums.shape)],
        out_specs=[
            pl.BlockSpec((3, rows, PAIR), lambda p: (0, 0, p)), col_block(rank), col_block(1),
            whole((rows, rank)),
        ],
        out_shape=[
            shape((3, rows, cols), BF16), shape((rank, cols)), shape((1, cols)), shape((rows, rank)),
        ],
        compiler_params=pltpu.CompilerParams(vmem_limit_bytes=32 * 2**20),
        name="across_chunks",
    )(r, k, v, dy, w, u, gr0, gk0, gv0, own, st_in, gt_in, st, end, decay_adapter_up, lora_t, sums, cums)

    def around(step):
        return [(i, (i + inner * step) % n_seq) for i in range(n_seq)]

    blocks = [proj]
    for _ in range(ring - 1):
        blocks.append(lax.ppermute(blocks[-1], "seq", around(1)))
    first = proj[:, :1]
    edges = []
    for q in range(ring):
        route = [
            (s + 1, (s + inner * q) % n_seq) for s in range(n_seq) if s + 1 < n_seq
        ]
        edges.append(lax.ppermute(first, "seq", route))
    pad = -ring % 16
    edge = jnp.concatenate(edges + [jnp.zeros((3, pad, cols), BF16)], 1)

    up_grad, base_grad, du = lax.psum((up_grad, base_grad, du), "seq")
    mid_grad = sum(head_parts(mid_grad)) * (1.0 - lora * lora)
    down_grad = lax.psum(jnp.dot(decay_input.T, mid_grad, precision=EXACT), "seq")
    grad_in = jnp.dot(mid_grad, decay_adapter_down.T, precision=EXACT)
    grad_next = jnp.concatenate([grad_in[1:], shift(grad_in[:1], -1)], 0)
    adapter_term = (1.0 - decay_shift_mix) * grad_in + decay_shift_mix * grad_next

    far_rows = proj_weights.shape[1]
    tile = min(far_rows, 256)
    tiles = far_rows // tile

    def column(i, place):
        side = jnp.where(i < tiles, place[0], 1 - place[0])
        return side * tiles + lax.rem(i, tiles)

    place = jnp.stack([lax.rem(seq, inner), seq // inner, hd]).astype(jnp.int32)
    partial_out = pl.pallas_call(
        lambda *refs: project_kernel(ring, tiles, *refs),
        grid_spec=pltpu.PrefetchScalarGridSpec(
            num_scalar_prefetch=1,
            grid=(inner * tiles,),
            in_specs=[pl.BlockSpec((3, rows, cols), lambda i, place: (0, 0, 0))] * ring
            + [
                pl.BlockSpec(edge.shape, lambda i, place: (0, 0, 0)),
                pl.BlockSpec((3, tile, cols), lambda i, place: (0, jnp.minimum(i, tiles - 1), 0)),
                pl.BlockSpec((3, tile, cols), lambda i, place: (0, jnp.maximum(i - tiles, 0), 0)),
                pl.BlockSpec(
                    (3, tile), lambda i, place: (0, place[1] * inner * tiles + column(i, place))
                ),
            ],
            out_specs=pl.BlockSpec((ring, rows, tile), lambda i, place: (0, 0, column(i, place))),
        ),
        out_shape=shape((ring, rows, cols), BF16),
        compiler_params=pltpu.CompilerParams(vmem_limit_bytes=40 * 2**20),
        name="projections",
    )(place, *blocks, edge, proj_weights, weights_far, mix_rkv)

    total = partial_out[0].astype(F32)
    for d in range(1, n_head):
        got = lax.ppermute(
            partial_out[d], "head", [(i, (i + d) % n_head) for i in range(n_head)]
        )
        total = total + got.astype(F32)
    swap = [
        (h * n_seq + z * inner + x, z * n_seq + h * inner + x)
        for h in range(n_head) for z in range(ring) for x in range(inner)
    ]
    summed = lax.ppermute(total.astype(BF16), ("head", "seq"), swap)
    result = (summed.astype(F32) + adapter_term).astype(BF16)
    return (result, down_grad, up_grad, base_grad.reshape(cols), du.reshape(heads, head))


def solution(mesh):
    return jax.shard_map(
        per_device,
        mesh=mesh,
        in_specs=(
            P("seq", "head"), P("seq", "head"), P("seq", "head"), P("seq", "head"), P("seq", "head"),
            P("head", None), P("head"), P("head"), P(), P("head", None), P(None, "head"),
            P(None, "seq", "head"),
        ),
        out_specs=(P("seq", "head"), P("head", None), P(None, "head"), P("head"), P("head", None)),
        check_vma=False,
    )
```

```python
import jax
import jax.numpy as jnp
import numpy as np
from jax import lax
from jax.experimental import pallas as pl
from jax.experimental.pallas import tpu as pltpu
from jax.sharding import PartitionSpec as P

F32 = jnp.float32
BF16 = jnp.bfloat16
PAIR = 128
VMEM = 56 * 2**20
NN = (((1,), (0,)), ((), ()))
NT = (((1,), (1,)), ((), ()))
TN = (((0,), (0,)), ((), ()))


def mm(a, b, dims=NN):
    return lax.dot_general(a, b, dims, preferred_element_type=F32)


def halves(a):
    hi = a.astype(BF16)
    return hi, (a - hi.astype(F32)).astype(BF16)


def low_lanes(shape, half):
    return lax.broadcasted_iota(jnp.int32, shape, len(shape) - 1) < half


def block_rows(a, half):
    low = low_lanes(a.shape, half)
    zero = jnp.zeros_like(a)
    return jnp.concatenate([jnp.where(low, a, zero), jnp.where(low, zero, a)], 0)


def fold(a, half):
    rows = a.shape[0] // 2
    return jnp.where(low_lanes((rows, a.shape[1]), half), a[:rows], a[rows:])


def sum_matrix(rows):
    t = np.arange(rows)
    both = np.concatenate([t[:, None] > t[None, :], t[:, None] < t[None, :]], 0)
    return np.concatenate([both, both], 1).astype(np.float32)


def level_matrix(rows):
    t = np.arange(rows)
    parts = []
    m = 1
    while m < rows:
        mid = (t // (2 * m)) * 2 * m + m
        right = t >= mid
        u = t[None, :]
        take_right = (u >= mid[:, None]) & (u < t[:, None])
        take_left = (u > t[:, None]) & (u < mid[:, None])
        parts.append(np.where(right[:, None], take_right, take_left))
        m *= 2
    both = np.concatenate(parts, 0)
    return np.concatenate([both, both], 1).astype(np.float32)


def cumulative_matrix(rows):
    t = np.arange(rows)
    strict = (t[:, None] < t[None, :]).astype(np.float32)
    full = (t[:, None] <= t[None, :]).astype(np.float32)
    return np.concatenate([strict, strict, -full, -full], 1)


def split_rows(a):
    hi, lo = halves(a)
    return jnp.broadcast_to(hi, (8, a.shape[1])), jnp.broadcast_to(lo, (8, a.shape[1]))


def joined(msg, at):
    return msg[at : at + 1].astype(F32) + msg[at + 8 : at + 9].astype(F32)


def mm3(a, b, dims=NN):
    ah, al = halves(a)
    bh, bl = halves(b)
    return mm(ah, bh, dims) + (mm(ah, bl, dims) + mm(al, bh, dims))


def mixed_input(x, carried, mix):
    features = x[...].astype(F32)
    row = lax.broadcasted_iota(jnp.int32, features.shape, 0)
    previous = jnp.where(row == 0, carried[...].astype(F32), pltpu.roll(features, 1, 0))
    return features + mix[...] * (previous - features)


def adapter_kernel(x, carried, mix, down, pre):
    pre[...] = mm3(mixed_input(x, carried, mix), down[...])


def decay_kernel(head, count, *refs):
    pres = refs[:count]
    base, up, r, k, v, dy, sums, lora, lora_t, w_out, eb, ee, end, st, msg = refs[count:]
    rows = r.shape[0]
    total = pres[0][...]
    for pre in pres[1:]:
        total = total + pre[...]
    mid = jnp.tanh(total)
    lora[...] = mid
    lora_t[...] = mid.T.astype(BF16)
    w = -jnp.exp(base[...] + mm3(mid, up[...]))
    w_out[...] = w
    hi, lo = halves(w)
    args = mm(sums[...], jnp.concatenate([hi, lo], 0))
    before, after = args[:rows], args[rows:]
    final = before[rows - 1 :] + w[rows - 1 :]
    end[...] = final
    from_start, to_end = jnp.exp(before), jnp.exp(after)
    eb[...] = from_start
    ee[...] = to_end
    kf = (k[...].astype(F32) * to_end).astype(BF16)
    rb = (r[...].astype(F32) * from_start).astype(BF16)
    for p in range(r.shape[1] // PAIR):
        cols = slice(p * PAIR, (p + 1) * PAIR)
        state = fold(mm(v[:, cols], kf[:, cols], TN), head)
        st[:, cols] = state
        msg[:head, cols] = state.astype(BF16)
        msg[head : 2 * head, cols] = fold(mm(dy[:, cols], rb[:, cols], TN), head).astype(BF16)
    msg[2 * head : 2 * head + 8], msg[2 * head + 8 :] = split_rows(final)


def pair_kernel(head, ring, place, own, far, *outs):
    late = place[0] == 1
    dec_own, dec_far = joined(own, 2 * head), joined(far, 2 * head)
    eo, ef = jnp.exp(dec_own), jnp.exp(dec_far)
    st_own, st_far = own[:head].astype(F32), far[:head].astype(F32)
    gt_own, gt_far = own[head : 2 * head].astype(F32), far[head : 2 * head].astype(F32)
    state = jnp.where(late, st_own + eo * st_far, st_far + ef * st_own).astype(BF16)
    grad = jnp.where(late, gt_far + ef * gt_own, gt_own + eo * gt_far).astype(BF16)
    hi, lo = split_rows(dec_own + dec_far)
    for d in range(1, ring):
        out = outs[d - 1]
        ahead = place[1] + d < ring

        @pl.when(ahead)
        def _():
            out[:head] = state

        @pl.when(jnp.logical_not(ahead))
        def _():
            out[:head] = grad

        out[head : head + 8] = hi
        out[head + 8 :] = lo


def inner_kernel(head, r, k, v, dy, w, u, levels, gr_out, gk_out, gv_out, self_out, du_out):
    rows, width = r.shape
    row = lax.broadcasted_iota(jnp.int32, (rows, PAIR), 0)
    row2 = lax.broadcasted_iota(jnp.int32, (rows, 2 * rows), 0)
    col2 = lax.broadcasted_iota(jnp.int32, (rows, 2 * rows), 1)
    apart = row2 ^ (col2 & (rows - 1))
    lane_r = lax.broadcasted_iota(jnp.int32, (2 * PAIR, PAIR), 0) & (PAIR - 1)
    lane_c = lax.broadcasted_iota(jnp.int32, (2 * PAIR, PAIR), 1)
    ones = jnp.where((lane_r < head) == (lane_c < head), 1.0, 0.0).astype(BF16)
    hi, lo = halves(w[...])
    decay = jnp.exp(mm(levels[...], jnp.concatenate([hi, lo], 0)))
    for p in range(width // PAIR):
        cols = slice(p * PAIR, (p + 1) * PAIR)
        rf, kf = r[:, cols].astype(F32), k[:, cols].astype(F32)
        vf, dyf = v[:, cols].astype(F32), dy[:, cols].astype(F32)
        dydy = block_rows(dy[:, cols], head)
        pairs = mm(dy[:, cols], block_rows(v[:, cols], head), NT)
        pairs_t = mm(v[:, cols], dydy, NT)
        gr = jnp.zeros((rows, PAIR), F32)
        gk = jnp.zeros((rows, PAIR), F32)
        scores_t = jnp.zeros((rows, 2 * rows), F32)
        m, level = 1, 0
        while m < rows:
            d = decay[level * rows : (level + 1) * rows, cols]
            right = (row & m) != 0
            rd = jnp.where(right, rf * d, 0.0).astype(BF16)
            kd = jnp.where(right, 0.0, kf * d).astype(BF16)
            kk, rr = block_rows(kd, head), block_rows(rd, head)
            near = apart < 2 * m
            a = mm(kd, rr, NT)
            scores_t = scores_t + jnp.where(near, a, 0.0)
            here = jnp.where(near, pairs, 0.0).astype(BF16)
            here_t = jnp.where(near, pairs_t, 0.0).astype(BF16)
            gr = gr + jnp.where(right, d * mm(here, kk), 0.0)
            gk = gk + jnp.where(right, 0.0, d * mm(here_t, rr))
            m, level = 2 * m, level + 1
        sh, sl = halves(dyf * vf)
        own = mm(jnp.concatenate([sh, sl], 1), ones)
        bh, bl = halves(rf * u[:, cols] * kf)
        bonus = mm(jnp.concatenate([bh, bl], 1), ones)
        gr_out[:, cols] = gr
        gk_out[:, cols] = gk
        gv_out[:, cols] = mm(scores_t.astype(BF16), dydy) + bonus * dyf
        self_out[:, cols] = own
        du_out[:, cols] = jnp.sum(rf * kf * own, 0, keepdims=True)


def outer_kernel(
    head, ring, place, r, k, v, dy, eb, ee, u, gr0, gk0, gv0, own, st, end, far, *refs
):
    msgs = refs[: ring - 1]
    proj, r_gr, k_gk, at_end = refs[ring - 1 :]
    width = r.shape[1]
    late, z = place[0] == 1, place[1]
    zero = jnp.zeros((head, width), F32)
    nothing = jnp.zeros((1, width), F32)
    state, grad, past, future = zero, zero, nothing, nothing
    for d in range(1, ring):
        msg = msgs[d - 1]
        live = d <= z
        state = state + jnp.where(live, jnp.exp(past) * msg[:head].astype(F32), 0.0)
        past = past + jnp.where(live, joined(msg, head), 0.0)
    for d in range(ring - 1, 0, -1):
        msg = msgs[d - 1]
        live = d > z
        grad = grad + jnp.where(live, jnp.exp(future) * msg[:head].astype(F32), 0.0)
        future = future + jnp.where(live, joined(msg, head), 0.0)
    ef = jnp.exp(joined(far, 2 * head))
    st_in = jnp.where(late, far[:head].astype(F32) + ef * state, state)
    gt_in = jnp.where(late, grad, far[head : 2 * head].astype(F32) + ef * grad)
    at_end[...] = jnp.sum(gt_in * (jnp.exp(end[...]) * st_in + st[...]), 0, keepdims=True)
    sb, gb = st_in.astype(BF16), gt_in.astype(BF16)
    for p in range(width // PAIR):
        cols = slice(p * PAIR, (p + 1) * PAIR)
        grads = block_rows(gb[:, cols], head)
        rf, kf = r[:, cols].astype(F32), k[:, cols].astype(F32)
        after = ee[:, cols]
        gr = gr0[:, cols] + eb[:, cols] * mm(dy[:, cols], block_rows(sb[:, cols], head))
        gk = gk0[:, cols] + after * mm(v[:, cols], grads)
        gv = gv0[:, cols] + mm((kf * after).astype(BF16), grads, NT)
        s = own[:, cols] * u[:, cols]
        proj[0, :, cols] = (gr + kf * s).astype(BF16)
        proj[1, :, cols] = (gk + rf * s).astype(BF16)
        proj[2, :, cols] = gv.astype(BF16)
        r_gr[:, cols] = rf * gr
        k_gk[:, cols] = kf * gk


def decay_grad_kernel(w, r_gr, k_gk, at_end, up, lora_t, cums, up_grad, base_grad, mid_grad):
    ah, al = halves(r_gr[...])
    bh, bl = halves(k_gk[...])
    gp = (mm(cums[...], jnp.concatenate([ah, al, bh, bl], 0)) + at_end[...]) * w[...]
    gpb = gp.astype(BF16)
    up_grad[...] = mm(lora_t[...], gpb)
    base_grad[...] = jnp.sum(gp, 0, keepdims=True)
    mid_grad[...] = mm(gpb, up[...].astype(BF16), NT)


def middle_kernel(count, place, x, carried, mix, down, lora, *refs):
    mids, sides, (keep, send, grad_in) = refs[:count], refs[count:-3], refs[-3:]
    total = mids[0][...]
    for part in mids[1:]:
        total = total + part[...]
    mid = total * (1.0 - lora[...] * lora[...])
    grad_in[...] = mm3(mid, down[...], NT)
    down_grad = mm3(mid.T, mixed_input(x, carried, mix))
    rank, half = mid.shape[1], x.shape[1] // 2
    wide = (8, half)
    late = place[0] == 1

    def choose(low, high, at, size):
        keep[at : at + size] = jnp.where(late, high, low).astype(BF16)
        send[at : at + size] = jnp.where(late, low, high).astype(BF16)

    up_low, up_high, base_low, base_high, du_low, du_high = [ref[...] for ref in sides]
    choose(up_low, up_high, 0, rank)
    choose(down_grad[:, :half], down_grad[:, half:], rank, rank)
    for at, low, high in ((0, base_low, base_high), (8, du_low, du_high)):
        choose(jnp.broadcast_to(low, wide), jnp.broadcast_to(high, wide), 2 * rank + at, 8)


def finish_kernel(rank, place, mine, theirs, up, down, base, du):
    late = place[0] == 1
    half = mine.shape[1]
    a, b = mine[...].astype(F32), theirs[...].astype(F32)
    for at, value in ((0, jnp.where(late, b, a)), (half, jnp.where(late, a, b))):
        here = slice(at, at + half)
        up[:, here] = value[:rank]
        down[here] = value[rank : 2 * rank].T
        base[:, here] = value[2 * rank : 2 * rank + 1]
        du[:, here] = value[2 * rank + 8 : 2 * rank + 9]


def project_kernel(count, ring, place, *refs):
    lows, highs = refs[:count], refs[count : 2 * count]
    w_own, w_far0, w_far1, mix = refs[2 * count : 2 * count + 4]
    rest, (own, prior, low_tail, high_tail) = refs[2 * count + 4 : -4], refs[-4:]
    final = count == 1
    done, outs = (rest[: ring - 1], rest[ring - 1 :]) if final else ((), rest)
    rows, width = lows[0].shape[1:]
    side, m = pl.program_id(0), pl.program_id(1)
    mains = count * rows

    @pl.when(m == 0)
    def _():
        for ref in (own, prior, low_tail, high_tail):
            ref[...] = jnp.zeros_like(ref)

    def product(pieces):
        tails = [high[0, rows:] for high in highs]
        low = jnp.concatenate([low[0] for low in lows] + tails, 0)
        high = jnp.concatenate([high[0, :rows] for high in highs] + tails, 0)
        lane = lax.broadcasted_iota(jnp.int32, mix.shape, 1)
        weight = jnp.sum(jnp.where(lane == m, mix[...], 0.0), 1, keepdims=True)
        at = 0
        for piece in pieces:
            size = piece.shape[1]
            here = slice(at, at + size)
            a = mm(piece[0, :, :width], low, NT)
            b = mm(piece[0, :, width:], high, NT)
            term = a[:, :mains] + b[:, :mains]
            later = weight[here] * term
            own[here] += term - later
            prior[here] += later
            low_tail[here] += weight[here] * a[:, mains:]
            high_tail[here] += weight[here] * b[:, mains:]
            at += size

    @pl.when(side == 0)
    def _():
        product([w_own])

    @pl.when(side == 1)
    def _():
        product([w_far0, w_far1])

    @pl.when(m == 2)
    def _():
        last = lax.broadcasted_iota(jnp.int32, (own.shape[0], rows), 1) == rows - 1
        for q in range(count):
            here = slice(q * rows, (q + 1) * rows)
            tail = low_tail[:, 16 * q : 16 * q + 1] + high_tail[:, 16 * q + 1 : 16 * q + 2]
            moved = jnp.where(last, tail, pltpu.roll(prior[:, here], rows - 1, 1))
            value = (own[:, here] + moved).T.astype(BF16)
            if not final:
                outs[q][...] = value
        if final:
            for d in range(ring):
                wanted = lax.rem(place[1] - place[2] - d + 2 * ring, ring)
                for q in range(ring):

                    @pl.when(wanted == q)
                    def _():
                        outs[d][...] = value if q == ring - 1 else done[q][...]


def per_device(
    layer_input, receptance, key_act, value_act, attention_result_sensitivity, time_first,
    decay_exponent_base, decay_shift_mix, mix_rkv, decay_adapter_down, decay_adapter_up, proj_weights,
):
    rows, cols = layer_input.shape
    heads, head = time_first.shape
    rank = decay_adapter_down.shape[1]
    n_seq, n_head = lax.axis_size("seq"), lax.axis_size("head")
    inner = n_seq // n_head
    ring = n_seq // inner
    pairs = cols // PAIR
    parts = 2
    part_cols = cols // parts
    block = min(part_cols, 2 * PAIR)
    seq, hd = lax.axis_index("seq"), lax.axis_index("head")
    place = jnp.stack([lax.rem(seq, inner), seq // inner, hd]).astype(jnp.int32)
    r, k, v, dy = receptance, key_act, value_act, attention_result_sensitivity
    params = pltpu.CompilerParams(vmem_limit_bytes=VMEM)

    def shape(s, t=F32):
        return jax.ShapeDtypeStruct(s, t)

    def work(us):
        return pl.CostEstimate(flops=0, transcendentals=0, bytes_accessed=int(us * 3.5e6))

    def shift(a, distance):
        return lax.ppermute(
            a, "seq", [(i - distance, i) for i in range(n_seq) if 0 <= i - distance < n_seq]
        )

    def around(a, step):
        return lax.ppermute(a, "seq", [(i, (i + inner * step) % n_seq) for i in range(n_seq)])

    def partner(a):
        return lax.ppermute(a, "seq", [(i, i ^ 1) for i in range(n_seq)])

    def head_shift(a, d):
        return lax.ppermute(a, "head", [(i, (i + d) % n_head) for i in range(n_head)])

    def head_parts(a):
        return [a] + [head_shift(a, d) for d in range(1, n_head)]

    weight_rows = proj_weights.shape[1]
    cut = max(weight_rows * 3 // 8, 16)
    mix_here = lax.dynamic_slice_in_dim(mix_rkv, place[1] * cols, cols, 1).T
    carried, u, place, mix_here, *pieces = lax.optimization_barrier(
        (
            shift(layer_input[rows - 1 :], 1), time_first.reshape(1, cols), place, mix_here,
            proj_weights[:, :cut], proj_weights[:, cut:],
        )
    )
    shift_mix = decay_shift_mix.reshape(1, cols)
    pre = pl.pallas_call(
        adapter_kernel,
        out_shape=shape((rows, rank)),
        compiler_params=params,
        cost_estimate=work(1.5),
        name="adapter_input",
    )(layer_input, carried, shift_mix, decay_adapter_down)
    pres = head_parts(pre)

    sums = jnp.asarray(sum_matrix(rows), BF16)
    levels = jnp.asarray(level_matrix(rows), BF16)
    cums = jnp.asarray(cumulative_matrix(rows), BF16)
    far_rows = 2 * head + 16

    lora, lora_t, w, eb, ee, end, st, msg = pl.pallas_call(
        lambda *refs: decay_kernel(head, n_head, *refs),
        out_shape=[
            shape((rows, rank)), shape((rank, rows), BF16), *[shape((rows, cols))] * 3, shape((1, cols)),
            shape((head, cols)), shape((far_rows, cols), BF16),
        ],
        compiler_params=params,
        cost_estimate=work(3),
        name="decay_and_states",
    )(*pres, decay_exponent_base.reshape(1, cols), decay_adapter_up, r, k, v, dy, sums)

    smem = pl.BlockSpec(memory_space=pltpu.SMEM)
    vmem = pl.BlockSpec(memory_space=pltpu.VMEM)
    def col_block(n, width=block, offset=0):
        return pl.BlockSpec((n, width), lambda p, *_: (0, p + offset))

    def whole(s):
        return pl.BlockSpec(s, lambda p, *_: (0,) * len(s))

    steps = part_cols // block
    here = col_block(rows)

    def inside(part):
        at = lambda n: col_block(n, block, part * steps)
        return pl.pallas_call(
            lambda *refs: inner_kernel(head, *refs),
            grid=(steps,),
            in_specs=[at(rows)] * 5 + [at(1), whole(levels.shape)],
            out_specs=[here] * 4 + [col_block(1)],
            out_shape=[shape((rows, part_cols))] * 4 + [shape((1, part_cols))],
            compiler_params=params,
            cost_estimate=work(4),
            name="inside_chunk",
        )(r, k, v, dy, w, u, levels)

    inner_parts = [inside(part) for part in range(parts)]
    far, pieces[0], inner_parts[0] = lax.optimization_barrier(
        (partner(msg), pieces[0], inner_parts[0])
    )
    far0 = partner(pieces[0])
    out_msgs = pl.pallas_call(
        lambda *refs: pair_kernel(head, ring, *refs),
        in_specs=[smem, vmem, vmem],
        out_shape=[shape((head + 16, cols), BF16)] * (ring - 1),
        compiler_params=params,
        cost_estimate=work(1.5),
        name="pair_states",
    )(place, msg, far)
    msgs = [around(m, d + 1) for d, m in enumerate(out_msgs)]

    outer = []
    for part in range(parts):
        at = lambda n: col_block(n, block, part * steps)
        outer.append(
            pl.pallas_call(
                lambda *refs: outer_kernel(head, ring, *refs),
                grid=(steps,),
                in_specs=[smem] + [at(rows)] * 6 + [at(1)] + [here] * 4
                + [at(head), at(1), at(far_rows)] + [at(head + 16)] * (ring - 1),
                out_specs=[pl.BlockSpec((3, rows, block), lambda p: (0, 0, p)), here, here, col_block(1)],
                out_shape=[
                    shape((3, rows, part_cols), BF16), shape((rows, part_cols)),
                    shape((rows, part_cols)), shape((1, part_cols)),
                ],
                compiler_params=params,
                cost_estimate=work(3),
                name="across_chunks",
            )(place, r, k, v, dy, eb, ee, u, *inner_parts[part][:4], st, end, far, *msgs)
        )
    projs = [o[0] for o in outer]

    first, far0 = lax.optimization_barrier((jnp.concatenate([p[:, :1] for p in projs], 1), far0))
    after, pieces[1] = lax.optimization_barrier((shift(first, -1), pieces[1]))
    far1 = partner(pieces[1])
    pad = jnp.zeros((3, 16 - parts, part_cols), BF16)
    lows, highs = [projs[0]], [jnp.concatenate([projs[1], after, pad], 1)]

    ups, bases, mid_parts = [], [], []
    for part in range(parts):
        at = lambda n: pl.BlockSpec((n, part_cols), lambda p: (0, part))
        up_grad, base_grad, mid_grad = pl.pallas_call(
            decay_grad_kernel,
            grid=(1,),
            in_specs=[at(rows), *[whole((rows, part_cols))] * 2, whole((1, part_cols)), at(rank)]
            + [whole((rank, rows)), whole(cums.shape)],
            out_specs=[whole((rank, part_cols)), whole((1, part_cols)), whole((rows, rank))],
            out_shape=[shape((rank, part_cols)), shape((1, part_cols)), shape((rows, rank))],
            compiler_params=params,
            cost_estimate=work(2),
            name="decay_gradient",
        )(w, *outer[part][1:], decay_adapter_up, lora_t, cums)
        ups.append(up_grad)
        bases.append(base_grad)
        mid_parts.append(mid_grad)
    mid_grad = sum(mid_parts)

    mids = head_parts(mid_grad)
    dus = [part[4] for part in inner_parts]
    keep, send, grad_in = pl.pallas_call(
        lambda *refs: middle_kernel(n_head, *refs),
        in_specs=[smem] + [vmem] * (5 + n_head + 3 * parts),
        out_shape=[shape((2 * rank + 16, part_cols), BF16)] * 2 + [shape((rows, cols))],
        compiler_params=params,
        cost_estimate=work(3),
        name="adapter_grads",
    )(
        place, layer_input, carried, shift_mix, decay_adapter_down, lora, *mids, *ups, *bases, *dus
    )

    for step in range(ring - 1):
        low, high = around(lows[-1], 1), around(highs[-1], 1)
        if step == 0:
            low, keep, send = lax.optimization_barrier((low, keep, send))
        lows.append(low)
        highs.append(high)

    def add(a, b):
        return (a.astype(F32) + b.astype(F32)).astype(BF16)

    token_sums = add(keep, partner(send))
    b = 1
    while b < ring:
        route = [(i, ((i // inner) ^ b) * inner + i % inner) for i in range(n_seq)]
        token_sums = add(token_sums, lax.ppermute(token_sums, "seq", route))
        b *= 2
    up_grad, down_grad, base_grad, du = pl.pallas_call(
        lambda *refs: finish_kernel(rank, *refs),
        in_specs=[smem, vmem, vmem],
        out_shape=[shape((rank, cols)), shape((cols, rank)), shape((1, cols)), shape((1, cols))],
        compiler_params=params,
        cost_estimate=work(2),
        name="token_sums",
    )(place, token_sums, partner(token_sums))

    grad_next = jnp.concatenate([grad_in[1:], shift(grad_in[:1], -1)], 0)
    adapter_term = (1.0 - decay_shift_mix) * grad_in + decay_shift_mix * grad_next

    def column(i, place):
        return jnp.where(i == 0, place[0], 1 - place[0])

    def project(low, high, done, n_out):
        count = len(low)
        out_block = pl.BlockSpec((rows, weight_rows), lambda i, m, place: (0, column(i, place)))
        part_of = lambda a: pl.BlockSpec((1,) + a.shape[1:], lambda i, m, place: (m, 0, 0))
        far_of = lambda a: pl.BlockSpec(
            (1,) + a.shape[1:], lambda i, m, place: (jnp.where(i == 0, 0, m), 0, 0)
        )
        sums_of = lambda n: pltpu.VMEM((weight_rows, n), F32)
        return pl.pallas_call(
            lambda *refs: project_kernel(count, ring, *refs),
            grid_spec=pltpu.PrefetchScalarGridSpec(
                num_scalar_prefetch=1,
                grid=(inner, 3),
                in_specs=[part_of(a) for a in low + high]
                + [
                    pl.BlockSpec(
                        (1, weight_rows, cols), lambda i, m, place: (jnp.where(i == 0, m, 2), 0, 0)
                    ),
                    far_of(far0),
                    far_of(far1),
                    pl.BlockSpec((weight_rows, 3), lambda i, m, place: (column(i, place), 0)),
                ]
                + [out_block] * len(done),
                out_specs=[out_block] * n_out,
                scratch_shapes=[
                    sums_of(count * rows), sums_of(count * rows), sums_of(16 * count), sums_of(16 * count),
                ],
            ),
            out_shape=[shape((rows, cols), BF16)] * n_out,
            compiler_params=params,
            cost_estimate=work(5),
            name="projections",
        )(place, *low, *high, proj_weights, far0, far1, mix_here, *done)

    done = project(lows[:-1], highs[:-1], [], ring - 1)
    sends = project(lows[-1:], highs[-1:], done, ring)
    total = sends[0].astype(F32)
    for d in range(1, n_head):
        total = total + head_shift(sends[d], d).astype(F32)
    swap = [
        (h * n_seq + z * inner + x, z * n_seq + h * inner + x)
        for h in range(n_head) for z in range(ring) for x in range(inner)
    ]
    summed = lax.ppermute(total.astype(BF16), ("head", "seq"), swap)
    result = (summed.astype(F32) + adapter_term).astype(BF16)
    return (result, down_grad, up_grad, base_grad.reshape(cols), du.reshape(heads, head))


def solution(mesh):
    return jax.shard_map(
        per_device,
        mesh=mesh,
        in_specs=(
            P("seq", "head"), P("seq", "head"), P("seq", "head"), P("seq", "head"), P("seq", "head"),
            P("head", None), P("head"), P("head"), P(), P("head", None), P(None, "head"),
            P(None, "seq", "head"),
        ),
        out_specs=(P("seq", "head"), P("head", None), P(None, "head"), P("head"), P("head", None)),
        check_vma=False,
    )
```

```python
import jax
import jax.numpy as jnp
import numpy as np
from jax import lax
from jax.experimental import pallas as pl
from jax.experimental.pallas import tpu as pltpu
from jax.sharding import PartitionSpec as P

F32 = jnp.float32
BF16 = jnp.bfloat16
PAIR = 128
VMEM = 56 * 2**20
NN = (((1,), (0,)), ((), ()))
NT = (((1,), (1,)), ((), ()))
TN = (((0,), (0,)), ((), ()))


def position():
    seq, head = lax.axis_index("seq"), lax.axis_index("head")
    inner = lax.axis_size("seq") // lax.axis_size("head")
    return lax.rem(seq, inner), lax.div(seq, inner), head


def mm(a, b, dims=NN):
    return lax.dot_general(a, b, dims, preferred_element_type=F32)


def halves(a):
    hi = a.astype(BF16)
    return hi, (a - hi.astype(F32)).astype(BF16)


def low_lanes(shape, half):
    return lax.broadcasted_iota(jnp.int32, shape, len(shape) - 1) < half


def block_rows(a, half):
    low = low_lanes(a.shape, half)
    zero = jnp.zeros_like(a)
    return jnp.concatenate([jnp.where(low, a, zero), jnp.where(low, zero, a)], 0)


def fold(a, half):
    rows = a.shape[0] // 2
    return jnp.where(low_lanes((rows, a.shape[1]), half), a[:rows], a[rows:])


def sum_matrix(rows):
    t = np.arange(rows)
    both = np.concatenate([t[:, None] > t[None, :], t[:, None] < t[None, :]], 0)
    return np.concatenate([both, both], 1).astype(np.float32)


def level_matrix(rows):
    t = np.arange(rows)
    parts = []
    m = 1
    while m < rows:
        mid = (t // (2 * m)) * 2 * m + m
        right = t >= mid
        u = t[None, :]
        take_right = (u >= mid[:, None]) & (u < t[:, None])
        take_left = (u > t[:, None]) & (u < mid[:, None])
        parts.append(np.where(right[:, None], take_right, take_left))
        m *= 2
    both = np.concatenate(parts, 0)
    return np.concatenate([both, both], 1).astype(np.float32)


def cumulative_matrix(rows):
    t = np.arange(rows)
    strict = (t[:, None] < t[None, :]).astype(np.float32)
    full = (t[:, None] <= t[None, :]).astype(np.float32)
    return np.concatenate([strict, strict, -full, -full], 1)


def split_rows(a):
    hi, lo = halves(a)
    wide = (4, a.shape[1])
    return jnp.concatenate([jnp.broadcast_to(hi, wide), jnp.broadcast_to(lo, wide)], 0)


def joined(msg, at):
    return msg[at : at + 1].astype(F32) + msg[at + 4 : at + 5].astype(F32)


def mm3(a, b, dims=NN):
    ah, al = halves(a)
    bh, bl = halves(b)
    return mm(ah, bh, dims) + (mm(ah, bl, dims) + mm(al, bh, dims))


def mixed_input(x, carried, mix):
    features = x[...].astype(F32)
    row = lax.broadcasted_iota(jnp.int32, features.shape, 0)
    previous = jnp.where(row == 0, carried[...].astype(F32), pltpu.roll(features, 1, 0))
    return features + mix[...] * (previous - features)


def copy_rows(weights, piece, at, sem):
    return pltpu.make_async_copy(weights.at[:, pl.ds(at, piece.shape[1])], piece, sem.at[0])


def adapter_kernel(x, carried, mix, down, weights, pre, piece, sem):
    copy = copy_rows(weights, piece, 0, sem)
    copy.start()
    pre[...] = mm3(mixed_input(x, carried, mix), down[...])
    copy.wait()


def decay_kernel(head, count, *refs):
    pres = refs[:count]
    base, up, r, k, v, dy, sums, lora, lora_t, w_out, end, st, msg = refs[count:]
    rows = r.shape[0]
    total = pres[0][...]
    for pre in pres[1:]:
        total = total + pre[...]
    mid = jnp.tanh(total)
    lora[...] = mid
    lora_t[...] = mid.T.astype(BF16)
    w = -jnp.exp(base[...] + mm3(mid, up[...]))
    w_out[...] = w
    hi, lo = halves(w)
    args = mm(sums[...], jnp.concatenate([hi, lo], 0))
    before, after = args[:rows], args[rows:]
    final = before[rows - 1 :] + w[rows - 1 :]
    end[...] = final
    from_start, to_end = jnp.exp(before), jnp.exp(after)
    kf = (k[...].astype(F32) * to_end).astype(BF16)
    rb = (r[...].astype(F32) * from_start).astype(BF16)
    for p in range(r.shape[1] // PAIR):
        cols = slice(p * PAIR, (p + 1) * PAIR)
        state = fold(mm(v[:, cols], kf[:, cols], TN), head)
        st[:, cols] = state
        msg[:head, cols] = state.astype(BF16)
        msg[head : 2 * head, cols] = fold(mm(dy[:, cols], rb[:, cols], TN), head).astype(BF16)
    msg[2 * head :] = split_rows(final)


def pair_kernel(head, ring, own, far, *outs):
    place = position()
    late = place[0] == 1
    dec_own, dec_far = joined(own, 2 * head), joined(far, 2 * head)
    eo, ef = jnp.exp(dec_own), jnp.exp(dec_far)
    st_own, st_far = own[:head].astype(F32), far[:head].astype(F32)
    gt_own, gt_far = own[head : 2 * head].astype(F32), far[head : 2 * head].astype(F32)
    state = jnp.where(late, st_own + eo * st_far, st_far + ef * st_own).astype(BF16)
    grad = jnp.where(late, gt_far + ef * gt_own, gt_own + eo * gt_far).astype(BF16)
    decays = split_rows(dec_own + dec_far)
    for d in range(1, ring):
        out = outs[d - 1]
        ahead = place[1] + d < ring

        @pl.when(ahead)
        def _():
            out[:head] = state

        @pl.when(jnp.logical_not(ahead))
        def _():
            out[:head] = grad

        out[head:] = decays


def inner_kernel(head, skip, r, k, v, dy, w, u, levels, sums, *refs):
    if skip:
        weights, piece, sem = refs[0], refs[8], refs[9]
        refs = refs[1:8]

        @pl.when(pl.program_id(0) == 0)
        def _():
            copy_rows(weights, piece, skip, sem).start()

        @pl.when(pl.program_id(0) == pl.num_programs(0) - 1)
        def _():
            copy_rows(weights, piece, skip, sem).wait()

    gr_out, gk_out, gv_out, self_out, eb_out, ee_out, du_out = refs
    rows, width = r.shape
    row = lax.broadcasted_iota(jnp.int32, (rows, PAIR), 0)
    row2 = lax.broadcasted_iota(jnp.int32, (rows, 2 * rows), 0)
    col2 = lax.broadcasted_iota(jnp.int32, (rows, 2 * rows), 1)
    apart = row2 ^ (col2 & (rows - 1))
    lane_r = lax.broadcasted_iota(jnp.int32, (2 * PAIR, PAIR), 0) & (PAIR - 1)
    lane_c = lax.broadcasted_iota(jnp.int32, (2 * PAIR, PAIR), 1)
    ones = jnp.where((lane_r < head) == (lane_c < head), 1.0, 0.0).astype(BF16)
    hi, lo = halves(w[...])
    both = jnp.concatenate([hi, lo], 0)
    decay = jnp.exp(mm(levels[...], both))
    ends = jnp.exp(mm(sums[...], both))
    eb_out[...], ee_out[...] = ends[:rows], ends[rows:]
    for p in range(width // PAIR):
        cols = slice(p * PAIR, (p + 1) * PAIR)
        rf, kf = r[:, cols].astype(F32), k[:, cols].astype(F32)
        vf, dyf = v[:, cols].astype(F32), dy[:, cols].astype(F32)
        dydy = block_rows(dy[:, cols], head)
        pairs = mm(dy[:, cols], block_rows(v[:, cols], head), NT)
        pairs_t = mm(v[:, cols], dydy, NT)
        gr = jnp.zeros((rows, PAIR), F32)
        gk = jnp.zeros((rows, PAIR), F32)
        scores_t = jnp.zeros((rows, 2 * rows), F32)
        m, level = 1, 0
        while m < rows:
            d = decay[level * rows : (level + 1) * rows, cols]
            right = (row & m) != 0
            rd = jnp.where(right, rf * d, 0.0).astype(BF16)
            kd = jnp.where(right, 0.0, kf * d).astype(BF16)
            kk, rr = block_rows(kd, head), block_rows(rd, head)
            near = apart < 2 * m
            a = mm(kd, rr, NT)
            scores_t = scores_t + jnp.where(near, a, 0.0)
            here = jnp.where(near, pairs, 0.0).astype(BF16)
            here_t = jnp.where(near, pairs_t, 0.0).astype(BF16)
            gr = gr + jnp.where(right, d * mm(here, kk), 0.0)
            gk = gk + jnp.where(right, 0.0, d * mm(here_t, rr))
            m, level = 2 * m, level + 1
        sh, sl = halves(dyf * vf)
        own = mm(jnp.concatenate([sh, sl], 1), ones)
        bh, bl = halves(rf * u[:, cols] * kf)
        bonus = mm(jnp.concatenate([bh, bl], 1), ones)
        gr_out[:, cols] = gr
        gk_out[:, cols] = gk
        gv_out[:, cols] = mm(scores_t.astype(BF16), dydy) + bonus * dyf
        self_out[:, cols] = own
        du_out[:, cols] = jnp.sum(rf * kf * own, 0, keepdims=True)


def outer_kernel(
    head, ring, r, k, v, dy, u, gr0, gk0, gv0, own, eb, ee, st, end, far, *refs
):
    place = position()
    msgs = refs[: ring - 1]
    proj, r_gr, k_gk, at_end = refs[ring - 1 :]
    width = r.shape[1]
    late, z = place[0] == 1, place[1]
    zero = jnp.zeros((head, width), F32)
    nothing = jnp.zeros((1, width), F32)
    state, grad, past, future = zero, zero, nothing, nothing
    for d in range(1, ring):
        msg = msgs[d - 1]
        live = d <= z
        state = state + jnp.where(live, jnp.exp(past) * msg[:head].astype(F32), 0.0)
        past = past + jnp.where(live, joined(msg, head), 0.0)
    for d in range(ring - 1, 0, -1):
        msg = msgs[d - 1]
        live = d > z
        grad = grad + jnp.where(live, jnp.exp(future) * msg[:head].astype(F32), 0.0)
        future = future + jnp.where(live, joined(msg, head), 0.0)
    ef = jnp.exp(joined(far, 2 * head))
    st_in = jnp.where(late, far[:head].astype(F32) + ef * state, state)
    gt_in = jnp.where(late, grad, far[head : 2 * head].astype(F32) + ef * grad)
    at_end[...] = jnp.sum(gt_in * (jnp.exp(end[...]) * st_in + st[...]), 0, keepdims=True)
    sb, gb = st_in.astype(BF16), gt_in.astype(BF16)
    for p in range(width // PAIR):
        cols = slice(p * PAIR, (p + 1) * PAIR)
        grads = block_rows(gb[:, cols], head)
        rf, kf = r[:, cols].astype(F32), k[:, cols].astype(F32)
        after = ee[:, cols]
        gr = gr0[:, cols] + eb[:, cols] * mm(dy[:, cols], block_rows(sb[:, cols], head))
        gk = gk0[:, cols] + after * mm(v[:, cols], grads)
        gv = gv0[:, cols] + mm((kf * after).astype(BF16), grads, NT)
        s = own[:, cols] * u[:, cols]
        proj[0, :, cols] = (gr + kf * s).astype(BF16)
        proj[1, :, cols] = (gk + rf * s).astype(BF16)
        proj[2, :, cols] = gv.astype(BF16)
        r_gr[:, cols] = rf * gr
        k_gk[:, cols] = kf * gk


def decay_grad_kernel(w, r_gr, k_gk, at_end, up, lora_t, cums, up_grad, base_grad, mid_grad):
    ah, al = halves(r_gr[...])
    bh, bl = halves(k_gk[...])
    gp = (mm(cums[...], jnp.concatenate([ah, al, bh, bl], 0)) + at_end[...]) * w[...]
    gpb = gp.astype(BF16)
    up_grad[...] = mm(lora_t[...], gpb)
    base_grad[...] = jnp.sum(gp, 0, keepdims=True)
    mid_grad[...] = mm(gpb, up[...].astype(BF16), NT)


def middle_kernel(count, x, carried, mix, down, lora, *refs):
    mids, sides, (keep, send, grad_in) = refs[:count], refs[count:-3], refs[-3:]
    total = mids[0][...]
    for part in mids[1:]:
        total = total + part[...]
    mid = total * (1.0 - lora[...] * lora[...])
    grad_in[...] = mm3(mid, down[...], NT)
    down_grad = mm3(mid.T, mixed_input(x, carried, mix))
    rank, half = mid.shape[1], x.shape[1] // 2
    wide = (8, half)
    late = position()[0] == 1

    def choose(low, high, at, size):
        keep[at : at + size] = jnp.where(late, high, low).astype(BF16)
        send[at : at + size] = jnp.where(late, low, high).astype(BF16)

    up_low, up_high, base_low, base_high, du_low, du_high = [ref[...] for ref in sides]
    choose(up_low, up_high, 0, rank)
    choose(down_grad[:, :half], down_grad[:, half:], rank, rank)
    for at, low, high in ((0, base_low, base_high), (8, du_low, du_high)):
        choose(jnp.broadcast_to(low, wide), jnp.broadcast_to(high, wide), 2 * rank + at, 8)


def finish_kernel(rank, mine, theirs, up, down, base, du):
    late = position()[0] == 1
    half = mine.shape[1]
    a, b = mine[...].astype(F32), theirs[...].astype(F32)
    for at, value in ((0, jnp.where(late, b, a)), (half, jnp.where(late, a, b))):
        here = slice(at, at + half)
        up[:, here] = value[:rank]
        down[here] = value[rank : 2 * rank].T
        for ref, row in ((base, 2 * rank), (du, 2 * rank + 8)):
            size = ref.shape[1]
            for i in range(half // size):
                to = at // size + i
                ref[to : to + 1] = value[row : row + 1, i * size : (i + 1) * size]


def project_kernel(count, ring, final, *refs):
    place = position()
    lows, highs, given, mix = refs[:count], refs[count : 2 * count], refs[2 * count : 2 * count + 3], refs[2 * count + 3]
    rest, (low, high, weights, own, prior, sem) = refs[2 * count + 4 : -6], refs[-6:]
    done, outs = (rest[:-ring], rest[-ring:]) if final else ((), rest)
    rows, width = lows[0].shape[1:]
    n = weights.shape[2]
    copies = []

    def fetch(source, target):
        copy = pltpu.make_async_copy(source, target, sem.at[len(copies)])
        copy.start()
        copies.append(copy)
        return copy

    weight_copies, block_copies = [], []
    for i in range(2):
        for m in range(3):
            if i == 0:
                weight_copies.append([fetch(given[0].at[m], weights.at[0, m])])
            else:
                first, cut = given[1].at[m], given[1].shape[1]
                weight_copies.append(
                    [
                        fetch(first, weights.at[1, m, pl.ds(0, cut)]),
                        fetch(given[2].at[m], weights.at[1, m, pl.ds(cut, n - cut)]),
                    ]
                )
            if i == 0:
                places = [pl.ds(q * rows, rows) for q in range(count)]
                block_copies.append(
                    [fetch(lows[q].at[m], low.at[m, at]) for q, at in enumerate(places)]
                    + [fetch(highs[q].at[m], high.at[m, at]) for q, at in enumerate(places)]
                )

    for i in range(2):
        column = pl.ds(pl.multiple_of((place[0] if i == 0 else 1 - place[0]) * n, n), n)
        for m in range(3):
            for copy in (block_copies[m] if i == 0 else []) + weight_copies[i * 3 + m]:
                copy.wait()
            term = mm(low[m], weights[i, m, :, :width], NT) + mm(high[m], weights[i, m, :, width:], NT)
            later = mix[m : m + 1, column] * term
            own[...] = term - later if m == 0 else own[...] + (term - later)
            prior[...] = later if m == 0 else prior[...] + later
        last = lax.broadcasted_iota(jnp.int32, (rows, n), 0) == rows - 1
        top = lax.broadcasted_iota(jnp.int32, (16, n), 0) == 0

        def store(out, q):
            here = slice(q * rows, (q + 1) * rows)
            part = prior[here]
            moved = jnp.where(last, 0.0, pltpu.roll(part, rows - 1, 0))
            out[:rows, column] = (own[here] + moved).astype(BF16)
            out[rows:, column] = jnp.where(top, part[:16], 0.0).astype(BF16)

        if not final:
            for q in range(count):
                store(outs[q], q)
            continue
        for d in range(ring):
            wanted = lax.rem(place[1] - place[2] - d + 2 * ring, ring)
            for q in range(ring):

                @pl.when(wanted == q)
                def _():
                    if q == ring - 1:
                        store(outs[d], 0)
                    else:
                        outs[d][:, column] = done[q][:, column]


def per_device(
    layer_input, receptance, key_act, value_act, attention_result_sensitivity, time_first,
    decay_exponent_base, decay_shift_mix, mix_rkv, decay_adapter_down, decay_adapter_up, proj_weights,
):
    rows, cols = layer_input.shape
    heads, head = time_first.shape
    rank = decay_adapter_down.shape[1]
    n_seq, n_head = lax.axis_size("seq"), lax.axis_size("head")
    inner = n_seq // n_head
    ring = n_seq // inner
    pairs = cols // PAIR
    parts = 2
    part_cols = cols // parts
    block = min(part_cols, 2 * PAIR)
    r, k, v, dy = receptance, key_act, value_act, attention_result_sensitivity
    params = pltpu.CompilerParams(vmem_limit_bytes=VMEM)

    def shape(s, t=F32):
        return jax.ShapeDtypeStruct(s, t)

    def work(us):
        return pl.CostEstimate(flops=0, transcendentals=0, bytes_accessed=int(us * 3.5e6))

    def shift(a, distance):
        return lax.ppermute(
            a, "seq", [(i - distance, i) for i in range(n_seq) if 0 <= i - distance < n_seq]
        )

    def around(a, step):
        return lax.ppermute(a, "seq", [(i, (i + inner * step) % n_seq) for i in range(n_seq)])

    def partner(a):
        return lax.ppermute(a, "seq", [(i, i ^ 1) for i in range(n_seq)])

    def head_shift(a, d):
        return lax.ppermute(a, "head", [(i, (i + d) % n_head) for i in range(n_head)])

    def head_parts(a):
        return [a] + [head_shift(a, d) for d in range(1, n_head)]

    def after_that(value, *others):
        return lax.optimization_barrier((value, *others))[0]

    weight_rows = proj_weights.shape[1]
    cut = weight_rows // 8
    anywhere = pl.BlockSpec(memory_space=pl.ANY)
    vmem = pl.BlockSpec(memory_space=pltpu.VMEM)

    carried = shift(layer_input[rows - 1 :], 1)
    shift_mix = decay_shift_mix.reshape(1, cols)
    pre, piece = pl.pallas_call(
        adapter_kernel,
        in_specs=[vmem] * 4 + [anywhere],
        out_specs=[vmem, anywhere],
        out_shape=[shape((rows, rank)), shape((3, cut, cols), BF16)],
        scratch_shapes=[pltpu.SemaphoreType.DMA((1,))],
        compiler_params=params,
        cost_estimate=work(1.5),
        name="adapter_input",
    )(layer_input, carried, shift_mix, decay_adapter_down, proj_weights)
    fars = [partner(piece)]
    pres = head_parts(pre)

    sums = jnp.asarray(sum_matrix(rows), BF16)
    levels = jnp.asarray(level_matrix(rows), BF16)
    cums = jnp.asarray(cumulative_matrix(rows), BF16)
    far_rows = 2 * head + 8

    lora, lora_t, w, end, st, msg = pl.pallas_call(
        lambda *refs: decay_kernel(head, n_head, *refs),
        out_shape=[
            shape((rows, rank)), shape((rank, rows), BF16), shape((rows, cols)), shape((1, cols)),
            shape((head, cols)), shape((far_rows, cols), BF16),
        ],
        compiler_params=params,
        cost_estimate=work(3),
        name="decay_and_states",
    )(*pres, decay_exponent_base.reshape(1, cols), decay_adapter_up, r, k, v, dy, sums)

    vmem = pl.BlockSpec(memory_space=pltpu.VMEM)
    u = after_that(time_first, msg).reshape(1, cols)

    def col_block(n, width=block, offset=0):
        return pl.BlockSpec((n, width), lambda p, *_: (0, p + offset))

    def whole(s):
        return pl.BlockSpec(s, lambda p, *_: (0,) * len(s))

    steps = part_cols // block
    here = col_block(rows)

    def inside(part):
        at = lambda n: col_block(n, block, part * steps)
        extra = part == 0
        return pl.pallas_call(
            lambda *refs: inner_kernel(head, cut if extra else 0, *refs),
            grid=(steps,),
            in_specs=[at(rows)] * 5 + [at(1), whole(levels.shape), whole(sums.shape)] + [anywhere] * extra,
            out_specs=[here] * 6 + [col_block(1)] + [anywhere] * extra,
            out_shape=[shape((rows, part_cols))] * 6 + [shape((1, part_cols))]
            + [shape((3, weight_rows - cut, cols), BF16)] * extra,
            scratch_shapes=[pltpu.SemaphoreType.DMA((1,))] * extra,
            compiler_params=params,
            cost_estimate=work(4),
            name="inside_chunk",
        )(r, k, v, dy, after_that(w, fars[0]) if extra else w, u, levels, sums, *[proj_weights] * extra)

    inner_parts = [inside(part) for part in range(parts)]
    far, piece, inner_parts[0] = lax.optimization_barrier(
        (partner(msg), inner_parts[0][7], inner_parts[0][:7])
    )
    fars.append(partner(piece))
    out_msgs = pl.pallas_call(
        lambda *refs: pair_kernel(head, ring, *refs),
                out_shape=[shape((head + 8, cols), BF16)] * (ring - 1),
        compiler_params=params,
        cost_estimate=work(1.5),
        name="pair_states",
    )(msg, far)
    msgs = [around(m, d + 1) for d, m in enumerate(out_msgs)]

    inner_parts[1], msgs = lax.optimization_barrier((inner_parts[1], msgs))
    outer = []
    for part in range(parts):
        at = lambda n: col_block(n, block, part * steps)
        outer.append(
            pl.pallas_call(
                lambda *refs: outer_kernel(head, ring, *refs),
                grid=(steps,),
                in_specs=[at(rows)] * 4 + [at(1)] + [here] * 6
                + [at(head), at(1), at(far_rows)] + [at(head + 8)] * (ring - 1),
                out_specs=[pl.BlockSpec((3, rows, block), lambda p: (0, 0, p)), here, here, col_block(1)],
                out_shape=[
                    shape((3, rows, part_cols), BF16), shape((rows, part_cols)),
                    shape((rows, part_cols)), shape((1, part_cols)),
                ],
                compiler_params=params,
                cost_estimate=work(3),
                name="across_chunks",
            )(r, k, v, dy, u, *inner_parts[part][:6], st, end, far, *msgs)
        )
    projs = [o[0] for o in outer]

    ups, bases, mid_parts = [], [], []
    for part in range(parts):
        at = lambda n: pl.BlockSpec((n, part_cols), lambda p: (0, part))
        up_grad, base_grad, mid_grad = pl.pallas_call(
            decay_grad_kernel,
            grid=(1,),
            in_specs=[at(rows), *[whole((rows, part_cols))] * 2, whole((1, part_cols)), at(rank)]
            + [whole((rank, rows)), whole(cums.shape)],
            out_specs=[whole((rank, part_cols)), whole((1, part_cols)), whole((rows, rank))],
            out_shape=[shape((rank, part_cols)), shape((1, part_cols)), shape((rows, rank))],
            compiler_params=params,
            cost_estimate=work(2),
            name="decay_gradient",
        )(w, *outer[part][1:], decay_adapter_up, lora_t, cums)
        ups.append(up_grad)
        bases.append(base_grad)
        mid_parts.append(mid_grad)
    mid_grad = sum(mid_parts)

    mids = head_parts(mid_grad)
    dus = [part[6] for part in inner_parts]
    keep, send, grad_in = pl.pallas_call(
        lambda *refs: middle_kernel(n_head, *refs),
        in_specs=[vmem] * (5 + n_head + 3 * parts),
        out_shape=[shape((2 * rank + 16, part_cols), BF16)] * 2 + [shape((rows, cols))],
        compiler_params=params,
        cost_estimate=work(3),
        name="adapter_grads",
    )(
        layer_input, carried, shift_mix, decay_adapter_down, lora, *mids, *ups, *bases, *dus
    )

    lows, highs = [projs[0]], [projs[1]]
    for step in range(ring - 1):
        low, high = lows[-1], highs[-1]
        lows.append(around(after_that(low, mid_grad) if step == 1 else low, 1))
        highs.append(around(high, 1))

    def add(a, b):
        return (a.astype(F32) + b.astype(F32)).astype(BF16)

    got = partner(after_that(send, lows[2]))

    mix_here = lax.dynamic_slice_in_dim(after_that(mix_rkv, *out_msgs), position()[1] * cols, cols, 1)

    tall = rows + 16

    def project(low, high, done=()):
        count, final = len(low), len(done) > 0
        return pl.pallas_call(
            lambda *refs: project_kernel(count, ring, final, *refs),
            in_specs=[anywhere] * (2 * count + 3) + [vmem] * (1 + len(done)),
            out_shape=[shape((tall, cols), BF16)] * (ring if final else count),
            scratch_shapes=[
                pltpu.VMEM((3, count * rows, part_cols), BF16),
                pltpu.VMEM((3, count * rows, part_cols), BF16),
                pltpu.VMEM((inner, 3, weight_rows, cols), BF16),
                pltpu.VMEM((count * rows, weight_rows), F32),
                pltpu.VMEM((count * rows, weight_rows), F32),
                pltpu.SemaphoreType.DMA((3 * (2 * count + 3),)),
            ],
            compiler_params=pltpu.CompilerParams(vmem_limit_bytes=24 * 2**20),
            cost_estimate=work(5),
            name="projections",
        )(*low, *high, proj_weights, *fars, mix_here, *done)

    done = project(lows[:-1], highs[:-1])
    sends = project(lows[-1:], highs[-1:], done)
    token_sums = add(keep, after_that(got, *done))
    b = 1
    while b < ring:
        route = [(i, ((i // inner) ^ b) * inner + i % inner) for i in range(n_seq)]
        got = lax.ppermute(token_sums, "seq", route)
        token_sums = add(token_sums, after_that(got, sends) if b == 1 else got)
        b *= 2
    up_grad, down_grad, base_grad, du = pl.pallas_call(
        lambda *refs: finish_kernel(rank, *refs),
                out_shape=[shape((rank, cols)), shape((cols, rank)), shape((pairs, PAIR)), shape((heads, head))],
        compiler_params=params,
        cost_estimate=work(2),
        name="token_sums",
    )(token_sums, partner(token_sums))

    total = sends[0].astype(F32)
    for d in range(1, n_head):
        total = total + head_shift(sends[d], d).astype(F32)
    swap, back = [], []
    for h in range(n_head):
        for z in range(ring):
            for x in range(inner):
                source = h * n_seq + z * inner + x
                block_at = h * inner + x
                swap.append((source, z * n_seq + block_at))
                if block_at > 0:
                    back.append((source, z * n_seq + block_at - 1))
    base_grad = base_grad.reshape(cols)
    summed = lax.ppermute(total[:rows].astype(BF16), ("head", "seq"), swap)
    edge = lax.ppermute(total[rows : rows + 1], ("head", "seq"), back)
    summed = after_that(summed, up_grad, base_grad, du)
    grad_next = jnp.concatenate([grad_in[1:], shift(grad_in[:1], -1)], 0)
    adapter_term = (1.0 - decay_shift_mix) * grad_in + decay_shift_mix * grad_next
    last = lax.broadcasted_iota(jnp.int32, (rows, 1), 0) == rows - 1
    result = (summed.astype(F32) + adapter_term + jnp.where(last, edge, 0.0)).astype(BF16)
    return (result, down_grad, up_grad, base_grad, du)


def solution(mesh):
    return jax.shard_map(
        per_device,
        mesh=mesh,
        in_specs=(
            P("seq", "head"), P("seq", "head"), P("seq", "head"), P("seq", "head"), P("seq", "head"),
            P("head", None), P("head"), P("head"), P(), P("head", None), P(None, "head"),
            P(None, "seq", "head"),
        ),
        out_specs=(P("seq", "head"), P("head", None), P(None, "head"), P("head"), P("head", None)),
        check_vma=False,
    )
```

```python
import jax
import jax.numpy as jnp
import numpy as np
from jax import lax
from jax.experimental import pallas as pl
from jax.experimental.pallas import tpu as pltpu
from jax.sharding import PartitionSpec as P

F32 = jnp.float32
BF16 = jnp.bfloat16
PAIR = 128
VMEM = 56 * 2**20
NN = (((1,), (0,)), ((), ()))
NT = (((1,), (1,)), ((), ()))
TN = (((0,), (0,)), ((), ()))


def position():
    seq, head = lax.axis_index("seq"), lax.axis_index("head")
    inner = lax.axis_size("seq") // lax.axis_size("head")
    return lax.rem(seq, inner), lax.div(seq, inner), head


def mm(a, b, dims=NN):
    return lax.dot_general(a, b, dims, preferred_element_type=F32)


def halves(a):
    hi = a.astype(BF16)
    return hi, (a - hi.astype(F32)).astype(BF16)


def low_lanes(shape, half):
    return lax.broadcasted_iota(jnp.int32, shape, len(shape) - 1) < half


def block_rows(a, half):
    low = low_lanes(a.shape, half)
    zero = jnp.zeros_like(a)
    return jnp.concatenate([jnp.where(low, a, zero), jnp.where(low, zero, a)], 0)


def fold(a, half):
    rows = a.shape[0] // 2
    return jnp.where(low_lanes((rows, a.shape[1]), half), a[:rows], a[rows:])


def sum_matrix(rows):
    t = np.arange(rows)
    both = np.concatenate([t[:, None] > t[None, :], t[:, None] < t[None, :]], 0)
    return np.concatenate([both, both], 1).astype(np.float32)


def level_matrix(rows):
    t = np.arange(rows)
    parts = []
    m = 1
    while m < rows:
        mid = (t // (2 * m)) * 2 * m + m
        right = t >= mid
        u = t[None, :]
        take_right = (u >= mid[:, None]) & (u < t[:, None])
        take_left = (u > t[:, None]) & (u < mid[:, None])
        parts.append(np.where(right[:, None], take_right, take_left))
        m *= 2
    both = np.concatenate(parts, 0)
    return np.concatenate([both, both], 1).astype(np.float32)


def cumulative_matrix(rows):
    t = np.arange(rows)
    strict = (t[:, None] < t[None, :]).astype(np.float32)
    full = (t[:, None] <= t[None, :]).astype(np.float32)
    return np.concatenate([strict, strict, -full, -full], 1)


def split_rows(a):
    hi, lo = halves(a)
    wide = (4, a.shape[1])
    return jnp.concatenate([jnp.broadcast_to(hi, wide), jnp.broadcast_to(lo, wide)], 0)


def joined(msg, at):
    return msg[at : at + 1].astype(F32) + msg[at + 4 : at + 5].astype(F32)


def mm3(a, b, dims=NN):
    ah, al = halves(a)
    bh, bl = halves(b)
    return mm(ah, bh, dims) + (mm(ah, bl, dims) + mm(al, bh, dims))


def mixed_input(x, carried, mix):
    features = x[...].astype(F32)
    row = lax.broadcasted_iota(jnp.int32, features.shape, 0)
    previous = jnp.where(row == 0, carried[...].astype(F32), pltpu.roll(features, 1, 0))
    return features + mix[...] * (previous - features)


def copy_rows(weights, piece, at, stage, sem):
    rows = pl.ds(at, piece.shape[1])
    into = [pltpu.make_async_copy(weights.at[m, rows], stage.at[m], sem.at[m]) for m in range(3)]
    out = [pltpu.make_async_copy(stage.at[m], piece.at[m], sem.at[3 + m]) for m in range(3)]
    return into, out


def adapter_kernel(x, carried, mix, down, weights, pre, piece, stage, sem):
    into, out = copy_rows(weights, piece, 0, stage, sem)
    for copy in into:
        copy.start()
    for first, second in zip(into, out):
        first.wait()
        second.start()
    pre[...] = mm3(mixed_input(x, carried, mix), down[...])
    for copy in out:
        copy.wait()


def decay_kernel(head, count, *refs):
    pres = refs[:count]
    base, up, r, k, v, dy, sums, lora, lora_t, w_out, end, st, msg = refs[count:]
    rows = r.shape[0]
    total = pres[0][...]
    for pre in pres[1:]:
        total = total + pre[...]
    mid = jnp.tanh(total)
    lora[...] = mid
    lora_t[...] = mid.T.astype(BF16)
    w = -jnp.exp(base[...] + mm3(mid, up[...]))
    w_out[...] = w
    hi, lo = halves(w)
    args = mm(sums[...], jnp.concatenate([hi, lo], 0))
    before, after = args[:rows], args[rows:]
    final = before[rows - 1 :] + w[rows - 1 :]
    end[...] = final
    from_start, to_end = jnp.exp(before), jnp.exp(after)
    kf = (k[...].astype(F32) * to_end).astype(BF16)
    rb = (r[...].astype(F32) * from_start).astype(BF16)
    for p in range(r.shape[1] // PAIR):
        cols = slice(p * PAIR, (p + 1) * PAIR)
        state = fold(mm(v[:, cols], kf[:, cols], TN), head)
        st[:, cols] = state
        msg[:head, cols] = state.astype(BF16)
        msg[head : 2 * head, cols] = fold(mm(dy[:, cols], rb[:, cols], TN), head).astype(BF16)
    msg[2 * head :] = split_rows(final)


def pair_kernel(head, ring, own, far, *outs):
    place = position()
    late = place[0] == 1
    dec_own, dec_far = joined(own, 2 * head), joined(far, 2 * head)
    eo, ef = jnp.exp(dec_own), jnp.exp(dec_far)
    st_own, st_far = own[:head].astype(F32), far[:head].astype(F32)
    gt_own, gt_far = own[head : 2 * head].astype(F32), far[head : 2 * head].astype(F32)
    state = jnp.where(late, st_own + eo * st_far, st_far + ef * st_own).astype(BF16)
    grad = jnp.where(late, gt_far + ef * gt_own, gt_own + eo * gt_far).astype(BF16)
    decays = split_rows(dec_own + dec_far)
    for d in range(1, ring):
        out = outs[d - 1]
        ahead = place[1] + d < ring

        @pl.when(ahead)
        def _():
            out[:head] = state

        @pl.when(jnp.logical_not(ahead))
        def _():
            out[:head] = grad

        out[head:] = decays


def inner_kernel(head, skip, r, k, v, dy, w, u, levels, sums, *refs):
    if skip:
        weights, piece, stage, sem = refs[0], refs[8], refs[9], refs[10]
        refs = refs[1:8]
        into, out = copy_rows(weights, piece, skip, stage, sem)
        at_last = pl.program_id(0) == pl.num_programs(0) - 1

        @pl.when(pl.program_id(0) == 0)
        def _():
            for copy in into:
                copy.start()

        @pl.when(at_last)
        def _():
            for first, second in zip(into, out):
                first.wait()
                second.start()

    gr_out, gk_out, gv_out, self_out, eb_out, ee_out, du_out = refs
    rows, width = r.shape
    row = lax.broadcasted_iota(jnp.int32, (rows, PAIR), 0)
    row2 = lax.broadcasted_iota(jnp.int32, (rows, 2 * rows), 0)
    col2 = lax.broadcasted_iota(jnp.int32, (rows, 2 * rows), 1)
    apart = row2 ^ (col2 & (rows - 1))
    lane_r = lax.broadcasted_iota(jnp.int32, (2 * PAIR, PAIR), 0) & (PAIR - 1)
    lane_c = lax.broadcasted_iota(jnp.int32, (2 * PAIR, PAIR), 1)
    ones = jnp.where((lane_r < head) == (lane_c < head), 1.0, 0.0).astype(BF16)
    hi, lo = halves(w[...])
    both = jnp.concatenate([hi, lo], 0)
    decay = jnp.exp(mm(levels[...], both))
    ends = jnp.exp(mm(sums[...], both))
    eb_out[...], ee_out[...] = ends[:rows], ends[rows:]
    for p in range(width // PAIR):
        cols = slice(p * PAIR, (p + 1) * PAIR)
        rf, kf = r[:, cols].astype(F32), k[:, cols].astype(F32)
        vf, dyf = v[:, cols].astype(F32), dy[:, cols].astype(F32)
        dydy = block_rows(dy[:, cols], head)
        pairs = mm(dy[:, cols], block_rows(v[:, cols], head), NT)
        pairs_t = mm(v[:, cols], dydy, NT)
        gr = jnp.zeros((rows, PAIR), F32)
        gk = jnp.zeros((rows, PAIR), F32)
        scores_t = jnp.zeros((rows, 2 * rows), F32)
        m, level = 1, 0
        while m < rows:
            d = decay[level * rows : (level + 1) * rows, cols]
            right = (row & m) != 0
            rd = jnp.where(right, rf * d, 0.0).astype(BF16)
            kd = jnp.where(right, 0.0, kf * d).astype(BF16)
            kk, rr = block_rows(kd, head), block_rows(rd, head)
            near = apart < 2 * m
            a = mm(kd, rr, NT)
            scores_t = scores_t + jnp.where(near, a, 0.0)
            here = jnp.where(near, pairs, 0.0).astype(BF16)
            here_t = jnp.where(near, pairs_t, 0.0).astype(BF16)
            gr = gr + jnp.where(right, d * mm(here, kk), 0.0)
            gk = gk + jnp.where(right, 0.0, d * mm(here_t, rr))
            m, level = 2 * m, level + 1
        sh, sl = halves(dyf * vf)
        own = mm(jnp.concatenate([sh, sl], 1), ones)
        bh, bl = halves(rf * u[:, cols] * kf)
        bonus = mm(jnp.concatenate([bh, bl], 1), ones)
        gr_out[:, cols] = gr
        gk_out[:, cols] = gk
        gv_out[:, cols] = mm(scores_t.astype(BF16), dydy) + bonus * dyf
        self_out[:, cols] = own
        du_out[:, cols] = jnp.sum(rf * kf * own, 0, keepdims=True)
    if skip:

        @pl.when(at_last)
        def _():
            for copy in out:
                copy.wait()


def outer_kernel(
    head, ring, r, k, v, dy, u, gr0, gk0, gv0, own, eb, ee, st, end, far, *refs
):
    place = position()
    msgs = refs[: ring - 1]
    proj, r_gr, k_gk, at_end = refs[ring - 1 :]
    width = r.shape[1]
    late, z = place[0] == 1, place[1]
    zero = jnp.zeros((head, width), F32)
    nothing = jnp.zeros((1, width), F32)
    state, grad, past, future = zero, zero, nothing, nothing
    for d in range(1, ring):
        msg = msgs[d - 1]
        live = d <= z
        state = state + jnp.where(live, jnp.exp(past) * msg[:head].astype(F32), 0.0)
        past = past + jnp.where(live, joined(msg, head), 0.0)
    for d in range(ring - 1, 0, -1):
        msg = msgs[d - 1]
        live = d > z
        grad = grad + jnp.where(live, jnp.exp(future) * msg[:head].astype(F32), 0.0)
        future = future + jnp.where(live, joined(msg, head), 0.0)
    ef = jnp.exp(joined(far, 2 * head))
    st_in = jnp.where(late, far[:head].astype(F32) + ef * state, state)
    gt_in = jnp.where(late, grad, far[head : 2 * head].astype(F32) + ef * grad)
    at_end[...] = jnp.sum(gt_in * (jnp.exp(end[...]) * st_in + st[...]), 0, keepdims=True)
    sb, gb = st_in.astype(BF16), gt_in.astype(BF16)
    for p in range(width // PAIR):
        cols = slice(p * PAIR, (p + 1) * PAIR)
        grads = block_rows(gb[:, cols], head)
        rf, kf = r[:, cols].astype(F32), k[:, cols].astype(F32)
        after = ee[:, cols]
        gr = gr0[:, cols] + eb[:, cols] * mm(dy[:, cols], block_rows(sb[:, cols], head))
        gk = gk0[:, cols] + after * mm(v[:, cols], grads)
        gv = gv0[:, cols] + mm((kf * after).astype(BF16), grads, NT)
        s = own[:, cols] * u[:, cols]
        proj[0, :, cols] = (gr + kf * s).astype(BF16)
        proj[1, :, cols] = (gk + rf * s).astype(BF16)
        proj[2, :, cols] = gv.astype(BF16)
        r_gr[:, cols] = rf * gr
        k_gk[:, cols] = kf * gk


def decay_grad_kernel(w, r_gr, k_gk, at_end, up, lora_t, cums, up_grad, base_grad, mid_grad):
    ah, al = halves(r_gr[...])
    bh, bl = halves(k_gk[...])
    gp = (mm(cums[...], jnp.concatenate([ah, al, bh, bl], 0)) + at_end[...]) * w[...]
    gpb = gp.astype(BF16)
    up_grad[...] = mm(lora_t[...], gpb)
    base_grad[...] = jnp.sum(gp, 0, keepdims=True)
    mid_grad[...] = mm(gpb, up[...].astype(BF16), NT)


def middle_kernel(count, x, carried, mix, down, lora, *refs):
    mids, sides, (keep, send, grad_in) = refs[:count], refs[count:-3], refs[-3:]
    total = mids[0][...]
    for part in mids[1:]:
        total = total + part[...]
    mid = total * (1.0 - lora[...] * lora[...])
    grad_in[...] = mm3(mid, down[...], NT)
    down_grad = mm3(mid.T, mixed_input(x, carried, mix))
    rank, half = mid.shape[1], x.shape[1] // 2
    wide = (8, half)
    late = position()[0] == 1

    def choose(low, high, at, size):
        keep[at : at + size] = jnp.where(late, high, low).astype(BF16)
        send[at : at + size] = jnp.where(late, low, high).astype(BF16)

    up_low, up_high, base_low, base_high, du_low, du_high = [ref[...] for ref in sides]
    choose(up_low, up_high, 0, rank)
    choose(down_grad[:, :half], down_grad[:, half:], rank, rank)
    for at, low, high in ((0, base_low, base_high), (8, du_low, du_high)):
        choose(jnp.broadcast_to(low, wide), jnp.broadcast_to(high, wide), 2 * rank + at, 8)


def finish_kernel(rank, mine, theirs, up, down, base, du):
    late = position()[0] == 1
    half = mine.shape[1]
    a, b = mine[...].astype(F32), theirs[...].astype(F32)
    for at, value in ((0, jnp.where(late, b, a)), (half, jnp.where(late, a, b))):
        here = slice(at, at + half)
        up[:, here] = value[:rank]
        down[here] = value[rank : 2 * rank].T
        for ref, row in ((base, 2 * rank), (du, 2 * rank + 8)):
            size = ref.shape[1]
            for i in range(half // size):
                to = at // size + i
                ref[to : to + 1] = value[row : row + 1, i * size : (i + 1) * size]


def project_kernel(count, ring, final, *refs):
    place = position()
    lows, highs, given, mix = refs[:count], refs[count : 2 * count], refs[2 * count : 2 * count + 3], refs[2 * count + 3]
    rest, (low, high, weights, own, prior, sem) = refs[2 * count + 4 : -6], refs[-6:]
    done, outs = (rest[:-ring], rest[-ring:]) if final else ((), rest)
    rows, width = lows[0].shape[1:]
    n = weights.shape[2]
    copies = []

    def fetch(source, target):
        copy = pltpu.make_async_copy(source, target, sem.at[len(copies)])
        copy.start()
        copies.append(copy)
        return copy

    weight_copies, block_copies = [], []
    for i in range(2):
        for m in range(3):
            if i == 0:
                weight_copies.append([fetch(given[0].at[m], weights.at[0, m])])
            else:
                first, cut = given[1].at[m], given[1].shape[1]
                weight_copies.append(
                    [
                        fetch(first, weights.at[1, m, pl.ds(0, cut)]),
                        fetch(given[2].at[m], weights.at[1, m, pl.ds(cut, n - cut)]),
                    ]
                )
            if i == 0:
                places = [pl.ds(q * rows, rows) for q in range(count)]
                block_copies.append(
                    [fetch(lows[q].at[m], low.at[m, at]) for q, at in enumerate(places)]
                    + [fetch(highs[q].at[m], high.at[m, at]) for q, at in enumerate(places)]
                )

    for i in range(2):
        column = pl.ds(pl.multiple_of((place[0] if i == 0 else 1 - place[0]) * n, n), n)
        for m in range(3):
            for copy in (block_copies[m] if i == 0 else []) + weight_copies[i * 3 + m]:
                copy.wait()
            term = mm(low[m], weights[i, m, :, :width], NT) + mm(high[m], weights[i, m, :, width:], NT)
            later = mix[m : m + 1, column] * term
            own[...] = term - later if m == 0 else own[...] + (term - later)
            prior[...] = later if m == 0 else prior[...] + later
        last = lax.broadcasted_iota(jnp.int32, (rows, n), 0) == rows - 1
        top = lax.broadcasted_iota(jnp.int32, (16, n), 0) == 0

        def store(out, q):
            here = slice(q * rows, (q + 1) * rows)
            part = prior[here]
            moved = jnp.where(last, 0.0, pltpu.roll(part, rows - 1, 0))
            out[:rows, column] = (own[here] + moved).astype(BF16)
            out[rows:, column] = jnp.where(top, part[:16], 0.0).astype(BF16)

        if not final:
            for q in range(count):
                store(outs[q], q)
            continue
        for d in range(ring):
            wanted = lax.rem(place[1] - place[2] - d + 2 * ring, ring)
            for q in range(ring):

                @pl.when(wanted == q)
                def _():
                    if q == ring - 1:
                        store(outs[d], 0)
                    else:
                        outs[d][:, column] = done[q][:, column]


def per_device(
    layer_input, receptance, key_act, value_act, attention_result_sensitivity, time_first,
    decay_exponent_base, decay_shift_mix, mix_rkv, decay_adapter_down, decay_adapter_up, proj_weights,
):
    rows, cols = layer_input.shape
    heads, head = time_first.shape
    rank = decay_adapter_down.shape[1]
    n_seq, n_head = lax.axis_size("seq"), lax.axis_size("head")
    inner = n_seq // n_head
    ring = n_seq // inner
    pairs = cols // PAIR
    parts = 2
    part_cols = cols // parts
    block = min(part_cols, 2 * PAIR)
    r, k, v, dy = receptance, key_act, value_act, attention_result_sensitivity
    params = pltpu.CompilerParams(vmem_limit_bytes=VMEM)

    def shape(s, t=F32):
        return jax.ShapeDtypeStruct(s, t)

    def work(us):
        return pl.CostEstimate(flops=0, transcendentals=0, bytes_accessed=int(us * 3.5e6))

    def shift(a, distance):
        return lax.ppermute(
            a, "seq", [(i - distance, i) for i in range(n_seq) if 0 <= i - distance < n_seq]
        )

    def around(a, step):
        return lax.ppermute(a, "seq", [(i, (i + inner * step) % n_seq) for i in range(n_seq)])

    def partner(a):
        return lax.ppermute(a, "seq", [(i, i ^ 1) for i in range(n_seq)])

    def head_shift(a, d):
        return lax.ppermute(a, "head", [(i, (i + d) % n_head) for i in range(n_head)])

    def head_parts(a):
        return [a] + [head_shift(a, d) for d in range(1, n_head)]

    def after_that(value, *others):
        return lax.optimization_barrier((value, *others))[0]

    weight_rows = proj_weights.shape[1]
    cut = weight_rows // 8
    anywhere = pl.BlockSpec(memory_space=pl.ANY)
    vmem = pl.BlockSpec(memory_space=pltpu.VMEM)

    carried = shift(layer_input[rows - 1 :], 1)
    shift_mix = decay_shift_mix.reshape(1, cols)
    pre, piece = pl.pallas_call(
        adapter_kernel,
        in_specs=[vmem] * 4 + [anywhere],
        out_specs=[vmem, anywhere],
        out_shape=[shape((rows, rank)), shape((3, cut, cols), BF16)],
        scratch_shapes=[pltpu.VMEM((3, cut, cols), BF16), pltpu.SemaphoreType.DMA((6,))],
        compiler_params=params,
        cost_estimate=work(1.5),
        name="adapter_input",
    )(layer_input, carried, shift_mix, decay_adapter_down, proj_weights)
    fars = [partner(piece)]
    pres = head_parts(pre)

    sums = jnp.asarray(sum_matrix(rows), BF16)
    levels = jnp.asarray(level_matrix(rows), BF16)
    cums = jnp.asarray(cumulative_matrix(rows), BF16)
    far_rows = 2 * head + 8

    lora, lora_t, w, end, st, msg = pl.pallas_call(
        lambda *refs: decay_kernel(head, n_head, *refs),
        out_shape=[
            shape((rows, rank)), shape((rank, rows), BF16), shape((rows, cols)), shape((1, cols)),
            shape((head, cols)), shape((far_rows, cols), BF16),
        ],
        compiler_params=params,
        cost_estimate=work(3),
        name="decay_and_states",
    )(*pres, decay_exponent_base.reshape(1, cols), decay_adapter_up, r, k, v, dy, sums)

    vmem = pl.BlockSpec(memory_space=pltpu.VMEM)
    u = after_that(time_first, msg).reshape(1, cols)

    def col_block(n, width=block, offset=0):
        return pl.BlockSpec((n, width), lambda p, *_: (0, p + offset))

    def whole(s):
        return pl.BlockSpec(s, lambda p, *_: (0,) * len(s))

    steps = part_cols // block
    here = col_block(rows)

    def inside(part):
        at = lambda n: col_block(n, block, part * steps)
        extra = part == 0
        return pl.pallas_call(
            lambda *refs: inner_kernel(head, cut if extra else 0, *refs),
            grid=(steps,),
            in_specs=[at(rows)] * 5 + [at(1), whole(levels.shape), whole(sums.shape)] + [anywhere] * extra,
            out_specs=[here] * 6 + [col_block(1)] + [anywhere] * extra,
            out_shape=[shape((rows, part_cols))] * 6 + [shape((1, part_cols))]
            + [shape((3, weight_rows - cut, cols), BF16)] * extra,
            scratch_shapes=[
                pltpu.VMEM((3, weight_rows - cut, cols), BF16), pltpu.SemaphoreType.DMA((6,)),
            ] * extra,
            compiler_params=params,
            cost_estimate=work(4),
            name="inside_chunk",
        )(r, k, v, dy, after_that(w, fars[0]) if extra else w, u, levels, sums, *[proj_weights] * extra)

    inner_parts = [inside(part) for part in range(parts)]
    far, piece, inner_parts[0] = lax.optimization_barrier(
        (partner(msg), inner_parts[0][7], inner_parts[0][:7])
    )
    fars.append(partner(piece))
    out_msgs = pl.pallas_call(
        lambda *refs: pair_kernel(head, ring, *refs),
                out_shape=[shape((head + 8, cols), BF16)] * (ring - 1),
        compiler_params=params,
        cost_estimate=work(1.5),
        name="pair_states",
    )(msg, far)
    msgs = [around(m, d + 1) for d, m in enumerate(out_msgs)]

    inner_parts[1], msgs = lax.optimization_barrier((inner_parts[1], msgs))
    outer = []
    for part in range(parts):
        at = lambda n: col_block(n, block, part * steps)
        outer.append(
            pl.pallas_call(
                lambda *refs: outer_kernel(head, ring, *refs),
                grid=(steps,),
                in_specs=[at(rows)] * 4 + [at(1)] + [here] * 6
                + [at(head), at(1), at(far_rows)] + [at(head + 8)] * (ring - 1),
                out_specs=[pl.BlockSpec((3, rows, block), lambda p: (0, 0, p)), here, here, col_block(1)],
                out_shape=[
                    shape((3, rows, part_cols), BF16), shape((rows, part_cols)),
                    shape((rows, part_cols)), shape((1, part_cols)),
                ],
                compiler_params=params,
                cost_estimate=work(3),
                name="across_chunks",
            )(r, k, v, dy, u, *inner_parts[part][:6], st, end, far, *msgs)
        )
    projs = [o[0] for o in outer]

    ups, bases, mid_parts = [], [], []
    for part in range(parts):
        at = lambda n: pl.BlockSpec((n, part_cols), lambda p: (0, part))
        up_grad, base_grad, mid_grad = pl.pallas_call(
            decay_grad_kernel,
            grid=(1,),
            in_specs=[at(rows), *[whole((rows, part_cols))] * 2, whole((1, part_cols)), at(rank)]
            + [whole((rank, rows)), whole(cums.shape)],
            out_specs=[whole((rank, part_cols)), whole((1, part_cols)), whole((rows, rank))],
            out_shape=[shape((rank, part_cols)), shape((1, part_cols)), shape((rows, rank))],
            compiler_params=params,
            cost_estimate=work(2),
            name="decay_gradient",
        )(w, *outer[part][1:], decay_adapter_up, lora_t, cums)
        ups.append(up_grad)
        bases.append(base_grad)
        mid_parts.append(mid_grad)
    mid_grad = sum(mid_parts)

    mids = head_parts(mid_grad)
    dus = [part[6] for part in inner_parts]
    keep, send, grad_in = pl.pallas_call(
        lambda *refs: middle_kernel(n_head, *refs),
        in_specs=[vmem] * (5 + n_head + 3 * parts),
        out_shape=[shape((2 * rank + 16, part_cols), BF16)] * 2 + [shape((rows, cols))],
        compiler_params=params,
        cost_estimate=work(3),
        name="adapter_grads",
    )(
        layer_input, carried, shift_mix, decay_adapter_down, lora, *mids, *ups, *bases, *dus
    )

    lows, highs = [projs[0]], [projs[1]]
    for step in range(ring - 1):
        low, high = lows[-1], highs[-1]
        lows.append(around(after_that(low, mid_grad) if step == 1 else low, 1))
        highs.append(around(high, 1))

    def add(a, b):
        return (a.astype(F32) + b.astype(F32)).astype(BF16)

    got = partner(after_that(send, lows[2]))

    mix_here = lax.dynamic_slice_in_dim(after_that(mix_rkv, *out_msgs), position()[1] * cols, cols, 1)

    tall = rows + 16

    def project(low, high, done=()):
        count, final = len(low), len(done) > 0
        return pl.pallas_call(
            lambda *refs: project_kernel(count, ring, final, *refs),
            in_specs=[anywhere] * (2 * count + 3) + [vmem] * (1 + len(done)),
            out_shape=[shape((tall, cols), BF16)] * (ring if final else count),
            scratch_shapes=[
                pltpu.VMEM((3, count * rows, part_cols), BF16),
                pltpu.VMEM((3, count * rows, part_cols), BF16),
                pltpu.VMEM((inner, 3, weight_rows, cols), BF16),
                pltpu.VMEM((count * rows, weight_rows), F32),
                pltpu.VMEM((count * rows, weight_rows), F32),
                pltpu.SemaphoreType.DMA((3 * (2 * count + 3),)),
            ],
            compiler_params=pltpu.CompilerParams(vmem_limit_bytes=24 * 2**20),
            cost_estimate=work(5),
            name="projections",
        )(*low, *high, proj_weights, *fars, mix_here, *done)

    done = project(lows[:-1], highs[:-1])
    sends = project(lows[-1:], highs[-1:], done)
    token_sums = add(keep, after_that(got, *done))
    b = 1
    while b < ring:
        route = [(i, ((i // inner) ^ b) * inner + i % inner) for i in range(n_seq)]
        got = lax.ppermute(token_sums, "seq", route)
        token_sums = add(token_sums, after_that(got, sends) if b == 1 else got)
        b *= 2
    up_grad, down_grad, base_grad, du = pl.pallas_call(
        lambda *refs: finish_kernel(rank, *refs),
                out_shape=[shape((rank, cols)), shape((cols, rank)), shape((pairs, PAIR)), shape((heads, head))],
        compiler_params=params,
        cost_estimate=work(2),
        name="token_sums",
    )(token_sums, partner(token_sums))

    total = sends[0].astype(F32)
    for d in range(1, n_head):
        total = total + head_shift(sends[d], d).astype(F32)
    swap, back = [], []
    for h in range(n_head):
        for z in range(ring):
            for x in range(inner):
                source = h * n_seq + z * inner + x
                block_at = h * inner + x
                swap.append((source, z * n_seq + block_at))
                if block_at > 0:
                    back.append((source, z * n_seq + block_at - 1))
    base_grad = base_grad.reshape(cols)
    summed = lax.ppermute(total[:rows].astype(BF16), ("head", "seq"), swap)
    edge = lax.ppermute(total[rows : rows + 1], ("head", "seq"), back)
    summed = after_that(summed, up_grad, base_grad, du)
    grad_next = jnp.concatenate([grad_in[1:], shift(grad_in[:1], -1)], 0)
    adapter_term = (1.0 - decay_shift_mix) * grad_in + decay_shift_mix * grad_next
    last = lax.broadcasted_iota(jnp.int32, (rows, 1), 0) == rows - 1
    result = (summed.astype(F32) + adapter_term + jnp.where(last, edge, 0.0)).astype(BF16)
    return (result, down_grad, up_grad, base_grad, du)


def solution(mesh):
    return jax.shard_map(
        per_device,
        mesh=mesh,
        in_specs=(
            P("seq", "head"), P("seq", "head"), P("seq", "head"), P("seq", "head"), P("seq", "head"),
            P("head", None), P("head"), P("head"), P(), P("head", None), P(None, "head"),
            P(None, "seq", "head"),
        ),
        out_specs=(P("seq", "head"), P("head", None), P(None, "head"), P("head"), P("head", None)),
        check_vma=False,
    )
```

```python
import jax
import jax.numpy as jnp
import numpy as np
from jax import lax
from jax.experimental import pallas as pl
from jax.experimental.pallas import tpu as pltpu
from jax.sharding import PartitionSpec as P

F32 = jnp.float32
BF16 = jnp.bfloat16
PAIR = 128
VMEM = 56 * 2**20
SMALL = 16 * 2**20
NN = (((1,), (0,)), ((), ()))
NT = (((1,), (1,)), ((), ()))
TN = (((0,), (0,)), ((), ()))


def position():
    seq, head = lax.axis_index("seq"), lax.axis_index("head")
    inner = lax.axis_size("seq") // lax.axis_size("head")
    return lax.rem(seq, inner), lax.div(seq, inner), head


def mm(a, b, dims=NN):
    return lax.dot_general(a, b, dims, preferred_element_type=F32)


def halves(a):
    hi = a.astype(BF16)
    return hi, (a - hi.astype(F32)).astype(BF16)


def low_lanes(shape, half):
    return lax.broadcasted_iota(jnp.int32, shape, len(shape) - 1) < half


def block_rows(a, half):
    low = low_lanes(a.shape, half)
    zero = jnp.zeros_like(a)
    return jnp.concatenate([jnp.where(low, a, zero), jnp.where(low, zero, a)], 0)


def fold(a, half):
    rows = a.shape[0] // 2
    return jnp.where(low_lanes((rows, a.shape[1]), half), a[:rows], a[rows:])


def sum_matrix(rows):
    t = np.arange(rows)
    both = np.concatenate([t[:, None] > t[None, :], t[:, None] < t[None, :]], 0)
    return np.concatenate([both, both], 1).astype(np.float32)


def level_matrix(rows):
    t = np.arange(rows)
    parts = []
    m = 1
    while m < rows:
        mid = (t // (2 * m)) * 2 * m + m
        right = t >= mid
        u = t[None, :]
        take_right = (u >= mid[:, None]) & (u < t[:, None])
        take_left = (u > t[:, None]) & (u < mid[:, None])
        parts.append(np.where(right[:, None], take_right, take_left))
        m *= 2
    both = np.concatenate(parts, 0)
    return np.concatenate([both, both], 1).astype(np.float32)


def cumulative_matrix(rows):
    t = np.arange(rows)
    strict = (t[:, None] < t[None, :]).astype(np.float32)
    full = (t[:, None] <= t[None, :]).astype(np.float32)
    return np.concatenate([strict, strict, -full, -full], 1)


def split_rows(a):
    hi, lo = halves(a)
    wide = (4, a.shape[1])
    return jnp.concatenate([jnp.broadcast_to(hi, wide), jnp.broadcast_to(lo, wide)], 0)


def joined(msg, at):
    return msg[at : at + 1].astype(F32) + msg[at + 4 : at + 5].astype(F32)


def mm3(a, b, dims=NN):
    ah, al = halves(a)
    bh, bl = halves(b)
    return mm(ah, bh, dims) + (mm(ah, bl, dims) + mm(al, bh, dims))


def mixed_input(x, carried, mix):
    features = x[...].astype(F32)
    row = lax.broadcasted_iota(jnp.int32, features.shape, 0)
    previous = jnp.where(row == 0, carried[...].astype(F32), pltpu.roll(features, 1, 0))
    return features + mix[...] * (previous - features)


def copy_rows(weights, piece, at, stage, sem):
    rows = pl.ds(at, piece.shape[1])
    into = [pltpu.make_async_copy(weights.at[m, rows], stage.at[m], sem.at[m]) for m in range(3)]
    out = [pltpu.make_async_copy(stage.at[m], piece.at[m], sem.at[3 + m]) for m in range(3)]
    return into, out


def adapter_kernel(x, carried, mix, down, weights, pre, piece, stage, sem):
    into, out = copy_rows(weights, piece, 0, stage, sem)
    for copy in into:
        copy.start()
    for first, second in zip(into, out):
        first.wait()
        second.start()
    pre[...] = mm3(mixed_input(x, carried, mix), down[...])
    for copy in out:
        copy.wait()


def decay_kernel(head, count, *refs):
    pres = refs[:count]
    base, up, r, k, v, dy, sums, lora, lora_t, w_out, end, st, msg = refs[count:]
    rows = r.shape[0]
    total = pres[0][...]
    for pre in pres[1:]:
        total = total + pre[...]
    mid = jnp.tanh(total)
    lora[...] = mid
    lora_t[...] = mid.T.astype(BF16)
    w = -jnp.exp(base[...] + mm3(mid, up[...]))
    w_out[...] = w
    hi, lo = halves(w)
    args = mm(sums[...], jnp.concatenate([hi, lo], 0))
    before, after = args[:rows], args[rows:]
    final = before[rows - 1 :] + w[rows - 1 :]
    end[...] = final
    from_start, to_end = jnp.exp(before), jnp.exp(after)
    kf = (k[...].astype(F32) * to_end).astype(BF16)
    rb = (r[...].astype(F32) * from_start).astype(BF16)
    for p in range(r.shape[1] // PAIR):
        cols = slice(p * PAIR, (p + 1) * PAIR)
        state = fold(mm(v[:, cols], kf[:, cols], TN), head)
        st[:, cols] = state
        msg[:head, cols] = state.astype(BF16)
        msg[head : 2 * head, cols] = fold(mm(dy[:, cols], rb[:, cols], TN), head).astype(BF16)
    msg[2 * head :] = split_rows(final)


def pair_kernel(head, ring, own, far, *outs):
    place = position()
    late = place[0] == 1
    dec_own, dec_far = joined(own, 2 * head), joined(far, 2 * head)
    eo, ef = jnp.exp(dec_own), jnp.exp(dec_far)
    st_own, st_far = own[:head].astype(F32), far[:head].astype(F32)
    gt_own, gt_far = own[head : 2 * head].astype(F32), far[head : 2 * head].astype(F32)
    state = jnp.where(late, st_own + eo * st_far, st_far + ef * st_own).astype(BF16)
    grad = jnp.where(late, gt_far + ef * gt_own, gt_own + eo * gt_far).astype(BF16)
    decays = split_rows(dec_own + dec_far)
    for d in range(1, ring):
        out = outs[d - 1]
        ahead = place[1] + d < ring

        @pl.when(ahead)
        def _():
            out[:head] = state

        @pl.when(jnp.logical_not(ahead))
        def _():
            out[:head] = grad

        out[head:] = decays


def inner_kernel(head, skip, r, k, v, dy, w, u, levels, sums, *refs):
    if skip:
        weights, piece, stage, sem = refs[0], refs[8], refs[9], refs[10]
        refs = refs[1:8]
        into, out = copy_rows(weights, piece, skip, stage, sem)
        at_last = pl.program_id(0) == pl.num_programs(0) - 1

        @pl.when(pl.program_id(0) == 0)
        def _():
            for copy in into:
                copy.start()

        @pl.when(at_last)
        def _():
            for first, second in zip(into, out):
                first.wait()
                second.start()

    gr_out, gk_out, gv_out, self_out, eb_out, ee_out, du_out = refs
    rows, width = r.shape
    row = lax.broadcasted_iota(jnp.int32, (rows, PAIR), 0)
    row2 = lax.broadcasted_iota(jnp.int32, (rows, 2 * rows), 0)
    col2 = lax.broadcasted_iota(jnp.int32, (rows, 2 * rows), 1)
    apart = row2 ^ (col2 & (rows - 1))
    lane_r = lax.broadcasted_iota(jnp.int32, (2 * PAIR, PAIR), 0) & (PAIR - 1)
    lane_c = lax.broadcasted_iota(jnp.int32, (2 * PAIR, PAIR), 1)
    ones = jnp.where((lane_r < head) == (lane_c < head), 1.0, 0.0).astype(BF16)
    hi, lo = halves(w[...])
    both = jnp.concatenate([hi, lo], 0)
    decay = jnp.exp(mm(levels[...], both))
    ends = jnp.exp(mm(sums[...], both))
    eb_out[...], ee_out[...] = ends[:rows], ends[rows:]
    for p in range(width // PAIR):
        cols = slice(p * PAIR, (p + 1) * PAIR)
        rf, kf = r[:, cols].astype(F32), k[:, cols].astype(F32)
        vf, dyf = v[:, cols].astype(F32), dy[:, cols].astype(F32)
        dydy = block_rows(dy[:, cols], head)
        pairs = mm(dy[:, cols], block_rows(v[:, cols], head), NT)
        pairs_t = mm(v[:, cols], dydy, NT)
        gr = jnp.zeros((rows, PAIR), F32)
        gk = jnp.zeros((rows, PAIR), F32)
        scores_t = jnp.zeros((rows, 2 * rows), F32)
        m, level = 1, 0
        while m < rows:
            d = decay[level * rows : (level + 1) * rows, cols]
            right = (row & m) != 0
            rd = jnp.where(right, rf * d, 0.0).astype(BF16)
            kd = jnp.where(right, 0.0, kf * d).astype(BF16)
            kk, rr = block_rows(kd, head), block_rows(rd, head)
            near = apart < 2 * m
            a = mm(kd, rr, NT)
            scores_t = scores_t + jnp.where(near, a, 0.0)
            here = jnp.where(near, pairs, 0.0).astype(BF16)
            here_t = jnp.where(near, pairs_t, 0.0).astype(BF16)
            gr = gr + jnp.where(right, d * mm(here, kk), 0.0)
            gk = gk + jnp.where(right, 0.0, d * mm(here_t, rr))
            m, level = 2 * m, level + 1
        sh, sl = halves(dyf * vf)
        own = mm(jnp.concatenate([sh, sl], 1), ones)
        bh, bl = halves(rf * u[:, cols] * kf)
        bonus = mm(jnp.concatenate([bh, bl], 1), ones)
        gr_out[:, cols] = gr
        gk_out[:, cols] = gk
        gv_out[:, cols] = mm(scores_t.astype(BF16), dydy) + bonus * dyf
        self_out[:, cols] = own
        du_out[:, cols] = jnp.sum(rf * kf * own, 0, keepdims=True)
    if skip:

        @pl.when(at_last)
        def _():
            for copy in out:
                copy.wait()


def outer_kernel(
    head, ring, r, k, v, dy, u, gr0, gk0, gv0, own, eb, ee, st, end, far, *refs
):
    place = position()
    msgs = refs[: ring - 1]
    proj, r_gr, k_gk, at_end = refs[ring - 1 :]
    width = r.shape[1]
    late, z = place[0] == 1, place[1]
    zero = jnp.zeros((head, width), F32)
    nothing = jnp.zeros((1, width), F32)
    state, grad, past, future = zero, zero, nothing, nothing
    for d in range(1, ring):
        msg = msgs[d - 1]
        live = d <= z
        state = state + jnp.where(live, jnp.exp(past) * msg[:head].astype(F32), 0.0)
        past = past + jnp.where(live, joined(msg, head), 0.0)
    for d in range(ring - 1, 0, -1):
        msg = msgs[d - 1]
        live = d > z
        grad = grad + jnp.where(live, jnp.exp(future) * msg[:head].astype(F32), 0.0)
        future = future + jnp.where(live, joined(msg, head), 0.0)
    ef = jnp.exp(joined(far, 2 * head))
    st_in = jnp.where(late, far[:head].astype(F32) + ef * state, state)
    gt_in = jnp.where(late, grad, far[head : 2 * head].astype(F32) + ef * grad)
    at_end[...] = jnp.sum(gt_in * (jnp.exp(end[...]) * st_in + st[...]), 0, keepdims=True)
    sb, gb = st_in.astype(BF16), gt_in.astype(BF16)
    for p in range(width // PAIR):
        cols = slice(p * PAIR, (p + 1) * PAIR)
        grads = block_rows(gb[:, cols], head)
        rf, kf = r[:, cols].astype(F32), k[:, cols].astype(F32)
        after = ee[:, cols]
        gr = gr0[:, cols] + eb[:, cols] * mm(dy[:, cols], block_rows(sb[:, cols], head))
        gk = gk0[:, cols] + after * mm(v[:, cols], grads)
        gv = gv0[:, cols] + mm((kf * after).astype(BF16), grads, NT)
        s = own[:, cols] * u[:, cols]
        proj[0, :, cols] = (gr + kf * s).astype(BF16)
        proj[1, :, cols] = (gk + rf * s).astype(BF16)
        proj[2, :, cols] = gv.astype(BF16)
        r_gr[:, cols] = rf * gr
        k_gk[:, cols] = kf * gk


def decay_grad_kernel(w, r_gr, k_gk, at_end, up, lora_t, cums, up_grad, base_grad, mid_grad):
    ah, al = halves(r_gr[...])
    bh, bl = halves(k_gk[...])
    gp = (mm(cums[...], jnp.concatenate([ah, al, bh, bl], 0)) + at_end[...]) * w[...]
    gpb = gp.astype(BF16)
    up_grad[...] = mm(lora_t[...], gpb)
    base_grad[...] = jnp.sum(gp, 0, keepdims=True)
    mid_grad[...] = mm(gpb, up[...].astype(BF16), NT)


def middle_kernel(count, x, carried, mix, down, lora, *refs):
    mids, sides, (keep, send, grad_in) = refs[:count], refs[count:-3], refs[-3:]
    total = mids[0][...]
    for part in mids[1:]:
        total = total + part[...]
    mid = total * (1.0 - lora[...] * lora[...])
    grad_in[...] = mm3(mid, down[...], NT)
    down_grad = mm3(mid.T, mixed_input(x, carried, mix))
    rank, half = mid.shape[1], x.shape[1] // 2
    wide = (8, half)
    for ref in (keep, send):
        ref[...] = jnp.zeros_like(ref)
    late = position()[0] == 1

    def choose(low, high, at, size):
        keep[at : at + size] = jnp.where(late, high, low).astype(BF16)
        send[at : at + size] = jnp.where(late, low, high).astype(BF16)

    up_low, up_high, base_low, base_high, du_low, du_high = [ref[...] for ref in sides]
    choose(up_low, up_high, 0, rank)
    choose(down_grad[:, :half], down_grad[:, half:], rank, rank)
    for at, low, high in ((0, base_low, base_high), (8, du_low, du_high)):
        choose(jnp.broadcast_to(low, wide), jnp.broadcast_to(high, wide), 2 * rank + at, 8)


def split_kernel(ring, keep, got, *refs):
    outs, total = refs[:-1], refs[-1]
    total[...] = keep[...].astype(F32) + got[...].astype(F32)
    z, chunk = position()[1], outs[0].shape[0]
    for d, out in enumerate(outs):
        at = pl.multiple_of(lax.rem(z + d, ring) * chunk, 8)
        out[...] = total[pl.ds(at, chunk)].astype(out.dtype)


def finish_kernel(rank, ring, mine, theirs, up, down, base, du, full):
    x, z, _ = position()
    late = x == 1
    half = mine.shape[1]
    chunk = mine.shape[0] // ring
    a, b = mine[...].astype(F32), theirs[...].astype(F32)
    low, high = jnp.where(late, b, a), jnp.where(late, a, b)
    for q in range(ring):
        to = pl.ds(pl.multiple_of(lax.rem(z - q + ring, ring) * chunk, 8), chunk)
        here = slice(q * chunk, (q + 1) * chunk)
        full[to, :half] = low[here]
        full[to, half:] = high[here]
    up[...] = full[:rank]
    down[...] = full[rank : 2 * rank].T
    for ref, row in ((base, 2 * rank), (du, 2 * rank + 8)):
        size = ref.shape[1]
        for i in range(ref.shape[0]):
            ref[i : i + 1] = full[row : row + 1, i * size : (i + 1) * size]


def project_kernel(count, ring, final, *refs):
    place = position()
    lows, highs, given, mix = refs[:count], refs[count : 2 * count], refs[2 * count : 2 * count + 3], refs[2 * count + 3]
    rest, (low, high, weights, own, prior, sem) = refs[2 * count + 4 : -6], refs[-6:]
    done, outs = (rest[:-ring], rest[-ring:]) if final else ((), rest)
    rows, width = lows[0].shape[1:]
    n = weights.shape[2]
    copies = []

    def fetch(source, target):
        copy = pltpu.make_async_copy(source, target, sem.at[len(copies)])
        copy.start()
        copies.append(copy)
        return copy

    weight_copies, block_copies = [], []
    for i in range(2):
        for m in range(3):
            if i == 0:
                weight_copies.append([fetch(given[0].at[m], weights.at[0, m])])
            else:
                first, cut = given[1].at[m], given[1].shape[1]
                weight_copies.append(
                    [
                        fetch(first, weights.at[1, m, pl.ds(0, cut)]),
                        fetch(given[2].at[m], weights.at[1, m, pl.ds(cut, n - cut)]),
                    ]
                )
            if i == 0:
                places = [pl.ds(q * rows, rows) for q in range(count)]
                block_copies.append(
                    [fetch(lows[q].at[m], low.at[m, at]) for q, at in enumerate(places)]
                    + [fetch(highs[q].at[m], high.at[m, at]) for q, at in enumerate(places)]
                )

    for i in range(2):
        column = pl.ds(pl.multiple_of((place[0] if i == 0 else 1 - place[0]) * n, n), n)
        for m in range(3):
            for copy in (block_copies[m] if i == 0 else []) + weight_copies[i * 3 + m]:
                copy.wait()
            term = mm(low[m], weights[i, m, :, :width], NT) + mm(high[m], weights[i, m, :, width:], NT)
            later = mix[m : m + 1, column] * term
            own[...] = term - later if m == 0 else own[...] + (term - later)
            prior[...] = later if m == 0 else prior[...] + later
        last = lax.broadcasted_iota(jnp.int32, (rows, n), 0) == rows - 1
        top = lax.broadcasted_iota(jnp.int32, (16, n), 0) == 0

        def store(out, q):
            here = slice(q * rows, (q + 1) * rows)
            part = prior[here]
            moved = jnp.where(last, 0.0, pltpu.roll(part, rows - 1, 0))
            out[:rows, column] = (own[here] + moved).astype(BF16)
            out[rows:, column] = jnp.where(top, part[:16], 0.0).astype(BF16)

        if not final:
            for q in range(count):
                store(outs[q], q)
            continue
        for d in range(ring):
            wanted = lax.rem(place[1] - place[2] - d + 2 * ring, ring)
            for q in range(ring):

                @pl.when(wanted == q)
                def _():
                    if q == ring - 1:
                        store(outs[d], 0)
                    else:
                        outs[d][:, column] = done[q][:, column]


def per_device(
    layer_input, receptance, key_act, value_act, attention_result_sensitivity, time_first,
    decay_exponent_base, decay_shift_mix, mix_rkv, decay_adapter_down, decay_adapter_up, proj_weights,
):
    rows, cols = layer_input.shape
    heads, head = time_first.shape
    rank = decay_adapter_down.shape[1]
    n_seq, n_head = lax.axis_size("seq"), lax.axis_size("head")
    inner = n_seq // n_head
    ring = n_seq // inner
    pairs = cols // PAIR
    parts = 2
    part_cols = cols // parts
    block = min(part_cols, 2 * PAIR)
    r, k, v, dy = receptance, key_act, value_act, attention_result_sensitivity
    params = pltpu.CompilerParams(vmem_limit_bytes=VMEM)
    small = pltpu.CompilerParams(vmem_limit_bytes=SMALL)

    def shape(s, t=F32):
        return jax.ShapeDtypeStruct(s, t)

    def work(us):
        return pl.CostEstimate(flops=0, transcendentals=0, bytes_accessed=int(us * 3.5e6))

    def shift(a, distance):
        return lax.ppermute(
            a, "seq", [(i - distance, i) for i in range(n_seq) if 0 <= i - distance < n_seq]
        )

    def around(a, step):
        return lax.ppermute(a, "seq", [(i, (i + inner * step) % n_seq) for i in range(n_seq)])

    def partner(a):
        return lax.ppermute(a, "seq", [(i, i ^ 1) for i in range(n_seq)])

    def head_shift(a, d):
        return lax.ppermute(a, "head", [(i, (i + d) % n_head) for i in range(n_head)])

    def head_parts(a):
        return [a] + [head_shift(a, d) for d in range(1, n_head)]

    def after_that(value, *others):
        return lax.optimization_barrier((value, *others))[0]

    weight_rows = proj_weights.shape[1]
    cut = weight_rows // 8
    anywhere = pl.BlockSpec(memory_space=pl.ANY)
    vmem = pl.BlockSpec(memory_space=pltpu.VMEM)

    carried = shift(layer_input[rows - 1 :], 1)
    shift_mix = decay_shift_mix.reshape(1, cols)
    pre, piece = pl.pallas_call(
        adapter_kernel,
        in_specs=[vmem] * 4 + [anywhere],
        out_specs=[vmem, anywhere],
        out_shape=[shape((rows, rank)), shape((3, cut, cols), BF16)],
        scratch_shapes=[pltpu.VMEM((3, cut, cols), BF16), pltpu.SemaphoreType.DMA((6,))],
        compiler_params=params,
        cost_estimate=work(1.5),
        name="adapter_input",
    )(layer_input, carried, shift_mix, decay_adapter_down, proj_weights)
    fars = [partner(piece)]
    pres = head_parts(pre)

    sums = jnp.asarray(sum_matrix(rows), BF16)
    levels = jnp.asarray(level_matrix(rows), BF16)
    cums = jnp.asarray(cumulative_matrix(rows), BF16)
    far_rows = 2 * head + 8

    lora, lora_t, w, end, st, msg = pl.pallas_call(
        lambda *refs: decay_kernel(head, n_head, *refs),
        out_shape=[
            shape((rows, rank)), shape((rank, rows), BF16), shape((rows, cols)), shape((1, cols)),
            shape((head, cols)), shape((far_rows, cols), BF16),
        ],
        compiler_params=params,
        cost_estimate=work(3),
        name="decay_and_states",
    )(*pres, decay_exponent_base.reshape(1, cols), decay_adapter_up, r, k, v, dy, sums)

    vmem = pl.BlockSpec(memory_space=pltpu.VMEM)
    u = after_that(time_first, msg).reshape(1, cols)

    def col_block(n, width=block, offset=0):
        return pl.BlockSpec((n, width), lambda p, *_: (0, p + offset))

    def whole(s):
        return pl.BlockSpec(s, lambda p, *_: (0,) * len(s))

    steps = part_cols // block
    here = col_block(rows)

    def inside(part):
        at = lambda n: col_block(n, block, part * steps)
        extra = part == 0
        return pl.pallas_call(
            lambda *refs: inner_kernel(head, cut if extra else 0, *refs),
            grid=(steps,),
            in_specs=[at(rows)] * 5 + [at(1), whole(levels.shape), whole(sums.shape)] + [anywhere] * extra,
            out_specs=[here] * 6 + [col_block(1)] + [anywhere] * extra,
            out_shape=[shape((rows, part_cols))] * 6 + [shape((1, part_cols))]
            + [shape((3, weight_rows - cut, cols), BF16)] * extra,
            scratch_shapes=[
                pltpu.VMEM((3, weight_rows - cut, cols), BF16), pltpu.SemaphoreType.DMA((6,)),
            ] * extra,
            compiler_params=params,
            cost_estimate=work(4),
            name="inside_chunk",
        )(r, k, v, dy, after_that(w, fars[0]) if extra else w, u, levels, sums, *[proj_weights] * extra)

    inner_parts = [inside(part) for part in range(parts)]
    far, piece, inner_parts[0] = lax.optimization_barrier(
        (partner(msg), inner_parts[0][7], inner_parts[0][:7])
    )
    fars.append(partner(piece))
    out_msgs = pl.pallas_call(
        lambda *refs: pair_kernel(head, ring, *refs),
                out_shape=[shape((head + 8, cols), BF16)] * (ring - 1),
        compiler_params=params,
        cost_estimate=work(1.5),
        name="pair_states",
    )(msg, far)
    msgs = [around(m, d + 1) for d, m in enumerate(out_msgs)]

    inner_parts[1], msgs = lax.optimization_barrier((inner_parts[1], msgs))
    outer = []
    for part in range(parts):
        at = lambda n: col_block(n, block, part * steps)
        outer.append(
            pl.pallas_call(
                lambda *refs: outer_kernel(head, ring, *refs),
                grid=(steps,),
                in_specs=[at(rows)] * 4 + [at(1)] + [here] * 6
                + [at(head), at(1), at(far_rows)] + [at(head + 8)] * (ring - 1),
                out_specs=[pl.BlockSpec((3, rows, block), lambda p: (0, 0, p)), here, here, col_block(1)],
                out_shape=[
                    shape((3, rows, part_cols), BF16), shape((rows, part_cols)),
                    shape((rows, part_cols)), shape((1, part_cols)),
                ],
                compiler_params=params,
                cost_estimate=work(3),
                name="across_chunks",
            )(r, k, v, dy, u, *inner_parts[part][:6], st, end, far, *msgs)
        )
    projs = [o[0] for o in outer]

    ups, bases, mid_parts = [], [], []
    for part in range(parts):
        at = lambda n: pl.BlockSpec((n, part_cols), lambda p: (0, part))
        up_grad, base_grad, mid_grad = pl.pallas_call(
            decay_grad_kernel,
            grid=(1,),
            in_specs=[at(rows), *[whole((rows, part_cols))] * 2, whole((1, part_cols)), at(rank)]
            + [whole((rank, rows)), whole(cums.shape)],
            out_specs=[whole((rank, part_cols)), whole((1, part_cols)), whole((rows, rank))],
            out_shape=[shape((rank, part_cols)), shape((1, part_cols)), shape((rows, rank))],
            compiler_params=params,
            cost_estimate=work(2),
            name="decay_gradient",
        )(w, *outer[part][1:], decay_adapter_up, lora_t, cums)
        ups.append(up_grad)
        bases.append(base_grad)
        mid_parts.append(mid_grad)
    mid_grad = sum(mid_parts)

    chunk = -(-(2 * rank + 16) // (8 * ring)) * 8
    mids = head_parts(mid_grad)
    dus = [part[6] for part in inner_parts]
    keep, send, grad_in = pl.pallas_call(
        lambda *refs: middle_kernel(n_head, *refs),
        in_specs=[vmem] * (5 + n_head + 3 * parts),
        out_shape=[shape((ring * chunk, part_cols), BF16)] * 2 + [shape((rows, cols))],
        compiler_params=params,
        cost_estimate=work(3),
        name="adapter_grads",
    )(
        layer_input, carried, shift_mix, decay_adapter_down, lora, *mids, *ups, *bases, *dus
    )

    lows, highs = [projs[0]], [projs[1]]
    for step in range(ring - 1):
        low, high = lows[-1], highs[-1]
        ready = [(), (mid_grad,), (keep,)][step] if step < 3 else ()
        lows.append(around(after_that(low, *ready), 1))
        highs.append(around(high, 1))

    got = partner(after_that(send, lows[2]))

    mix_here = lax.dynamic_slice_in_dim(after_that(mix_rkv, *out_msgs), position()[1] * cols, cols, 1)

    tall = rows + 16

    def project(low, high, done=()):
        count, final = len(low), len(done) > 0
        return pl.pallas_call(
            lambda *refs: project_kernel(count, ring, final, *refs),
            in_specs=[anywhere if final else pl.BlockSpec(memory_space=pltpu.HBM)] * (2 * count)
            + [anywhere] * 3 + [vmem] * (1 + len(done)),
            out_shape=[shape((tall, cols), BF16)] * (ring if final else count),
            scratch_shapes=[
                pltpu.VMEM((3, count * rows, part_cols), BF16),
                pltpu.VMEM((3, count * rows, part_cols), BF16),
                pltpu.VMEM((inner, 3, weight_rows, cols), BF16),
                pltpu.VMEM((count * rows, weight_rows), F32),
                pltpu.VMEM((count * rows, weight_rows), F32),
                pltpu.SemaphoreType.DMA((3 * (2 * count + 3),)),
            ],
            compiler_params=pltpu.CompilerParams(vmem_limit_bytes=24 * 2**20),
            cost_estimate=work(5),
            name="projections",
        )(*low, *high, proj_weights, *fars, mix_here, *done)

    done = project(lows[:-1], highs[:-1])
    sends = project(lows[-1:], highs[-1:], done)
    chunks = pl.pallas_call(
        lambda *refs: split_kernel(ring, *refs),
        out_shape=[shape((chunk, part_cols))] + [shape((chunk, part_cols), BF16)] * (ring - 1),
        scratch_shapes=[pltpu.VMEM((ring * chunk, part_cols), F32)],
        compiler_params=small,
        cost_estimate=work(2),
        name="token_chunks",
    )(keep, after_that(got, *done))
    mine = chunks[0]
    for d in range(1, ring):
        mine = mine + after_that(around(chunks[d], d), *sends).astype(F32)
    mine = mine.astype(BF16)
    mine = jnp.concatenate([mine] + [around(mine, q) for q in range(1, ring)], 0)
    up_grad, down_grad, base_grad, du = pl.pallas_call(
        lambda *refs: finish_kernel(rank, ring, *refs),
        out_shape=[shape((rank, cols)), shape((cols, rank)), shape((pairs, PAIR)), shape((heads, head))],
        scratch_shapes=[pltpu.VMEM((ring * chunk, cols), F32)],
        compiler_params=small,
        cost_estimate=work(2),
        name="token_sums",
    )(mine, partner(mine))

    total = sends[0].astype(F32)
    for d in range(1, n_head):
        total = total + head_shift(sends[d], d).astype(F32)
    swap, back = [], []
    for h in range(n_head):
        for z in range(ring):
            for x in range(inner):
                source = h * n_seq + z * inner + x
                block_at = h * inner + x
                swap.append((source, z * n_seq + block_at))
                if block_at > 0:
                    back.append((source, z * n_seq + block_at - 1))
    base_grad = base_grad.reshape(cols)
    summed = lax.ppermute(total[:rows].astype(BF16), ("head", "seq"), swap)
    edge = lax.ppermute(total[rows : rows + 1], ("head", "seq"), back)
    summed = after_that(summed, up_grad, base_grad, du)
    grad_next = jnp.concatenate([grad_in[1:], shift(grad_in[:1], -1)], 0)
    adapter_term = (1.0 - decay_shift_mix) * grad_in + decay_shift_mix * grad_next
    last = lax.broadcasted_iota(jnp.int32, (rows, 1), 0) == rows - 1
    result = (summed.astype(F32) + adapter_term + jnp.where(last, edge, 0.0)).astype(BF16)
    return (result, down_grad, up_grad, base_grad, du)


def solution(mesh):
    return jax.shard_map(
        per_device,
        mesh=mesh,
        in_specs=(
            P("seq", "head"), P("seq", "head"), P("seq", "head"), P("seq", "head"), P("seq", "head"),
            P("head", None), P("head"), P("head"), P(), P("head", None), P(None, "head"),
            P(None, "seq", "head"),
        ),
        out_specs=(P("seq", "head"), P("head", None), P(None, "head"), P("head"), P("head", None)),
        check_vma=False,
    )
```

```python
import jax
import jax.numpy as jnp
import numpy as np
from jax import lax
from jax.experimental import pallas as pl
from jax.experimental.pallas import tpu as pltpu
from jax.sharding import PartitionSpec as P

F32 = jnp.float32
BF16 = jnp.bfloat16
PAIR = 128
VMEM = 56 * 2**20
NN = (((1,), (0,)), ((), ()))
NT = (((1,), (1,)), ((), ()))
TN = (((0,), (0,)), ((), ()))


def position():
    seq, head = lax.axis_index("seq"), lax.axis_index("head")
    inner = lax.axis_size("seq") // lax.axis_size("head")
    return lax.rem(seq, inner), lax.div(seq, inner), head


def mm(a, b, dims=NN):
    return lax.dot_general(a, b, dims, preferred_element_type=F32)


def halves(a):
    hi = a.astype(BF16)
    return hi, (a - hi.astype(F32)).astype(BF16)


def low_lanes(shape, half):
    return lax.broadcasted_iota(jnp.int32, shape, len(shape) - 1) < half


def block_rows(a, half):
    low = low_lanes(a.shape, half)
    zero = jnp.zeros_like(a)
    return jnp.concatenate([jnp.where(low, a, zero), jnp.where(low, zero, a)], 0)


def fold(a, half):
    rows = a.shape[0] // 2
    return jnp.where(low_lanes((rows, a.shape[1]), half), a[:rows], a[rows:])


def sum_matrix(rows):
    t = np.arange(rows)
    both = np.concatenate([t[:, None] > t[None, :], t[:, None] < t[None, :]], 0)
    return np.concatenate([both, both], 1).astype(np.float32)


def level_matrix(rows):
    t = np.arange(rows)
    parts = []
    m = 1
    while m < rows:
        mid = (t // (2 * m)) * 2 * m + m
        right = t >= mid
        u = t[None, :]
        take_right = (u >= mid[:, None]) & (u < t[:, None])
        take_left = (u > t[:, None]) & (u < mid[:, None])
        parts.append(np.where(right[:, None], take_right, take_left))
        m *= 2
    both = np.concatenate(parts, 0)
    return np.concatenate([both, both], 1).astype(np.float32)


def cumulative_matrix(rows):
    t = np.arange(rows)
    strict = (t[:, None] < t[None, :]).astype(np.float32)
    full = (t[:, None] <= t[None, :]).astype(np.float32)
    return np.concatenate([strict, strict, -full, -full], 1)


def split_rows(a):
    hi, lo = halves(a)
    wide = (4, a.shape[1])
    return jnp.concatenate([jnp.broadcast_to(hi, wide), jnp.broadcast_to(lo, wide)], 0)


def joined(msg, at):
    return msg[at : at + 1].astype(F32) + msg[at + 4 : at + 5].astype(F32)


def mm3(a, b, dims=NN):
    ah, al = halves(a)
    bh, bl = halves(b)
    return mm(ah, bh, dims) + (mm(ah, bl, dims) + mm(al, bh, dims))


def mixed_input(x, carried, mix):
    features = x[...].astype(F32)
    row = lax.broadcasted_iota(jnp.int32, features.shape, 0)
    previous = jnp.where(row == 0, carried[...].astype(F32), pltpu.roll(features, 1, 0))
    return features + mix[...] * (previous - features)


def copy_rows(weights, piece, at, stage, sem):
    rows = pl.ds(at, piece.shape[1])
    into = [pltpu.make_async_copy(weights.at[m, rows], stage.at[m], sem.at[m]) for m in range(3)]
    out = [pltpu.make_async_copy(stage.at[m], piece.at[m], sem.at[3 + m]) for m in range(3)]
    return into, out


def adapter_kernel(x, carried, mix, down, pre):
    pre[...] = mm3(mixed_input(x, carried, mix), down[...])


def decay_kernel(head, count, *refs):
    pres = refs[:count]
    base, up, r, k, v, dy, sums, lora, lora_t, w_out, end, st, msg = refs[count:]
    rows = r.shape[0]
    total = pres[0][...]
    for pre in pres[1:]:
        total = total + pre[...]
    mid = jnp.tanh(total)
    lora[...] = mid
    lora_t[...] = mid.T.astype(BF16)
    w = -jnp.exp(base[...] + mm3(mid, up[...]))
    w_out[...] = w
    hi, lo = halves(w)
    args = mm(sums[...], jnp.concatenate([hi, lo], 0))
    before, after = args[:rows], args[rows:]
    final = before[rows - 1 :] + w[rows - 1 :]
    end[...] = final
    from_start, to_end = jnp.exp(before), jnp.exp(after)
    kf = (k[...].astype(F32) * to_end).astype(BF16)
    rb = (r[...].astype(F32) * from_start).astype(BF16)
    for p in range(r.shape[1] // PAIR):
        cols = slice(p * PAIR, (p + 1) * PAIR)
        state = fold(mm(v[:, cols], kf[:, cols], TN), head)
        st[:, cols] = state
        msg[:head, cols] = state.astype(BF16)
        msg[head : 2 * head, cols] = fold(mm(dy[:, cols], rb[:, cols], TN), head).astype(BF16)
    msg[2 * head :] = split_rows(final)


def pair_kernel(head, ring, own, far, *outs):
    place = position()
    late = place[0] == 1
    dec_own, dec_far = joined(own, 2 * head), joined(far, 2 * head)
    eo, ef = jnp.exp(dec_own), jnp.exp(dec_far)
    st_own, st_far = own[:head].astype(F32), far[:head].astype(F32)
    gt_own, gt_far = own[head : 2 * head].astype(F32), far[head : 2 * head].astype(F32)
    state = jnp.where(late, st_own + eo * st_far, st_far + ef * st_own).astype(BF16)
    grad = jnp.where(late, gt_far + ef * gt_own, gt_own + eo * gt_far).astype(BF16)
    decays = split_rows(dec_own + dec_far)
    for d in range(1, ring):
        out = outs[d - 1]
        ahead = place[1] + d < ring

        @pl.when(ahead)
        def _():
            out[:head] = state

        @pl.when(jnp.logical_not(ahead))
        def _():
            out[:head] = grad

        out[head:] = decays


def inner_kernel(head, skip, r, k, v, dy, w, u, levels, sums, *refs):
    if skip:
        weights, piece, stage, sem = refs[0], refs[8], refs[9], refs[10]
        refs = refs[1:8]
        into, out = copy_rows(weights, piece, skip, stage, sem)
        at_last = pl.program_id(0) == pl.num_programs(0) - 1

        @pl.when(pl.program_id(0) == 0)
        def _():
            for copy in into:
                copy.start()

        @pl.when(at_last)
        def _():
            for first, second in zip(into, out):
                first.wait()
                second.start()

    gr_out, gk_out, gv_out, self_out, eb_out, ee_out, du_out = refs
    rows, width = r.shape
    row = lax.broadcasted_iota(jnp.int32, (rows, PAIR), 0)
    row2 = lax.broadcasted_iota(jnp.int32, (rows, 2 * rows), 0)
    col2 = lax.broadcasted_iota(jnp.int32, (rows, 2 * rows), 1)
    apart = row2 ^ (col2 & (rows - 1))
    lane_r = lax.broadcasted_iota(jnp.int32, (2 * PAIR, PAIR), 0) & (PAIR - 1)
    lane_c = lax.broadcasted_iota(jnp.int32, (2 * PAIR, PAIR), 1)
    ones = jnp.where((lane_r < head) == (lane_c < head), 1.0, 0.0).astype(BF16)
    hi, lo = halves(w[...])
    both = jnp.concatenate([hi, lo], 0)
    decay = jnp.exp(mm(levels[...], both))
    ends = jnp.exp(mm(sums[...], both))
    eb_out[...], ee_out[...] = ends[:rows], ends[rows:]
    for p in range(width // PAIR):
        cols = slice(p * PAIR, (p + 1) * PAIR)
        rf, kf = r[:, cols].astype(F32), k[:, cols].astype(F32)
        vf, dyf = v[:, cols].astype(F32), dy[:, cols].astype(F32)
        dydy = block_rows(dy[:, cols], head)
        pairs = mm(dy[:, cols], block_rows(v[:, cols], head), NT)
        pairs_t = mm(v[:, cols], dydy, NT)
        gr = jnp.zeros((rows, PAIR), F32)
        gk = jnp.zeros((rows, PAIR), F32)
        scores_t = jnp.zeros((rows, 2 * rows), F32)
        m, level = 1, 0
        while m < rows:
            d = decay[level * rows : (level + 1) * rows, cols]
            right = (row & m) != 0
            rd = jnp.where(right, rf * d, 0.0).astype(BF16)
            kd = jnp.where(right, 0.0, kf * d).astype(BF16)
            kk, rr = block_rows(kd, head), block_rows(rd, head)
            near = apart < 2 * m
            a = mm(kd, rr, NT)
            scores_t = scores_t + jnp.where(near, a, 0.0)
            here = jnp.where(near, pairs, 0.0).astype(BF16)
            here_t = jnp.where(near, pairs_t, 0.0).astype(BF16)
            gr = gr + jnp.where(right, d * mm(here, kk), 0.0)
            gk = gk + jnp.where(right, 0.0, d * mm(here_t, rr))
            m, level = 2 * m, level + 1
        sh, sl = halves(dyf * vf)
        own = mm(jnp.concatenate([sh, sl], 1), ones)
        bh, bl = halves(rf * u[:, cols] * kf)
        bonus = mm(jnp.concatenate([bh, bl], 1), ones)
        gr_out[:, cols] = gr
        gk_out[:, cols] = gk
        gv_out[:, cols] = mm(scores_t.astype(BF16), dydy) + bonus * dyf
        self_out[:, cols] = own
        du_out[:, cols] = jnp.sum(rf * kf * own, 0, keepdims=True)
    if skip:

        @pl.when(at_last)
        def _():
            for copy in out:
                copy.wait()


def outer_kernel(
    head, ring, r, k, v, dy, u, gr0, gk0, gv0, own, eb, ee, st, end, far, *refs
):
    place = position()
    msgs = refs[: ring - 1]
    proj, r_gr, k_gk, at_end = refs[ring - 1 :]
    width = r.shape[1]
    late, z = place[0] == 1, place[1]
    zero = jnp.zeros((head, width), F32)
    nothing = jnp.zeros((1, width), F32)
    state, grad, past, future = zero, zero, nothing, nothing
    for d in range(1, ring):
        msg = msgs[d - 1]
        live = d <= z
        state = state + jnp.where(live, jnp.exp(past) * msg[:head].astype(F32), 0.0)
        past = past + jnp.where(live, joined(msg, head), 0.0)
    for d in range(ring - 1, 0, -1):
        msg = msgs[d - 1]
        live = d > z
        grad = grad + jnp.where(live, jnp.exp(future) * msg[:head].astype(F32), 0.0)
        future = future + jnp.where(live, joined(msg, head), 0.0)
    ef = jnp.exp(joined(far, 2 * head))
    st_in = jnp.where(late, far[:head].astype(F32) + ef * state, state)
    gt_in = jnp.where(late, grad, far[head : 2 * head].astype(F32) + ef * grad)
    at_end[...] = jnp.sum(gt_in * (jnp.exp(end[...]) * st_in + st[...]), 0, keepdims=True)
    sb, gb = st_in.astype(BF16), gt_in.astype(BF16)
    for p in range(width // PAIR):
        cols = slice(p * PAIR, (p + 1) * PAIR)
        grads = block_rows(gb[:, cols], head)
        rf, kf = r[:, cols].astype(F32), k[:, cols].astype(F32)
        after = ee[:, cols]
        gr = gr0[:, cols] + eb[:, cols] * mm(dy[:, cols], block_rows(sb[:, cols], head))
        gk = gk0[:, cols] + after * mm(v[:, cols], grads)
        gv = gv0[:, cols] + mm((kf * after).astype(BF16), grads, NT)
        s = own[:, cols] * u[:, cols]
        proj[0, :, cols] = (gr + kf * s).astype(BF16)
        proj[1, :, cols] = (gk + rf * s).astype(BF16)
        proj[2, :, cols] = gv.astype(BF16)
        r_gr[:, cols] = rf * gr
        k_gk[:, cols] = kf * gk


def decay_grad_kernel(w, r_gr, k_gk, at_end, up, lora_t, cums, up_grad, base_grad, mid_grad):
    ah, al = halves(r_gr[...])
    bh, bl = halves(k_gk[...])
    gp = (mm(cums[...], jnp.concatenate([ah, al, bh, bl], 0)) + at_end[...]) * w[...]
    gpb = gp.astype(BF16)
    up_grad[...] = mm(lora_t[...], gpb)
    base_grad[...] = jnp.sum(gp, 0, keepdims=True)
    mid_grad[...] = mm(gpb, up[...].astype(BF16), NT)


def middle_kernel(count, x, carried, mix, down, lora, *refs):
    mids, sides, (keep, send, grad_in) = refs[:count], refs[count:-3], refs[-3:]
    total = mids[0][...]
    for part in mids[1:]:
        total = total + part[...]
    mid = total * (1.0 - lora[...] * lora[...])
    grad_in[...] = mm3(mid, down[...], NT)
    down_grad = mm3(mid.T, mixed_input(x, carried, mix))
    rank, half = mid.shape[1], x.shape[1] // 2
    wide = (8, half)
    late = position()[0] == 1

    def choose(low, high, at, size):
        keep[at : at + size] = jnp.where(late, high, low).astype(BF16)
        send[at : at + size] = jnp.where(late, low, high).astype(BF16)

    up_low, up_high, base_low, base_high, du_low, du_high = [ref[...] for ref in sides]
    choose(up_low, up_high, 0, rank)
    choose(down_grad[:, :half], down_grad[:, half:], rank, rank)
    for at, low, high in ((0, base_low, base_high), (8, du_low, du_high)):
        choose(jnp.broadcast_to(low, wide), jnp.broadcast_to(high, wide), 2 * rank + at, 8)


def finish_kernel(rank, mine, theirs, up, down, base, du):
    late = position()[0] == 1
    half = mine.shape[1]
    a, b = mine[...].astype(F32), theirs[...].astype(F32)
    for at, value in ((0, jnp.where(late, b, a)), (half, jnp.where(late, a, b))):
        here = slice(at, at + half)
        up[:, here] = value[:rank]
        down[here] = value[rank : 2 * rank].T
        for ref, row in ((base, 2 * rank), (du, 2 * rank + 8)):
            size = ref.shape[1]
            for i in range(half // size):
                to = at // size + i
                ref[to : to + 1] = value[row : row + 1, i * size : (i + 1) * size]


def project_kernel(count, ring, final, *refs):
    place = position()
    lows, highs, given, mix = refs[:count], refs[count : 2 * count], refs[2 * count : 2 * count + 3], refs[2 * count + 3]
    rest, (low, high, weights, own, prior, sem) = refs[2 * count + 4 : -6], refs[-6:]
    done, outs = (rest[:-ring], rest[-ring:]) if final else ((), rest)
    rows, width = lows[0].shape[1:]
    n = weights.shape[2]
    copies = []

    def fetch(source, target):
        copy = pltpu.make_async_copy(source, target, sem.at[len(copies)])
        copy.start()
        copies.append(copy)
        return copy

    weight_copies, block_copies = [], []
    for i in range(2):
        for m in range(3):
            if i == 0:
                weight_copies.append([fetch(given[0].at[m], weights.at[0, m])])
            else:
                first, cut = given[1].at[m], given[1].shape[1]
                weight_copies.append(
                    [
                        fetch(first, weights.at[1, m, pl.ds(0, cut)]),
                        fetch(given[2].at[m], weights.at[1, m, pl.ds(cut, n - cut)]),
                    ]
                )
            if i == 0:
                places = [pl.ds(q * rows, rows) for q in range(count)]
                block_copies.append(
                    [fetch(lows[q].at[m], low.at[m, at]) for q, at in enumerate(places)]
                    + [fetch(highs[q].at[m], high.at[m, at]) for q, at in enumerate(places)]
                )

    for i in range(2):
        column = pl.ds(pl.multiple_of((place[0] if i == 0 else 1 - place[0]) * n, n), n)
        for m in range(3):
            for copy in (block_copies[m] if i == 0 else []) + weight_copies[i * 3 + m]:
                copy.wait()
            term = mm(low[m], weights[i, m, :, :width], NT) + mm(high[m], weights[i, m, :, width:], NT)
            later = mix[m : m + 1, column] * term
            own[...] = term - later if m == 0 else own[...] + (term - later)
            prior[...] = later if m == 0 else prior[...] + later
        last = lax.broadcasted_iota(jnp.int32, (rows, n), 0) == rows - 1
        top = lax.broadcasted_iota(jnp.int32, (16, n), 0) == 0

        def store(out, q):
            here = slice(q * rows, (q + 1) * rows)
            part = prior[here]
            moved = jnp.where(last, 0.0, pltpu.roll(part, rows - 1, 0))
            out[:rows, column] = (own[here] + moved).astype(BF16)
            out[rows:, column] = jnp.where(top, part[:16], 0.0).astype(BF16)

        if not final:
            for q in range(count):
                store(outs[q], q)
            continue
        for d in range(ring):
            wanted = lax.rem(place[1] - place[2] - d + 2 * ring, ring)
            for q in range(ring):

                @pl.when(wanted == q)
                def _():
                    if q == ring - 1:
                        store(outs[d], 0)
                    else:
                        outs[d][:, column] = done[q][:, column]


def per_device(
    layer_input, receptance, key_act, value_act, attention_result_sensitivity, time_first,
    decay_exponent_base, decay_shift_mix, mix_rkv, decay_adapter_down, decay_adapter_up, proj_weights,
):
    rows, cols = layer_input.shape
    heads, head = time_first.shape
    rank = decay_adapter_down.shape[1]
    n_seq, n_head = lax.axis_size("seq"), lax.axis_size("head")
    inner = n_seq // n_head
    ring = n_seq // inner
    pairs = cols // PAIR
    parts = 2
    part_cols = cols // parts
    block = min(part_cols, 2 * PAIR)
    r, k, v, dy = receptance, key_act, value_act, attention_result_sensitivity
    params = pltpu.CompilerParams(vmem_limit_bytes=VMEM)

    def shape(s, t=F32):
        return jax.ShapeDtypeStruct(s, t)

    def work(us):
        return pl.CostEstimate(flops=0, transcendentals=0, bytes_accessed=int(us * 3.5e6))

    def shift(a, distance):
        return lax.ppermute(
            a, "seq", [(i - distance, i) for i in range(n_seq) if 0 <= i - distance < n_seq]
        )

    def around(a, step):
        return lax.ppermute(a, "seq", [(i, (i + inner * step) % n_seq) for i in range(n_seq)])

    def partner(a):
        return lax.ppermute(a, "seq", [(i, i ^ 1) for i in range(n_seq)])

    def head_shift(a, d):
        return lax.ppermute(a, "head", [(i, (i + d) % n_head) for i in range(n_head)])

    def head_parts(a):
        return [a] + [head_shift(a, d) for d in range(1, n_head)]

    def after_that(value, *others):
        return lax.optimization_barrier((value, *others))[0]

    weight_rows = proj_weights.shape[1]
    cut = max(weight_rows * 3 // 256, 1) * 16
    anywhere = pl.BlockSpec(memory_space=pl.ANY)
    vmem = pl.BlockSpec(memory_space=pltpu.VMEM)

    carried, piece = lax.optimization_barrier((shift(layer_input[rows - 1 :], 1), proj_weights[:, :cut]))
    fars = [partner(piece)]
    shift_mix = decay_shift_mix.reshape(1, cols)
    pre = pl.pallas_call(
        adapter_kernel,
        out_shape=shape((rows, rank)),
        compiler_params=params,
        cost_estimate=work(1.5),
        name="adapter_input",
    )(layer_input, carried, shift_mix, decay_adapter_down)
    pres = head_parts(pre)

    sums = jnp.asarray(sum_matrix(rows), BF16)
    levels = jnp.asarray(level_matrix(rows), BF16)
    cums = jnp.asarray(cumulative_matrix(rows), BF16)
    far_rows = 2 * head + 8

    lora, lora_t, w, end, st, msg = pl.pallas_call(
        lambda *refs: decay_kernel(head, n_head, *refs),
        out_shape=[
            shape((rows, rank)), shape((rank, rows), BF16), shape((rows, cols)), shape((1, cols)),
            shape((head, cols)), shape((far_rows, cols), BF16),
        ],
        compiler_params=params,
        cost_estimate=work(3),
        name="decay_and_states",
    )(*pres, decay_exponent_base.reshape(1, cols), decay_adapter_up, r, k, v, dy, sums)

    vmem = pl.BlockSpec(memory_space=pltpu.VMEM)
    u = after_that(time_first, msg).reshape(1, cols)

    def col_block(n, width=block, offset=0):
        return pl.BlockSpec((n, width), lambda p, *_: (0, p + offset))

    def whole(s):
        return pl.BlockSpec(s, lambda p, *_: (0,) * len(s))

    steps = part_cols // block
    here = col_block(rows)

    def inside(part):
        at = lambda n: col_block(n, block, part * steps)
        extra = part == 0
        return pl.pallas_call(
            lambda *refs: inner_kernel(head, cut if extra else 0, *refs),
            grid=(steps,),
            in_specs=[at(rows)] * 5 + [at(1), whole(levels.shape), whole(sums.shape)] + [anywhere] * extra,
            out_specs=[here] * 6 + [col_block(1)] + [anywhere] * extra,
            out_shape=[shape((rows, part_cols))] * 6 + [shape((1, part_cols))]
            + [shape((3, weight_rows - cut, cols), BF16)] * extra,
            scratch_shapes=[
                pltpu.VMEM((3, weight_rows - cut, cols), BF16), pltpu.SemaphoreType.DMA((6,)),
            ] * extra,
            compiler_params=params,
            cost_estimate=work(4),
            name="inside_chunk",
        )(r, k, v, dy, after_that(w, fars[0]) if extra else w, u, levels, sums, *[proj_weights] * extra)

    inner_parts = [inside(part) for part in range(parts)]
    far, piece, inner_parts[0] = lax.optimization_barrier(
        (partner(msg), inner_parts[0][7], inner_parts[0][:7])
    )
    fars.append(partner(piece))
    out_msgs = pl.pallas_call(
        lambda *refs: pair_kernel(head, ring, *refs),
                out_shape=[shape((head + 8, cols), BF16)] * (ring - 1),
        compiler_params=params,
        cost_estimate=work(1.5),
        name="pair_states",
    )(msg, far)
    msgs = [around(m, d + 1) for d, m in enumerate(out_msgs)]

    inner_parts[1], msgs = lax.optimization_barrier((inner_parts[1], msgs))
    outer = []
    for part in range(parts):
        at = lambda n: col_block(n, block, part * steps)
        outer.append(
            pl.pallas_call(
                lambda *refs: outer_kernel(head, ring, *refs),
                grid=(steps,),
                in_specs=[at(rows)] * 4 + [at(1)] + [here] * 6
                + [at(head), at(1), at(far_rows)] + [at(head + 8)] * (ring - 1),
                out_specs=[pl.BlockSpec((3, rows, block), lambda p: (0, 0, p)), here, here, col_block(1)],
                out_shape=[
                    shape((3, rows, part_cols), BF16), shape((rows, part_cols)),
                    shape((rows, part_cols)), shape((1, part_cols)),
                ],
                compiler_params=params,
                cost_estimate=work(3),
                name="across_chunks",
            )(r, k, v, dy, u, *inner_parts[part][:6], st, end, far, *msgs)
        )
    projs = [o[0] for o in outer]

    ups, bases, mid_parts = [], [], []
    for part in range(parts):
        at = lambda n: pl.BlockSpec((n, part_cols), lambda p: (0, part))
        up_grad, base_grad, mid_grad = pl.pallas_call(
            decay_grad_kernel,
            grid=(1,),
            in_specs=[at(rows), *[whole((rows, part_cols))] * 2, whole((1, part_cols)), at(rank)]
            + [whole((rank, rows)), whole(cums.shape)],
            out_specs=[whole((rank, part_cols)), whole((1, part_cols)), whole((rows, rank))],
            out_shape=[shape((rank, part_cols)), shape((1, part_cols)), shape((rows, rank))],
            compiler_params=params,
            cost_estimate=work(2),
            name="decay_gradient",
        )(w, *outer[part][1:], decay_adapter_up, lora_t, cums)
        ups.append(up_grad)
        bases.append(base_grad)
        mid_parts.append(mid_grad)
    mid_grad = sum(mid_parts)

    mids = head_parts(mid_grad)
    dus = [part[6] for part in inner_parts]
    keep, send, grad_in = pl.pallas_call(
        lambda *refs: middle_kernel(n_head, *refs),
        in_specs=[vmem] * (5 + n_head + 3 * parts),
        out_shape=[shape((2 * rank + 16, part_cols), BF16)] * 2 + [shape((rows, cols))],
        compiler_params=params,
        cost_estimate=work(3),
        name="adapter_grads",
    )(
        layer_input, carried, shift_mix, decay_adapter_down, lora, *mids, *ups, *bases, *dus
    )

    lows, highs = [projs[0]], [projs[1]]
    for step in range(ring - 1):
        low, high = lows[-1], highs[-1]
        lows.append(around(after_that(low, mid_grad) if step == 1 else low, 1))
        highs.append(around(after_that(high, keep) if step == 1 else high, 1))

    def add(a, b):
        return (a.astype(F32) + b.astype(F32)).astype(BF16)

    got = partner(after_that(send, lows[2]))

    mix_here = lax.dynamic_slice_in_dim(after_that(mix_rkv, *out_msgs), position()[1] * cols, cols, 1)

    tall = rows + 16

    def project(low, high, done=()):
        count, final = len(low), len(done) > 0
        return pl.pallas_call(
            lambda *refs: project_kernel(count, ring, final, *refs),
            in_specs=[anywhere] * (2 * count + 3) + [vmem] * (1 + len(done)),
            out_shape=[shape((tall, cols), BF16)] * (ring if final else count),
            scratch_shapes=[
                pltpu.VMEM((3, count * rows, part_cols), BF16),
                pltpu.VMEM((3, count * rows, part_cols), BF16),
                pltpu.VMEM((inner, 3, weight_rows, cols), BF16),
                pltpu.VMEM((count * rows, weight_rows), F32),
                pltpu.VMEM((count * rows, weight_rows), F32),
                pltpu.SemaphoreType.DMA((3 * (2 * count + 3),)),
            ],
            compiler_params=pltpu.CompilerParams(vmem_limit_bytes=24 * 2**20),
            cost_estimate=work(5),
            name="projections",
        )(*low, *high, proj_weights, *fars, mix_here, *done)

    done = project(lows[:-1], highs[:-1])
    sends = project(lows[-1:], highs[-1:], done)
    token_sums = add(keep, after_that(got, *done))
    b = 1
    while b < ring:
        route = [(i, ((i // inner) ^ b) * inner + i % inner) for i in range(n_seq)]
        got = lax.ppermute(token_sums, "seq", route)
        token_sums = add(token_sums, after_that(got, sends) if b == 1 else got)
        b *= 2
    up_grad, down_grad, base_grad, du = pl.pallas_call(
        lambda *refs: finish_kernel(rank, *refs),
                out_shape=[shape((rank, cols)), shape((cols, rank)), shape((pairs, PAIR)), shape((heads, head))],
        compiler_params=pltpu.CompilerParams(vmem_limit_bytes=16 * 2**20),
        cost_estimate=work(2),
        name="token_sums",
    )(token_sums, partner(token_sums))

    total = sends[0].astype(F32)
    for d in range(1, n_head):
        total = total + head_shift(sends[d], d).astype(F32)
    swap, back = [], []
    for h in range(n_head):
        for z in range(ring):
            for x in range(inner):
                source = h * n_seq + z * inner + x
                block_at = h * inner + x
                swap.append((source, z * n_seq + block_at))
                if block_at > 0:
                    back.append((source, z * n_seq + block_at - 1))
    base_grad = base_grad.reshape(cols)
    summed = lax.ppermute(total[:rows].astype(BF16), ("head", "seq"), swap)
    edge = lax.ppermute(total[rows : rows + 1], ("head", "seq"), back)
    summed = after_that(summed, up_grad, base_grad, du)
    grad_next = jnp.concatenate([grad_in[1:], shift(grad_in[:1], -1)], 0)
    adapter_term = (1.0 - decay_shift_mix) * grad_in + decay_shift_mix * grad_next
    last = lax.broadcasted_iota(jnp.int32, (rows, 1), 0) == rows - 1
    result = (summed.astype(F32) + adapter_term + jnp.where(last, edge, 0.0)).astype(BF16)
    return (result, down_grad, up_grad, base_grad, du)


def solution(mesh):
    return jax.shard_map(
        per_device,
        mesh=mesh,
        in_specs=(
            P("seq", "head"), P("seq", "head"), P("seq", "head"), P("seq", "head"), P("seq", "head"),
            P("head", None), P("head"), P("head"), P(), P("head", None), P(None, "head"),
            P(None, "seq", "head"),
        ),
        out_specs=(P("seq", "head"), P("head", None), P(None, "head"), P("head"), P("head", None)),
        check_vma=False,
    )
```

```python
import jax
import jax.numpy as jnp
import numpy as np
from jax import lax
from jax.experimental import pallas as pl
from jax.experimental.pallas import tpu as pltpu
from jax.sharding import PartitionSpec as P

F32 = jnp.float32
BF16 = jnp.bfloat16
PAIR = 128
VMEM = 56 * 2**20
NN = (((1,), (0,)), ((), ()))
NT = (((1,), (1,)), ((), ()))
TN = (((0,), (0,)), ((), ()))


def position():
    seq, head = lax.axis_index("seq"), lax.axis_index("head")
    inner = lax.axis_size("seq") // lax.axis_size("head")
    return lax.rem(seq, inner), lax.div(seq, inner), head


def mm(a, b, dims=NN):
    return lax.dot_general(a, b, dims, preferred_element_type=F32)


def halves(a):
    hi = a.astype(BF16)
    return hi, (a - hi.astype(F32)).astype(BF16)


def low_lanes(shape, half):
    return lax.broadcasted_iota(jnp.int32, shape, len(shape) - 1) < half


def block_rows(a, half):
    low = low_lanes(a.shape, half)
    zero = jnp.zeros_like(a)
    return jnp.concatenate([jnp.where(low, a, zero), jnp.where(low, zero, a)], 0)


def fold(a, half):
    rows = a.shape[0] // 2
    return jnp.where(low_lanes((rows, a.shape[1]), half), a[:rows], a[rows:])


def sum_matrix(rows):
    t = np.arange(rows)
    both = np.concatenate([t[:, None] > t[None, :], t[:, None] < t[None, :]], 0)
    return np.concatenate([both, both], 1).astype(np.float32)


def level_matrix(rows):
    t = np.arange(rows)
    parts = []
    m = 1
    while m < rows:
        mid = (t // (2 * m)) * 2 * m + m
        right = t >= mid
        u = t[None, :]
        take_right = (u >= mid[:, None]) & (u < t[:, None])
        take_left = (u > t[:, None]) & (u < mid[:, None])
        parts.append(np.where(right[:, None], take_right, take_left))
        m *= 2
    both = np.concatenate(parts, 0)
    return np.concatenate([both, both], 1).astype(np.float32)


def cumulative_matrix(rows):
    t = np.arange(rows)
    strict = (t[:, None] < t[None, :]).astype(np.float32)
    full = (t[:, None] <= t[None, :]).astype(np.float32)
    return np.concatenate([strict, strict, -full, -full], 1)


def split_rows(a):
    hi, lo = halves(a)
    wide = (4, a.shape[1])
    return jnp.concatenate([jnp.broadcast_to(hi, wide), jnp.broadcast_to(lo, wide)], 0)


def joined(msg, at):
    return msg[at : at + 1].astype(F32) + msg[at + 4 : at + 5].astype(F32)


def mm3(a, b, dims=NN):
    ah, al = halves(a)
    bh, bl = halves(b)
    return mm(ah, bh, dims) + (mm(ah, bl, dims) + mm(al, bh, dims))


def mixed_input(x, carried, mix):
    features = x[...].astype(F32)
    row = lax.broadcasted_iota(jnp.int32, features.shape, 0)
    previous = jnp.where(row == 0, carried[...].astype(F32), pltpu.roll(features, 1, 0))
    return features + mix[...] * (previous - features)


def copy_rows(weights, piece, at, stage, sem):
    rows = pl.ds(at, piece.shape[1])
    into = [pltpu.make_async_copy(weights.at[m, rows], stage.at[m], sem.at[m]) for m in range(3)]
    out = [pltpu.make_async_copy(stage.at[m], piece.at[m], sem.at[3 + m]) for m in range(3)]
    return into, out


def adapter_kernel(x, carried, mix, down, pre):
    pre[...] = mm3(mixed_input(x, carried, mix), down[...])


def decay_kernel(head, count, *refs):
    pres = refs[:count]
    base, up, r, k, v, dy, sums, lora, lora_t, w_out, end, st, msg = refs[count:]
    rows = r.shape[0]
    total = pres[0][...]
    for pre in pres[1:]:
        total = total + pre[...]
    mid = jnp.tanh(total)
    lora[...] = mid
    lora_t[...] = mid.T.astype(BF16)
    w = -jnp.exp(base[...] + mm3(mid, up[...]))
    w_out[...] = w
    hi, lo = halves(w)
    args = mm(sums[...], jnp.concatenate([hi, lo], 0))
    before, after = args[:rows], args[rows:]
    final = before[rows - 1 :] + w[rows - 1 :]
    end[...] = final
    from_start, to_end = jnp.exp(before), jnp.exp(after)
    kf = (k[...].astype(F32) * to_end).astype(BF16)
    rb = (r[...].astype(F32) * from_start).astype(BF16)
    for p in range(r.shape[1] // PAIR):
        cols = slice(p * PAIR, (p + 1) * PAIR)
        state = fold(mm(v[:, cols], kf[:, cols], TN), head)
        st[:, cols] = state
        msg[:head, cols] = state.astype(BF16)
        msg[head : 2 * head, cols] = fold(mm(dy[:, cols], rb[:, cols], TN), head).astype(BF16)
    msg[2 * head :] = split_rows(final)


def pair_kernel(head, ring, own, far, *outs):
    place = position()
    late = place[0] == 1
    dec_own, dec_far = joined(own, 2 * head), joined(far, 2 * head)
    eo, ef = jnp.exp(dec_own), jnp.exp(dec_far)
    st_own, st_far = own[:head].astype(F32), far[:head].astype(F32)
    gt_own, gt_far = own[head : 2 * head].astype(F32), far[head : 2 * head].astype(F32)
    state = jnp.where(late, st_own + eo * st_far, st_far + ef * st_own).astype(BF16)
    grad = jnp.where(late, gt_far + ef * gt_own, gt_own + eo * gt_far).astype(BF16)
    decays = split_rows(dec_own + dec_far)
    for d in range(1, ring):
        out = outs[d - 1]
        ahead = place[1] + d < ring

        @pl.when(ahead)
        def _():
            out[:head] = state

        @pl.when(jnp.logical_not(ahead))
        def _():
            out[:head] = grad

        out[head:] = decays


def inner_kernel(head, skip, r, k, v, dy, w, u, levels, sums, *refs):
    if skip:
        weights, piece, stage, sem = refs[0], refs[8], refs[9], refs[10]
        refs = refs[1:8]
        into, out = copy_rows(weights, piece, skip, stage, sem)
        at_last = pl.program_id(0) == pl.num_programs(0) - 1

        @pl.when(pl.program_id(0) == 0)
        def _():
            for copy in into:
                copy.start()

        @pl.when(at_last)
        def _():
            for first, second in zip(into, out):
                first.wait()
                second.start()

    gr_out, gk_out, gv_out, self_out, eb_out, ee_out, du_out = refs
    rows, width = r.shape
    row = lax.broadcasted_iota(jnp.int32, (rows, PAIR), 0)
    row2 = lax.broadcasted_iota(jnp.int32, (rows, 2 * rows), 0)
    col2 = lax.broadcasted_iota(jnp.int32, (rows, 2 * rows), 1)
    apart = row2 ^ (col2 & (rows - 1))
    lane_r = lax.broadcasted_iota(jnp.int32, (2 * PAIR, PAIR), 0) & (PAIR - 1)
    lane_c = lax.broadcasted_iota(jnp.int32, (2 * PAIR, PAIR), 1)
    ones = jnp.where((lane_r < head) == (lane_c < head), 1.0, 0.0).astype(BF16)
    hi, lo = halves(w[...])
    both = jnp.concatenate([hi, lo], 0)
    decay = jnp.exp(mm(levels[...], both))
    ends = jnp.exp(mm(sums[...], both))
    eb_out[...], ee_out[...] = ends[:rows], ends[rows:]
    for p in range(width // PAIR):
        cols = slice(p * PAIR, (p + 1) * PAIR)
        rf, kf = r[:, cols].astype(F32), k[:, cols].astype(F32)
        vf, dyf = v[:, cols].astype(F32), dy[:, cols].astype(F32)
        dydy = block_rows(dy[:, cols], head)
        pairs = mm(dy[:, cols], block_rows(v[:, cols], head), NT)
        pairs_t = mm(v[:, cols], dydy, NT)
        gr = jnp.zeros((rows, PAIR), F32)
        gk = jnp.zeros((rows, PAIR), F32)
        scores_t = jnp.zeros((rows, 2 * rows), F32)
        m, level = 1, 0
        while m < rows:
            d = decay[level * rows : (level + 1) * rows, cols]
            right = (row & m) != 0
            rd = jnp.where(right, rf * d, 0.0).astype(BF16)
            kd = jnp.where(right, 0.0, kf * d).astype(BF16)
            kk, rr = block_rows(kd, head), block_rows(rd, head)
            near = apart < 2 * m
            a = mm(kd, rr, NT)
            scores_t = scores_t + jnp.where(near, a, 0.0)
            here = jnp.where(near, pairs, 0.0).astype(BF16)
            here_t = jnp.where(near, pairs_t, 0.0).astype(BF16)
            gr = gr + jnp.where(right, d * mm(here, kk), 0.0)
            gk = gk + jnp.where(right, 0.0, d * mm(here_t, rr))
            m, level = 2 * m, level + 1
        sh, sl = halves(dyf * vf)
        own = mm(jnp.concatenate([sh, sl], 1), ones)
        bh, bl = halves(rf * u[:, cols] * kf)
        bonus = mm(jnp.concatenate([bh, bl], 1), ones)
        gr_out[:, cols] = gr
        gk_out[:, cols] = gk
        gv_out[:, cols] = mm(scores_t.astype(BF16), dydy) + bonus * dyf
        self_out[:, cols] = own
        du_out[:, cols] = jnp.sum(rf * kf * own, 0, keepdims=True)
    if skip:

        @pl.when(at_last)
        def _():
            for copy in out:
                copy.wait()


def outer_kernel(
    head, ring, r, k, v, dy, u, gr0, gk0, gv0, own, eb, ee, st, end, far, *refs
):
    place = position()
    msgs = refs[: ring - 1]
    proj, r_gr, k_gk, at_end = refs[ring - 1 :]
    width = r.shape[1]
    late, z = place[0] == 1, place[1]
    zero = jnp.zeros((head, width), F32)
    nothing = jnp.zeros((1, width), F32)
    state, grad, past, future = zero, zero, nothing, nothing
    for d in range(1, ring):
        msg = msgs[d - 1]
        live = d <= z
        state = state + jnp.where(live, jnp.exp(past) * msg[:head].astype(F32), 0.0)
        past = past + jnp.where(live, joined(msg, head), 0.0)
    for d in range(ring - 1, 0, -1):
        msg = msgs[d - 1]
        live = d > z
        grad = grad + jnp.where(live, jnp.exp(future) * msg[:head].astype(F32), 0.0)
        future = future + jnp.where(live, joined(msg, head), 0.0)
    ef = jnp.exp(joined(far, 2 * head))
    st_in = jnp.where(late, far[:head].astype(F32) + ef * state, state)
    gt_in = jnp.where(late, grad, far[head : 2 * head].astype(F32) + ef * grad)
    at_end[...] = jnp.sum(gt_in * (jnp.exp(end[...]) * st_in + st[...]), 0, keepdims=True)
    sb, gb = st_in.astype(BF16), gt_in.astype(BF16)
    for p in range(width // PAIR):
        cols = slice(p * PAIR, (p + 1) * PAIR)
        grads = block_rows(gb[:, cols], head)
        rf, kf = r[:, cols].astype(F32), k[:, cols].astype(F32)
        after = ee[:, cols]
        gr = gr0[:, cols] + eb[:, cols] * mm(dy[:, cols], block_rows(sb[:, cols], head))
        gk = gk0[:, cols] + after * mm(v[:, cols], grads)
        gv = gv0[:, cols] + mm((kf * after).astype(BF16), grads, NT)
        s = own[:, cols] * u[:, cols]
        proj[0, :, cols] = (gr + kf * s).astype(BF16)
        proj[1, :, cols] = (gk + rf * s).astype(BF16)
        proj[2, :, cols] = gv.astype(BF16)
        r_gr[:, cols] = rf * gr
        k_gk[:, cols] = kf * gk


def decay_grad_kernel(w, r_gr, k_gk, at_end, up, lora_t, cums, up_grad, base_grad, mid_grad):
    ah, al = halves(r_gr[...])
    bh, bl = halves(k_gk[...])
    gp = (mm(cums[...], jnp.concatenate([ah, al, bh, bl], 0)) + at_end[...]) * w[...]
    gpb = gp.astype(BF16)
    up_grad[...] = mm(lora_t[...], gpb)
    base_grad[...] = jnp.sum(gp, 0, keepdims=True)
    mid_grad[...] = mm(gpb, up[...].astype(BF16), NT)


def middle_kernel(count, x, carried, mix, down, lora, *refs):
    mids, sides, (keep, send, grad_in) = refs[:count], refs[count:-3], refs[-3:]
    total = mids[0][...]
    for part in mids[1:]:
        total = total + part[...]
    mid = total * (1.0 - lora[...] * lora[...])
    grad_in[...] = mm3(mid, down[...], NT)
    down_grad = mm3(mid.T, mixed_input(x, carried, mix))
    rank, half = mid.shape[1], x.shape[1] // 2
    wide = (8, half)
    late = position()[0] == 1

    def choose(low, high, at, size):
        keep[at : at + size] = jnp.where(late, high, low).astype(BF16)
        send[at : at + size] = jnp.where(late, low, high).astype(BF16)

    up_low, up_high, base_low, base_high, du_low, du_high = [ref[...] for ref in sides]
    choose(up_low, up_high, 0, rank)
    choose(down_grad[:, :half], down_grad[:, half:], rank, rank)
    for at, low, high in ((0, base_low, base_high), (8, du_low, du_high)):
        choose(jnp.broadcast_to(low, wide), jnp.broadcast_to(high, wide), 2 * rank + at, 8)


def finish_kernel(rank, mine, theirs, up, down, base, du):
    late = position()[0] == 1
    half = mine.shape[1]
    a, b = mine[...].astype(F32), theirs[...].astype(F32)
    for at, value in ((0, jnp.where(late, b, a)), (half, jnp.where(late, a, b))):
        here = slice(at, at + half)
        up[:, here] = value[:rank]
        down[here] = value[rank : 2 * rank].T
        for ref, row in ((base, 2 * rank), (du, 2 * rank + 8)):
            size = ref.shape[1]
            for i in range(half // size):
                to = at // size + i
                ref[to : to + 1] = value[row : row + 1, i * size : (i + 1) * size]


def project_kernel(count, ring, final, *refs):
    place = position()
    lows, highs, given, mix = refs[:count], refs[count : 2 * count], refs[2 * count : 2 * count + 3], refs[2 * count + 3]
    rest, (low, high, weights, own, prior, sem) = refs[2 * count + 4 : -6], refs[-6:]
    done, outs = (rest[:-ring], rest[-ring:]) if final else ((), rest)
    rows, width = lows[0].shape[1:]
    n = weights.shape[2]
    copies = []

    def fetch(source, target):
        copy = pltpu.make_async_copy(source, target, sem.at[len(copies)])
        copy.start()
        copies.append(copy)
        return copy

    weight_copies, block_copies = [], []
    for i in range(2):
        for m in range(3):
            if i == 0:
                weight_copies.append([fetch(given[0].at[m], weights.at[0, m])])
            else:
                first, cut = given[1].at[m], given[1].shape[1]
                weight_copies.append(
                    [
                        fetch(first, weights.at[1, m, pl.ds(0, cut)]),
                        fetch(given[2].at[m], weights.at[1, m, pl.ds(cut, n - cut)]),
                    ]
                )
            if i == 0:
                places = [pl.ds(q * rows, rows) for q in range(count)]
                block_copies.append(
                    [fetch(lows[q].at[m], low.at[m, at]) for q, at in enumerate(places)]
                    + [fetch(highs[q].at[m], high.at[m, at]) for q, at in enumerate(places)]
                )

    for i in range(2):
        column = pl.ds(pl.multiple_of((place[0] if i == 0 else 1 - place[0]) * n, n), n)
        for m in range(3):
            for copy in (block_copies[m] if i == 0 else []) + weight_copies[i * 3 + m]:
                copy.wait()
            term = mm(low[m], weights[i, m, :, :width], NT) + mm(high[m], weights[i, m, :, width:], NT)
            later = mix[m : m + 1, column] * term
            own[...] = term - later if m == 0 else own[...] + (term - later)
            prior[...] = later if m == 0 else prior[...] + later
        last = lax.broadcasted_iota(jnp.int32, (rows, n), 0) == rows - 1
        top = lax.broadcasted_iota(jnp.int32, (16, n), 0) == 0

        def store(out, q):
            here = slice(q * rows, (q + 1) * rows)
            part = prior[here]
            moved = jnp.where(last, 0.0, pltpu.roll(part, rows - 1, 0))
            out[:rows, column] = (own[here] + moved).astype(BF16)
            out[rows:, column] = jnp.where(top, part[:16], 0.0).astype(BF16)

        if not final:
            for q in range(count):
                store(outs[q], q)
            continue
        for d in range(ring):
            wanted = lax.rem(place[1] - lax.bitwise_xor(place[2], d) + ring, ring)
            for q in range(ring):

                @pl.when(wanted == q)
                def _():
                    if q == ring - 1:
                        store(outs[d], 0)
                    else:
                        outs[d][:, column] = done[q][:, column]


def per_device(
    layer_input, receptance, key_act, value_act, attention_result_sensitivity, time_first,
    decay_exponent_base, decay_shift_mix, mix_rkv, decay_adapter_down, decay_adapter_up, proj_weights,
):
    rows, cols = layer_input.shape
    heads, head = time_first.shape
    rank = decay_adapter_down.shape[1]
    n_seq, n_head = lax.axis_size("seq"), lax.axis_size("head")
    inner = n_seq // n_head
    ring = n_seq // inner
    pairs = cols // PAIR
    parts = 2
    part_cols = cols // parts
    block = min(part_cols, 2 * PAIR)
    r, k, v, dy = receptance, key_act, value_act, attention_result_sensitivity
    params = pltpu.CompilerParams(vmem_limit_bytes=VMEM)

    def shape(s, t=F32):
        return jax.ShapeDtypeStruct(s, t)

    def work(us):
        return pl.CostEstimate(flops=0, transcendentals=0, bytes_accessed=int(us * 3.5e6))

    def shift(a, distance):
        return lax.ppermute(
            a, "seq", [(i - distance, i) for i in range(n_seq) if 0 <= i - distance < n_seq]
        )

    def around(a, step):
        return lax.ppermute(a, "seq", [(i, (i + inner * step) % n_seq) for i in range(n_seq)])

    def partner(a):
        return lax.ppermute(a, "seq", [(i, i ^ 1) for i in range(n_seq)])

    def head_shift(a, d):
        return lax.ppermute(a, "head", [(i, (i + d) % n_head) for i in range(n_head)])

    def head_parts(a):
        return [a] + [head_shift(a, d) for d in range(1, n_head)]

    def after_that(value, *others):
        return lax.optimization_barrier((value, *others))[0]

    weight_rows = proj_weights.shape[1]
    cut = max(weight_rows * 3 // 256, 1) * 16
    anywhere = pl.BlockSpec(memory_space=pl.ANY)
    vmem = pl.BlockSpec(memory_space=pltpu.VMEM)

    carried, piece = lax.optimization_barrier((shift(layer_input[rows - 1 :], 1), proj_weights[:, :cut]))
    fars = [partner(piece)]
    shift_mix = decay_shift_mix.reshape(1, cols)
    pre = pl.pallas_call(
        adapter_kernel,
        out_shape=shape((rows, rank)),
        compiler_params=params,
        cost_estimate=work(1.5),
        name="adapter_input",
    )(layer_input, carried, shift_mix, decay_adapter_down)
    pres = head_parts(pre)

    sums = jnp.asarray(sum_matrix(rows), BF16)
    levels = jnp.asarray(level_matrix(rows), BF16)
    cums = jnp.asarray(cumulative_matrix(rows), BF16)
    far_rows = 2 * head + 8

    lora, lora_t, w, end, st, msg = pl.pallas_call(
        lambda *refs: decay_kernel(head, n_head, *refs),
        out_shape=[
            shape((rows, rank)), shape((rank, rows), BF16), shape((rows, cols)), shape((1, cols)),
            shape((head, cols)), shape((far_rows, cols), BF16),
        ],
        compiler_params=params,
        cost_estimate=work(3),
        name="decay_and_states",
    )(*pres, decay_exponent_base.reshape(1, cols), decay_adapter_up, r, k, v, dy, sums)

    vmem = pl.BlockSpec(memory_space=pltpu.VMEM)
    u = after_that(time_first, msg).reshape(1, cols)

    def col_block(n, width=block, offset=0):
        return pl.BlockSpec((n, width), lambda p, *_: (0, p + offset))

    def whole(s):
        return pl.BlockSpec(s, lambda p, *_: (0,) * len(s))

    steps = part_cols // block
    here = col_block(rows)

    def inside(part):
        at = lambda n: col_block(n, block, part * steps)
        extra = part == 0
        return pl.pallas_call(
            lambda *refs: inner_kernel(head, cut if extra else 0, *refs),
            grid=(steps,),
            in_specs=[at(rows)] * 5 + [at(1), whole(levels.shape), whole(sums.shape)] + [anywhere] * extra,
            out_specs=[here] * 6 + [col_block(1)] + [anywhere] * extra,
            out_shape=[shape((rows, part_cols))] * 6 + [shape((1, part_cols))]
            + [shape((3, weight_rows - cut, cols), BF16)] * extra,
            scratch_shapes=[
                pltpu.VMEM((3, weight_rows - cut, cols), BF16), pltpu.SemaphoreType.DMA((6,)),
            ] * extra,
            compiler_params=params,
            cost_estimate=work(4),
            name="inside_chunk",
        )(r, k, v, dy, after_that(w, fars[0]) if extra else w, u, levels, sums, *[proj_weights] * extra)

    inner_parts = [inside(part) for part in range(parts)]
    far, piece, inner_parts[0] = lax.optimization_barrier(
        (partner(msg), inner_parts[0][7], inner_parts[0][:7])
    )
    fars.append(partner(piece))
    out_msgs = pl.pallas_call(
        lambda *refs: pair_kernel(head, ring, *refs),
                out_shape=[shape((head + 8, cols), BF16)] * (ring - 1),
        compiler_params=params,
        cost_estimate=work(1.5),
        name="pair_states",
    )(msg, far)
    msgs = [around(m, d + 1) for d, m in enumerate(out_msgs)]

    inner_parts[1], msgs = lax.optimization_barrier((inner_parts[1], msgs))
    outer = []
    for part in range(parts):
        at = lambda n: col_block(n, block, part * steps)
        outer.append(
            pl.pallas_call(
                lambda *refs: outer_kernel(head, ring, *refs),
                grid=(steps,),
                in_specs=[at(rows)] * 4 + [at(1)] + [here] * 6
                + [at(head), at(1), at(far_rows)] + [at(head + 8)] * (ring - 1),
                out_specs=[pl.BlockSpec((3, rows, block), lambda p: (0, 0, p)), here, here, col_block(1)],
                out_shape=[
                    shape((3, rows, part_cols), BF16), shape((rows, part_cols)),
                    shape((rows, part_cols)), shape((1, part_cols)),
                ],
                compiler_params=params,
                cost_estimate=work(3),
                name="across_chunks",
            )(r, k, v, dy, u, *inner_parts[part][:6], st, end, far, *msgs)
        )
    projs = [o[0] for o in outer]

    ups, bases, mid_parts = [], [], []
    for part in range(parts):
        at = lambda n: pl.BlockSpec((n, part_cols), lambda p: (0, part))
        up_grad, base_grad, mid_grad = pl.pallas_call(
            decay_grad_kernel,
            grid=(1,),
            in_specs=[at(rows), *[whole((rows, part_cols))] * 2, whole((1, part_cols)), at(rank)]
            + [whole((rank, rows)), whole(cums.shape)],
            out_specs=[whole((rank, part_cols)), whole((1, part_cols)), whole((rows, rank))],
            out_shape=[shape((rank, part_cols)), shape((1, part_cols)), shape((rows, rank))],
            compiler_params=params,
            cost_estimate=work(2),
            name="decay_gradient",
        )(w, *outer[part][1:], decay_adapter_up, lora_t, cums)
        ups.append(up_grad)
        bases.append(base_grad)
        mid_parts.append(mid_grad)
    mid_grad = sum(mid_parts)

    mids = head_parts(mid_grad)
    dus = [part[6] for part in inner_parts]
    keep, send, grad_in = pl.pallas_call(
        lambda *refs: middle_kernel(n_head, *refs),
        in_specs=[vmem] * (5 + n_head + 3 * parts),
        out_shape=[shape((2 * rank + 16, part_cols), BF16)] * 2 + [shape((rows, cols))],
        compiler_params=params,
        cost_estimate=work(3),
        name="adapter_grads",
    )(
        layer_input, carried, shift_mix, decay_adapter_down, lora, *mids, *ups, *bases, *dus
    )

    lows, highs = [projs[0]], [projs[1]]
    for step in range(ring - 1):
        low, high = lows[-1], highs[-1]
        lows.append(around(after_that(low, mid_grad) if step == 1 else low, 1))
        highs.append(around(after_that(high, keep) if step == 1 else high, 1))

    def add(a, b):
        return (a.astype(F32) + b.astype(F32)).astype(BF16)

    got = partner(after_that(send, lows[2]))

    mix_here = lax.dynamic_slice_in_dim(after_that(mix_rkv, *out_msgs), position()[1] * cols, cols, 1)

    tall = rows + 16

    def project(low, high, done=()):
        count, final = len(low), len(done) > 0
        return pl.pallas_call(
            lambda *refs: project_kernel(count, ring, final, *refs),
            in_specs=[anywhere] * (2 * count + 3) + [vmem] * (1 + len(done)),
            out_shape=[shape((tall, cols), BF16)] * (ring if final else count),
            scratch_shapes=[
                pltpu.VMEM((3, count * rows, part_cols), BF16),
                pltpu.VMEM((3, count * rows, part_cols), BF16),
                pltpu.VMEM((inner, 3, weight_rows, cols), BF16),
                pltpu.VMEM((count * rows, weight_rows), F32),
                pltpu.VMEM((count * rows, weight_rows), F32),
                pltpu.SemaphoreType.DMA((3 * (2 * count + 3),)),
            ],
            compiler_params=pltpu.CompilerParams(vmem_limit_bytes=24 * 2**20),
            cost_estimate=work(5),
            name="projections",
        )(*low, *high, proj_weights, *fars, mix_here, *done)

    done = project(lows[:-1], highs[:-1])
    sends = project(lows[-1:], highs[-1:], done)
    token_sums = add(keep, after_that(got, *done))
    b = 1
    while b < ring:
        route = [(i, ((i // inner) ^ b) * inner + i % inner) for i in range(n_seq)]
        got = lax.ppermute(token_sums, "seq", route)
        token_sums = add(token_sums, after_that(got, sends) if b == 1 else got)
        b *= 2
    up_grad, down_grad, base_grad, du = pl.pallas_call(
        lambda *refs: finish_kernel(rank, *refs),
                out_shape=[shape((rank, cols)), shape((cols, rank)), shape((pairs, PAIR)), shape((heads, head))],
        compiler_params=pltpu.CompilerParams(vmem_limit_bytes=16 * 2**20),
        cost_estimate=work(2),
        name="token_sums",
    )(token_sums, partner(token_sums))

    def across(a, bit):
        return lax.ppermute(a, "head", [(i, i ^ bit) for i in range(n_head)])

    left, bit = dict(enumerate(sends)), 1
    while bit < n_head:
        got = {e: across(left[e | bit], bit) for e in left if not e & bit}
        left = {e: left[e].astype(F32) + got[e].astype(F32) for e in got}
        bit *= 2
        if bit < n_head:
            left = {e: value.astype(BF16) for e, value in left.items()}
    total = left[0]
    swap, back = [], []
    for h in range(n_head):
        for z in range(ring):
            for x in range(inner):
                source = h * n_seq + z * inner + x
                block_at = h * inner + x
                swap.append((source, z * n_seq + block_at))
                if block_at > 0:
                    back.append((source, z * n_seq + block_at - 1))
    base_grad = base_grad.reshape(cols)
    summed = lax.ppermute(total[:rows].astype(BF16), ("head", "seq"), swap)
    edge = lax.ppermute(total[rows : rows + 1], ("head", "seq"), back)
    summed = after_that(summed, up_grad, base_grad, du)
    grad_next = jnp.concatenate([grad_in[1:], shift(grad_in[:1], -1)], 0)
    adapter_term = (1.0 - decay_shift_mix) * grad_in + decay_shift_mix * grad_next
    last = lax.broadcasted_iota(jnp.int32, (rows, 1), 0) == rows - 1
    result = (summed.astype(F32) + adapter_term + jnp.where(last, edge, 0.0)).astype(BF16)
    return (result, down_grad, up_grad, base_grad, du)


def solution(mesh):
    return jax.shard_map(
        per_device,
        mesh=mesh,
        in_specs=(
            P("seq", "head"), P("seq", "head"), P("seq", "head"), P("seq", "head"), P("seq", "head"),
            P("head", None), P("head"), P("head"), P(), P("head", None), P(None, "head"),
            P(None, "seq", "head"),
        ),
        out_specs=(P("seq", "head"), P("head", None), P(None, "head"), P("head"), P("head", None)),
        check_vma=False,
    )
```

```python
import jax
import jax.numpy as jnp
import numpy as np
from jax import lax
from jax.experimental import pallas as pl
from jax.experimental.pallas import tpu as pltpu
from jax.sharding import PartitionSpec as P

F32 = jnp.float32
BF16 = jnp.bfloat16
PAIR = 128
VMEM = 56 * 2**20
NN = (((1,), (0,)), ((), ()))
NT = (((1,), (1,)), ((), ()))
TN = (((0,), (0,)), ((), ()))


def position():
    seq, head = lax.axis_index("seq"), lax.axis_index("head")
    inner = lax.axis_size("seq") // lax.axis_size("head")
    return lax.rem(seq, inner), lax.div(seq, inner), head


def mm(a, b, dims=NN):
    return lax.dot_general(a, b, dims, preferred_element_type=F32)


def halves(a):
    hi = a.astype(BF16)
    return hi, (a - hi.astype(F32)).astype(BF16)


def low_lanes(shape, half):
    return lax.broadcasted_iota(jnp.int32, shape, len(shape) - 1) < half


def block_rows(a, half):
    low = low_lanes(a.shape, half)
    zero = jnp.zeros_like(a)
    return jnp.concatenate([jnp.where(low, a, zero), jnp.where(low, zero, a)], 0)


def fold(a, half):
    rows = a.shape[0] // 2
    return jnp.where(low_lanes((rows, a.shape[1]), half), a[:rows], a[rows:])


def sum_matrix(rows):
    t = np.arange(rows)
    both = np.concatenate([t[:, None] > t[None, :], t[:, None] < t[None, :]], 0)
    return np.concatenate([both, both], 1).astype(np.float32)


def level_matrix(rows):
    t = np.arange(rows)
    parts = []
    m = 1
    while m < rows:
        mid = (t // (2 * m)) * 2 * m + m
        right = t >= mid
        u = t[None, :]
        take_right = (u >= mid[:, None]) & (u < t[:, None])
        take_left = (u > t[:, None]) & (u < mid[:, None])
        parts.append(np.where(right[:, None], take_right, take_left))
        m *= 2
    both = np.concatenate(parts, 0)
    return np.concatenate([both, both], 1).astype(np.float32)


def cumulative_matrix(rows):
    t = np.arange(rows)
    strict = (t[:, None] < t[None, :]).astype(np.float32)
    full = (t[:, None] <= t[None, :]).astype(np.float32)
    return np.concatenate([strict, strict, -full, -full], 1)


def split_rows(a):
    hi, lo = halves(a)
    wide = (4, a.shape[1])
    return jnp.concatenate([jnp.broadcast_to(hi, wide), jnp.broadcast_to(lo, wide)], 0)


def joined(msg, at):
    return msg[at : at + 1].astype(F32) + msg[at + 4 : at + 5].astype(F32)


def mm3(a, b, dims=NN):
    ah, al = halves(a)
    bh, bl = halves(b)
    return mm(ah, bh, dims) + (mm(ah, bl, dims) + mm(al, bh, dims))


def mixed_input(x, carried, mix):
    features = x[...].astype(F32)
    row = lax.broadcasted_iota(jnp.int32, features.shape, 0)
    previous = jnp.where(row == 0, carried[...].astype(F32), pltpu.roll(features, 1, 0))
    return features + mix[...] * (previous - features)


def copy_rows(weights, piece, at, stage, sem):
    rows = pl.ds(at, piece.shape[1])
    into = [pltpu.make_async_copy(weights.at[m, rows], stage.at[m], sem.at[m]) for m in range(3)]
    out = [pltpu.make_async_copy(stage.at[m], piece.at[m], sem.at[3 + m]) for m in range(3)]
    return into, out


def adapter_kernel(x, carried, mix, down, pre):
    pre[...] = mm3(mixed_input(x, carried, mix), down[...])


def decay_kernel(head, count, *refs):
    pres = refs[:count]
    base, up, r, k, v, dy, sums, lora, lora_t, w_out, end, st, msg = refs[count:]
    rows = r.shape[0]
    total = pres[0][...]
    for pre in pres[1:]:
        total = total + pre[...]
    mid = jnp.tanh(total)
    lora[...] = mid
    lora_t[...] = mid.T.astype(BF16)
    w = -jnp.exp(base[...] + mm3(mid, up[...]))
    w_out[...] = w
    hi, lo = halves(w)
    args = mm(sums[...], jnp.concatenate([hi, lo], 0))
    before, after = args[:rows], args[rows:]
    final = before[rows - 1 :] + w[rows - 1 :]
    end[...] = final
    from_start, to_end = jnp.exp(before), jnp.exp(after)
    kf = (k[...].astype(F32) * to_end).astype(BF16)
    rb = (r[...].astype(F32) * from_start).astype(BF16)
    for p in range(r.shape[1] // PAIR):
        cols = slice(p * PAIR, (p + 1) * PAIR)
        state = fold(mm(v[:, cols], kf[:, cols], TN), head)
        st[:, cols] = state
        msg[:head, cols] = state.astype(BF16)
        msg[head : 2 * head, cols] = fold(mm(dy[:, cols], rb[:, cols], TN), head).astype(BF16)
    msg[2 * head :] = split_rows(final)


def pair_kernel(head, ring, own, far, *outs):
    place = position()
    late = place[0] == 1
    dec_own, dec_far = joined(own, 2 * head), joined(far, 2 * head)
    eo, ef = jnp.exp(dec_own), jnp.exp(dec_far)
    st_own, st_far = own[:head].astype(F32), far[:head].astype(F32)
    gt_own, gt_far = own[head : 2 * head].astype(F32), far[head : 2 * head].astype(F32)
    state = jnp.where(late, st_own + eo * st_far, st_far + ef * st_own).astype(BF16)
    grad = jnp.where(late, gt_far + ef * gt_own, gt_own + eo * gt_far).astype(BF16)
    decays = split_rows(dec_own + dec_far)
    for d in range(1, ring):
        out = outs[d - 1]
        ahead = place[1] + d < ring

        @pl.when(ahead)
        def _():
            out[:head] = state

        @pl.when(jnp.logical_not(ahead))
        def _():
            out[:head] = grad

        out[head:] = decays


def inner_kernel(head, skip, r, k, v, dy, w, u, levels, sums, *refs):
    if skip:
        weights, piece, stage, sem = refs[0], refs[8], refs[9], refs[10]
        refs = refs[1:8]
        into, out = copy_rows(weights, piece, skip, stage, sem)
        at_last = pl.program_id(0) == pl.num_programs(0) - 1

        @pl.when(pl.program_id(0) == 0)
        def _():
            for copy in into:
                copy.start()

        @pl.when(at_last)
        def _():
            for first, second in zip(into, out):
                first.wait()
                second.start()

    gr_out, gk_out, gv_out, self_out, eb_out, ee_out, du_out = refs
    rows, width = r.shape
    row = lax.broadcasted_iota(jnp.int32, (rows, PAIR), 0)
    row2 = lax.broadcasted_iota(jnp.int32, (rows, 2 * rows), 0)
    col2 = lax.broadcasted_iota(jnp.int32, (rows, 2 * rows), 1)
    apart = row2 ^ (col2 & (rows - 1))
    lane_r = lax.broadcasted_iota(jnp.int32, (2 * PAIR, PAIR), 0) & (PAIR - 1)
    lane_c = lax.broadcasted_iota(jnp.int32, (2 * PAIR, PAIR), 1)
    ones = jnp.where((lane_r < head) == (lane_c < head), 1.0, 0.0).astype(BF16)
    hi, lo = halves(w[...])
    both = jnp.concatenate([hi, lo], 0)
    decay = jnp.exp(mm(levels[...], both))
    ends = jnp.exp(mm(sums[...], both))
    eb_out[...], ee_out[...] = ends[:rows], ends[rows:]
    for p in range(width // PAIR):
        cols = slice(p * PAIR, (p + 1) * PAIR)
        rf, kf = r[:, cols].astype(F32), k[:, cols].astype(F32)
        vf, dyf = v[:, cols].astype(F32), dy[:, cols].astype(F32)
        dydy = block_rows(dy[:, cols], head)
        pairs = mm(dy[:, cols], block_rows(v[:, cols], head), NT)
        pairs_t = mm(v[:, cols], dydy, NT)
        gr = jnp.zeros((rows, PAIR), F32)
        gk = jnp.zeros((rows, PAIR), F32)
        scores_t = jnp.zeros((rows, 2 * rows), F32)
        m, level = 1, 0
        while m < rows:
            d = decay[level * rows : (level + 1) * rows, cols]
            right = (row & m) != 0
            rd = jnp.where(right, rf * d, 0.0).astype(BF16)
            kd = jnp.where(right, 0.0, kf * d).astype(BF16)
            kk, rr = block_rows(kd, head), block_rows(rd, head)
            near = apart < 2 * m
            a = mm(kd, rr, NT)
            scores_t = scores_t + jnp.where(near, a, 0.0)
            here = jnp.where(near, pairs, 0.0).astype(BF16)
            here_t = jnp.where(near, pairs_t, 0.0).astype(BF16)
            gr = gr + jnp.where(right, d * mm(here, kk), 0.0)
            gk = gk + jnp.where(right, 0.0, d * mm(here_t, rr))
            m, level = 2 * m, level + 1
        sh, sl = halves(dyf * vf)
        own = mm(jnp.concatenate([sh, sl], 1), ones)
        bh, bl = halves(rf * u[:, cols] * kf)
        bonus = mm(jnp.concatenate([bh, bl], 1), ones)
        gr_out[:, cols] = gr
        gk_out[:, cols] = gk
        gv_out[:, cols] = mm(scores_t.astype(BF16), dydy) + bonus * dyf
        self_out[:, cols] = own
        du_out[:, cols] = jnp.sum(rf * kf * own, 0, keepdims=True)
    if skip:

        @pl.when(at_last)
        def _():
            for copy in out:
                copy.wait()


def outer_kernel(
    head, ring, r, k, v, dy, u, gr0, gk0, gv0, own, eb, ee, st, end, far, *refs
):
    place = position()
    msgs = refs[: ring - 1]
    proj, r_gr, k_gk, at_end = refs[ring - 1 :]
    width = r.shape[1]
    late, z = place[0] == 1, place[1]
    zero = jnp.zeros((head, width), F32)
    nothing = jnp.zeros((1, width), F32)
    state, grad, past, future = zero, zero, nothing, nothing
    for d in range(1, ring):
        msg = msgs[d - 1]
        live = d <= z
        state = state + jnp.where(live, jnp.exp(past) * msg[:head].astype(F32), 0.0)
        past = past + jnp.where(live, joined(msg, head), 0.0)
    for d in range(ring - 1, 0, -1):
        msg = msgs[d - 1]
        live = d > z
        grad = grad + jnp.where(live, jnp.exp(future) * msg[:head].astype(F32), 0.0)
        future = future + jnp.where(live, joined(msg, head), 0.0)
    ef = jnp.exp(joined(far, 2 * head))
    st_in = jnp.where(late, far[:head].astype(F32) + ef * state, state)
    gt_in = jnp.where(late, grad, far[head : 2 * head].astype(F32) + ef * grad)
    at_end[...] = jnp.sum(gt_in * (jnp.exp(end[...]) * st_in + st[...]), 0, keepdims=True)
    sb, gb = st_in.astype(BF16), gt_in.astype(BF16)
    for p in range(width // PAIR):
        cols = slice(p * PAIR, (p + 1) * PAIR)
        grads = block_rows(gb[:, cols], head)
        rf, kf = r[:, cols].astype(F32), k[:, cols].astype(F32)
        after = ee[:, cols]
        gr = gr0[:, cols] + eb[:, cols] * mm(dy[:, cols], block_rows(sb[:, cols], head))
        gk = gk0[:, cols] + after * mm(v[:, cols], grads)
        gv = gv0[:, cols] + mm((kf * after).astype(BF16), grads, NT)
        s = own[:, cols] * u[:, cols]
        proj[0, :, cols] = (gr + kf * s).astype(BF16)
        proj[1, :, cols] = (gk + rf * s).astype(BF16)
        proj[2, :, cols] = gv.astype(BF16)
        r_gr[:, cols] = rf * gr
        k_gk[:, cols] = kf * gk


def decay_grad_kernel(w, r_gr, k_gk, at_end, up, lora_t, cums, up_grad, base_grad, mid_grad):
    ah, al = halves(r_gr[...])
    bh, bl = halves(k_gk[...])
    gp = (mm(cums[...], jnp.concatenate([ah, al, bh, bl], 0)) + at_end[...]) * w[...]
    gpb = gp.astype(BF16)
    up_grad[...] = mm(lora_t[...], gpb)
    base_grad[...] = jnp.sum(gp, 0, keepdims=True)
    mid_grad[...] = mm(gpb, up[...].astype(BF16), NT)


def middle_kernel(count, x, carried, mix, down, lora, *refs):
    mids, sides, (keep, send, grad_in) = refs[:count], refs[count:-3], refs[-3:]
    total = mids[0][...]
    for part in mids[1:]:
        total = total + part[...]
    mid = total * (1.0 - lora[...] * lora[...])
    grad_in[...] = mm3(mid, down[...], NT)
    down_grad = mm3(mid.T, mixed_input(x, carried, mix))
    rank, half = mid.shape[1], x.shape[1] // 2
    wide = (8, half)
    late = position()[0] == 1

    def choose(low, high, at, size):
        keep[at : at + size] = jnp.where(late, high, low).astype(BF16)
        send[at : at + size] = jnp.where(late, low, high).astype(BF16)

    up_low, up_high, base_low, base_high, du_low, du_high = [ref[...] for ref in sides]
    choose(up_low, up_high, 0, rank)
    choose(down_grad[:, :half], down_grad[:, half:], rank, rank)
    for at, low, high in ((0, base_low, base_high), (8, du_low, du_high)):
        choose(jnp.broadcast_to(low, wide), jnp.broadcast_to(high, wide), 2 * rank + at, 8)


def finish_kernel(rank, mine, theirs, up, down, base, du):
    late = position()[0] == 1
    half = mine.shape[1]
    a, b = mine[...].astype(F32), theirs[...].astype(F32)
    for at, value in ((0, jnp.where(late, b, a)), (half, jnp.where(late, a, b))):
        here = slice(at, at + half)
        up[:, here] = value[:rank]
        down[here] = value[rank : 2 * rank].T
        for ref, row in ((base, 2 * rank), (du, 2 * rank + 8)):
            size = ref.shape[1]
            for i in range(half // size):
                to = at // size + i
                ref[to : to + 1] = value[row : row + 1, i * size : (i + 1) * size]


def project_kernel(count, ring, final, *refs):
    place = position()
    lows, highs, given, mix = refs[:count], refs[count : 2 * count], refs[2 * count : 2 * count + 3], refs[2 * count + 3]
    rest, (low, high, weights, own, prior, sem) = refs[2 * count + 4 : -6], refs[-6:]
    done, outs = (rest[:-ring], rest[-ring:]) if final else ((), rest)
    rows, width = lows[0].shape[1:]
    n = weights.shape[2]
    copies = []

    def fetch(source, target):
        copy = pltpu.make_async_copy(source, target, sem.at[len(copies)])
        copy.start()
        copies.append(copy)
        return copy

    weight_copies, block_copies = [], []
    for i in range(2):
        for m in range(3):
            if i == 0:
                weight_copies.append([fetch(given[0].at[m], weights.at[0, m])])
            else:
                first, cut = given[1].at[m], given[1].shape[1]
                weight_copies.append(
                    [
                        fetch(first, weights.at[1, m, pl.ds(0, cut)]),
                        fetch(given[2].at[m], weights.at[1, m, pl.ds(cut, n - cut)]),
                    ]
                )
            if i == 0:
                places = [pl.ds(q * rows, rows) for q in range(count)]
                block_copies.append(
                    [fetch(lows[q].at[m], low.at[m, at]) for q, at in enumerate(places)]
                    + [fetch(highs[q].at[m], high.at[m, at]) for q, at in enumerate(places)]
                )

    for i in range(2):
        column = pl.ds(pl.multiple_of((place[0] if i == 0 else 1 - place[0]) * n, n), n)
        for m in range(3):
            for copy in (block_copies[m] if i == 0 else []) + weight_copies[i * 3 + m]:
                copy.wait()
            term = mm(low[m], weights[i, m, :, :width], NT) + mm(high[m], weights[i, m, :, width:], NT)
            later = mix[m : m + 1, column] * term
            own[...] = term - later if m == 0 else own[...] + (term - later)
            prior[...] = later if m == 0 else prior[...] + later
        last = lax.broadcasted_iota(jnp.int32, (rows, n), 0) == rows - 1
        top = lax.broadcasted_iota(jnp.int32, (16, n), 0) == 0

        def store(out, q):
            here = slice(q * rows, (q + 1) * rows)
            part = prior[here]
            moved = jnp.where(last, 0.0, pltpu.roll(part, rows - 1, 0))
            out[:rows, column] = (own[here] + moved).astype(BF16)
            out[rows:, column] = jnp.where(top, part[:16], 0.0).astype(BF16)

        if not final:
            for q in range(count):
                store(outs[q], q)
            continue
        for d in range(ring):
            wanted = lax.rem(place[1] - lax.bitwise_xor(place[2], d) + ring, ring)
            for q in range(ring):

                @pl.when(wanted == q)
                def _():
                    if q == ring - 1:
                        store(outs[d], 0)
                    else:
                        outs[d][:, column] = done[q][:, column]


def per_device(
    layer_input, receptance, key_act, value_act, attention_result_sensitivity, time_first,
    decay_exponent_base, decay_shift_mix, mix_rkv, decay_adapter_down, decay_adapter_up, proj_weights,
):
    rows, cols = layer_input.shape
    heads, head = time_first.shape
    rank = decay_adapter_down.shape[1]
    n_seq, n_head = lax.axis_size("seq"), lax.axis_size("head")
    inner = n_seq // n_head
    ring = n_seq // inner
    pairs = cols // PAIR
    parts = 2
    part_cols = cols // parts
    block = min(part_cols, 2 * PAIR)
    r, k, v, dy = receptance, key_act, value_act, attention_result_sensitivity
    params = pltpu.CompilerParams(vmem_limit_bytes=VMEM)

    def shape(s, t=F32):
        return jax.ShapeDtypeStruct(s, t)

    def work(us):
        return pl.CostEstimate(flops=0, transcendentals=0, bytes_accessed=int(us * 3.5e6))

    def shift(a, distance):
        return lax.ppermute(
            a, "seq", [(i - distance, i) for i in range(n_seq) if 0 <= i - distance < n_seq]
        )

    def around(a, step):
        return lax.ppermute(a, "seq", [(i, (i + inner * step) % n_seq) for i in range(n_seq)])

    def partner(a):
        return lax.ppermute(a, "seq", [(i, i ^ 1) for i in range(n_seq)])

    def head_shift(a, d):
        return lax.ppermute(a, "head", [(i, (i + d) % n_head) for i in range(n_head)])

    def head_parts(a):
        return [a] + [head_shift(a, d) for d in range(1, n_head)]

    def after_that(value, *others):
        return lax.optimization_barrier((value, *others))[0]

    weight_rows = proj_weights.shape[1]
    cut = max(weight_rows * 3 // 256, 1) * 16
    anywhere = pl.BlockSpec(memory_space=pl.ANY)
    vmem = pl.BlockSpec(memory_space=pltpu.VMEM)

    carried, piece = lax.optimization_barrier((shift(layer_input[rows - 1 :], 1), proj_weights[:, :cut]))
    fars = [partner(piece)]
    shift_mix = decay_shift_mix.reshape(1, cols)
    pre = pl.pallas_call(
        adapter_kernel,
        out_shape=shape((rows, rank)),
        compiler_params=params,
        cost_estimate=work(1.5),
        name="adapter_input",
    )(layer_input, carried, shift_mix, decay_adapter_down)
    pres = head_parts(pre)

    sums = jnp.asarray(sum_matrix(rows), BF16)
    levels = jnp.asarray(level_matrix(rows), BF16)
    cums = jnp.asarray(cumulative_matrix(rows), BF16)
    far_rows = 2 * head + 8

    lora, lora_t, w, end, st, msg = pl.pallas_call(
        lambda *refs: decay_kernel(head, n_head, *refs),
        out_shape=[
            shape((rows, rank)), shape((rank, rows), BF16), shape((rows, cols)), shape((1, cols)),
            shape((head, cols)), shape((far_rows, cols), BF16),
        ],
        compiler_params=params,
        cost_estimate=work(3),
        name="decay_and_states",
    )(*pres, decay_exponent_base.reshape(1, cols), decay_adapter_up, r, k, v, dy, sums)

    vmem = pl.BlockSpec(memory_space=pltpu.VMEM)
    u = after_that(time_first, msg).reshape(1, cols)

    def col_block(n, width=block, offset=0):
        return pl.BlockSpec((n, width), lambda p, *_: (0, p + offset))

    def whole(s):
        return pl.BlockSpec(s, lambda p, *_: (0,) * len(s))

    steps = part_cols // block
    here = col_block(rows)

    def inside(part):
        at = lambda n: col_block(n, block, part * steps)
        extra = part == 0
        return pl.pallas_call(
            lambda *refs: inner_kernel(head, cut if extra else 0, *refs),
            grid=(steps,),
            in_specs=[at(rows)] * 5 + [at(1), whole(levels.shape), whole(sums.shape)] + [anywhere] * extra,
            out_specs=[here] * 6 + [col_block(1)] + [anywhere] * extra,
            out_shape=[shape((rows, part_cols))] * 6 + [shape((1, part_cols))]
            + [shape((3, weight_rows - cut, cols), BF16)] * extra,
            scratch_shapes=[
                pltpu.VMEM((3, weight_rows - cut, cols), BF16), pltpu.SemaphoreType.DMA((6,)),
            ] * extra,
            compiler_params=params,
            cost_estimate=work(4),
            name="inside_chunk",
        )(r, k, v, dy, after_that(w, fars[0]) if extra else w, u, levels, sums, *[proj_weights] * extra)

    inner_parts = [inside(part) for part in range(parts)]
    far, piece, inner_parts[0] = lax.optimization_barrier(
        (partner(msg), inner_parts[0][7], inner_parts[0][:7])
    )
    fars.append(partner(piece))
    out_msgs = pl.pallas_call(
        lambda *refs: pair_kernel(head, ring, *refs),
                out_shape=[shape((head + 8, cols), BF16)] * (ring - 1),
        compiler_params=params,
        cost_estimate=work(1.5),
        name="pair_states",
    )(msg, far)
    msgs = [around(m, d + 1) for d, m in enumerate(out_msgs)]

    inner_parts[1], msgs = lax.optimization_barrier((inner_parts[1], msgs))
    outer = []
    for part in range(parts):
        at = lambda n: col_block(n, block, part * steps)
        outer.append(
            pl.pallas_call(
                lambda *refs: outer_kernel(head, ring, *refs),
                grid=(steps,),
                in_specs=[at(rows)] * 4 + [at(1)] + [here] * 6
                + [at(head), at(1), at(far_rows)] + [at(head + 8)] * (ring - 1),
                out_specs=[pl.BlockSpec((3, rows, block), lambda p: (0, 0, p)), here, here, col_block(1)],
                out_shape=[
                    shape((3, rows, part_cols), BF16), shape((rows, part_cols)),
                    shape((rows, part_cols)), shape((1, part_cols)),
                ],
                compiler_params=params,
                cost_estimate=work(3),
                name="across_chunks",
            )(r, k, v, dy, u, *inner_parts[part][:6], st, end, far, *msgs)
        )
    projs = [o[0] for o in outer]

    ups, bases, mid_parts = [], [], []
    for part in range(parts):
        at = lambda n: pl.BlockSpec((n, part_cols), lambda p: (0, part))
        up_grad, base_grad, mid_grad = pl.pallas_call(
            decay_grad_kernel,
            grid=(1,),
            in_specs=[at(rows), *[whole((rows, part_cols))] * 2, whole((1, part_cols)), at(rank)]
            + [whole((rank, rows)), whole(cums.shape)],
            out_specs=[whole((rank, part_cols)), whole((1, part_cols)), whole((rows, rank))],
            out_shape=[shape((rank, part_cols)), shape((1, part_cols)), shape((rows, rank))],
            compiler_params=params,
            cost_estimate=work(2),
            name="decay_gradient",
        )(w, *outer[part][1:], decay_adapter_up, lora_t, cums)
        ups.append(up_grad)
        bases.append(base_grad)
        mid_parts.append(mid_grad)
    mid_grad = sum(mid_parts)

    mids = head_parts(mid_grad)
    dus = [part[6] for part in inner_parts]
    keep, send, grad_in = pl.pallas_call(
        lambda *refs: middle_kernel(n_head, *refs),
        in_specs=[vmem] * (5 + n_head + 3 * parts),
        out_shape=[shape((2 * rank + 16, part_cols), BF16)] * 2 + [shape((rows, cols))],
        compiler_params=params,
        cost_estimate=work(3),
        name="adapter_grads",
    )(
        layer_input, carried, shift_mix, decay_adapter_down, lora, *mids, *ups, *bases, *dus
    )

    lows, highs = [projs[0]], [projs[1]]
    for step in range(ring - 1):
        low, high = lows[-1], highs[-1]
        lows.append(around(after_that(low, mid_grad) if step == 1 else low, 1))
        highs.append(around(after_that(high, keep) if step == 1 else high, 1))

    def add(a, b):
        return (a.astype(F32) + b.astype(F32)).astype(BF16)

    got = partner(after_that(send, lows[2]))

    mix_here = lax.dynamic_slice_in_dim(after_that(mix_rkv, *out_msgs), position()[1] * cols, cols, 1)

    tall = rows + 16

    def project(low, high, done=()):
        count, final = len(low), len(done) > 0
        return pl.pallas_call(
            lambda *refs: project_kernel(count, ring, final, *refs),
            in_specs=[anywhere] * (2 * count + 3) + [vmem] * (1 + len(done)),
            out_shape=[shape((tall, cols), BF16)] * (ring if final else count),
            scratch_shapes=[
                pltpu.VMEM((3, count * rows, part_cols), BF16),
                pltpu.VMEM((3, count * rows, part_cols), BF16),
                pltpu.VMEM((inner, 3, weight_rows, cols), BF16),
                pltpu.VMEM((count * rows, weight_rows), F32),
                pltpu.VMEM((count * rows, weight_rows), F32),
                pltpu.SemaphoreType.DMA((3 * (2 * count + 3),)),
            ],
            compiler_params=pltpu.CompilerParams(vmem_limit_bytes=24 * 2**20),
            cost_estimate=work(5),
            name="projections",
        )(*low, *high, proj_weights, *fars, mix_here, *done)

    done = project(lows[:-1], highs[:-1])
    sends = project(lows[-1:], highs[-1:], done)
    def across(a, bit):
        return lax.ppermute(a, "head", [(i, i ^ bit) for i in range(n_head)])

    left, bit = dict(enumerate(sends)), 1
    while bit < n_head:
        came = {e: across(left[e | bit], bit) for e in left if not e & bit}
        left = {e: left[e].astype(F32) + came[e].astype(F32) for e in came}
        bit *= 2
        if bit < n_head:
            left = {e: value.astype(BF16) for e, value in left.items()}
    total = left[0]
    token_sums = add(keep, after_that(got, *done))
    b = 1
    while b < ring:
        route = [(i, ((i // inner) ^ b) * inner + i % inner) for i in range(n_seq)]
        got = lax.ppermute(token_sums, "seq", route)
        token_sums = add(token_sums, after_that(got, {1: sends, 2: total}.get(b, ())))
        b *= 2
    up_grad, down_grad, base_grad, du = pl.pallas_call(
        lambda *refs: finish_kernel(rank, *refs),
                out_shape=[shape((rank, cols)), shape((cols, rank)), shape((pairs, PAIR)), shape((heads, head))],
        compiler_params=pltpu.CompilerParams(vmem_limit_bytes=16 * 2**20),
        cost_estimate=work(2),
        name="token_sums",
    )(token_sums, partner(token_sums))

    swap, back = [], []
    for h in range(n_head):
        for z in range(ring):
            for x in range(inner):
                source = h * n_seq + z * inner + x
                block_at = h * inner + x
                swap.append((source, z * n_seq + block_at))
                if block_at > 0:
                    back.append((source, z * n_seq + block_at - 1))
    base_grad = base_grad.reshape(cols)
    summed = lax.ppermute(total[:rows].astype(BF16), ("head", "seq"), swap)
    edge = lax.ppermute(total[rows : rows + 1], ("head", "seq"), back)
    summed = after_that(summed, up_grad, base_grad, du)
    grad_next = jnp.concatenate([grad_in[1:], shift(grad_in[:1], -1)], 0)
    adapter_term = (1.0 - decay_shift_mix) * grad_in + decay_shift_mix * grad_next
    last = lax.broadcasted_iota(jnp.int32, (rows, 1), 0) == rows - 1
    result = (summed.astype(F32) + adapter_term + jnp.where(last, edge, 0.0)).astype(BF16)
    return (result, down_grad, up_grad, base_grad, du)


def solution(mesh):
    return jax.shard_map(
        per_device,
        mesh=mesh,
        in_specs=(
            P("seq", "head"), P("seq", "head"), P("seq", "head"), P("seq", "head"), P("seq", "head"),
            P("head", None), P("head"), P("head"), P(), P("head", None), P(None, "head"),
            P(None, "seq", "head"),
        ),
        out_specs=(P("seq", "head"), P("head", None), P(None, "head"), P("head"), P("head", None)),
        check_vma=False,
    )
```

```python
import jax
import jax.numpy as jnp
import numpy as np
from jax import lax
from jax.experimental import pallas as pl
from jax.experimental.pallas import tpu as pltpu
from jax.sharding import PartitionSpec as P

F32 = jnp.float32
BF16 = jnp.bfloat16
PAIR = 128
VMEM = 56 * 2**20
NN = (((1,), (0,)), ((), ()))
NT = (((1,), (1,)), ((), ()))
TN = (((0,), (0,)), ((), ()))


def position():
    seq, head = lax.axis_index("seq"), lax.axis_index("head")
    inner = lax.axis_size("seq") // lax.axis_size("head")
    return lax.rem(seq, inner), lax.div(seq, inner), head


def mm(a, b, dims=NN):
    return lax.dot_general(a, b, dims, preferred_element_type=F32)


def halves(a):
    hi = a.astype(BF16)
    return hi, (a - hi.astype(F32)).astype(BF16)


def low_lanes(shape, half):
    return lax.broadcasted_iota(jnp.int32, shape, len(shape) - 1) < half


def block_rows(a, half):
    low = low_lanes(a.shape, half)
    zero = jnp.zeros_like(a)
    return jnp.concatenate([jnp.where(low, a, zero), jnp.where(low, zero, a)], 0)


def fold(a, half):
    rows = a.shape[0] // 2
    return jnp.where(low_lanes((rows, a.shape[1]), half), a[:rows], a[rows:])


def sum_matrix(rows):
    t = np.arange(rows)
    both = np.concatenate([t[:, None] > t[None, :], t[:, None] < t[None, :]], 0)
    return np.concatenate([both, both], 1).astype(np.float32)


def level_matrix(rows):
    t = np.arange(rows)
    parts = []
    m = 1
    while m < rows:
        mid = (t // (2 * m)) * 2 * m + m
        right = t >= mid
        u = t[None, :]
        take_right = (u >= mid[:, None]) & (u < t[:, None])
        take_left = (u > t[:, None]) & (u < mid[:, None])
        parts.append(np.where(right[:, None], take_right, take_left))
        m *= 2
    both = np.concatenate(parts, 0)
    return np.concatenate([both, both], 1).astype(np.float32)


def cumulative_matrix(rows):
    t = np.arange(rows)
    strict = (t[:, None] < t[None, :]).astype(np.float32)
    full = (t[:, None] <= t[None, :]).astype(np.float32)
    return np.concatenate([strict, strict, -full, -full], 1)


def split_rows(a):
    hi, lo = halves(a)
    wide = (4, a.shape[1])
    return jnp.concatenate([jnp.broadcast_to(hi, wide), jnp.broadcast_to(lo, wide)], 0)


def joined(msg, at):
    return msg[at : at + 1].astype(F32) + msg[at + 4 : at + 5].astype(F32)


def mm3(a, b, dims=NN):
    ah, al = halves(a)
    bh, bl = halves(b)
    return mm(ah, bh, dims) + (mm(ah, bl, dims) + mm(al, bh, dims))


def mixed_input(x, carried, mix):
    features = x[...].astype(F32)
    row = lax.broadcasted_iota(jnp.int32, features.shape, 0)
    previous = jnp.where(row == 0, carried[...].astype(F32), pltpu.roll(features, 1, 0))
    return features + mix[...] * (previous - features)


def copy_rows(weights, piece, at, stage, sem):
    rows = pl.ds(at, piece.shape[1])
    into = [pltpu.make_async_copy(weights.at[m, rows], stage.at[m], sem.at[m]) for m in range(3)]
    out = [pltpu.make_async_copy(stage.at[m], piece.at[m], sem.at[3 + m]) for m in range(3)]
    return into, out


def adapter_kernel(x, carried, mix, down, pre):
    pre[...] = mm3(mixed_input(x, carried, mix), down[...])


def decay_kernel(head, count, *refs):
    pres = refs[:count]
    base, up, r, k, v, dy, sums, lora, lora_t, w_out, end, st, msg = refs[count:]
    rows = r.shape[0]
    total = pres[0][...]
    for pre in pres[1:]:
        total = total + pre[...]
    mid = jnp.tanh(total)
    lora[...] = mid
    lora_t[...] = mid.T.astype(BF16)
    w = -jnp.exp(base[...] + mm3(mid, up[...]))
    w_out[...] = w
    hi, lo = halves(w)
    args = mm(sums[...], jnp.concatenate([hi, lo], 0))
    before, after = args[:rows], args[rows:]
    final = before[rows - 1 :] + w[rows - 1 :]
    end[...] = final
    from_start, to_end = jnp.exp(before), jnp.exp(after)
    kf = (k[...].astype(F32) * to_end).astype(BF16)
    rb = (r[...].astype(F32) * from_start).astype(BF16)
    for p in range(r.shape[1] // PAIR):
        cols = slice(p * PAIR, (p + 1) * PAIR)
        state = fold(mm(v[:, cols], kf[:, cols], TN), head)
        st[:, cols] = state
        msg[:head, cols] = state.astype(BF16)
        msg[head : 2 * head, cols] = fold(mm(dy[:, cols], rb[:, cols], TN), head).astype(BF16)
    msg[2 * head :] = split_rows(final)


def pair_kernel(head, ring, own, far, *outs):
    place = position()
    late = place[0] == 1
    dec_own, dec_far = joined(own, 2 * head), joined(far, 2 * head)
    eo, ef = jnp.exp(dec_own), jnp.exp(dec_far)
    st_own, st_far = own[:head].astype(F32), far[:head].astype(F32)
    gt_own, gt_far = own[head : 2 * head].astype(F32), far[head : 2 * head].astype(F32)
    state = jnp.where(late, st_own + eo * st_far, st_far + ef * st_own).astype(BF16)
    grad = jnp.where(late, gt_far + ef * gt_own, gt_own + eo * gt_far).astype(BF16)
    decays = split_rows(dec_own + dec_far)
    for d in range(1, ring):
        out = outs[d - 1]
        ahead = place[1] + d < ring

        @pl.when(ahead)
        def _():
            out[:head] = state

        @pl.when(jnp.logical_not(ahead))
        def _():
            out[:head] = grad

        out[head:] = decays


def inner_kernel(head, skip, r, k, v, dy, w, u, levels, sums, *refs):
    if skip:
        weights, piece, stage, sem = refs[0], refs[8], refs[9], refs[10]
        refs = refs[1:8]
        into, out = copy_rows(weights, piece, skip, stage, sem)
        at_last = pl.program_id(0) == pl.num_programs(0) - 1

        @pl.when(pl.program_id(0) == 0)
        def _():
            for copy in into:
                copy.start()

        @pl.when(at_last)
        def _():
            for first, second in zip(into, out):
                first.wait()
                second.start()

    gr_out, gk_out, gv_out, self_out, eb_out, ee_out, du_out = refs
    rows, width = r.shape
    row = lax.broadcasted_iota(jnp.int32, (rows, PAIR), 0)
    row2 = lax.broadcasted_iota(jnp.int32, (rows, 2 * rows), 0)
    col2 = lax.broadcasted_iota(jnp.int32, (rows, 2 * rows), 1)
    apart = row2 ^ (col2 & (rows - 1))
    lane_r = lax.broadcasted_iota(jnp.int32, (2 * PAIR, PAIR), 0) & (PAIR - 1)
    lane_c = lax.broadcasted_iota(jnp.int32, (2 * PAIR, PAIR), 1)
    ones = jnp.where((lane_r < head) == (lane_c < head), 1.0, 0.0).astype(BF16)
    hi, lo = halves(w[...])
    both = jnp.concatenate([hi, lo], 0)
    decay = jnp.exp(mm(levels[...], both))
    ends = jnp.exp(mm(sums[...], both))
    eb_out[...], ee_out[...] = ends[:rows], ends[rows:]
    for p in range(width // PAIR):
        cols = slice(p * PAIR, (p + 1) * PAIR)
        rf, kf = r[:, cols].astype(F32), k[:, cols].astype(F32)
        vf, dyf = v[:, cols].astype(F32), dy[:, cols].astype(F32)
        dydy = block_rows(dy[:, cols], head)
        pairs = mm(dy[:, cols], block_rows(v[:, cols], head), NT)
        pairs_t = mm(v[:, cols], dydy, NT)
        gr = jnp.zeros((rows, PAIR), F32)
        gk = jnp.zeros((rows, PAIR), F32)
        scores_t = jnp.zeros((rows, 2 * rows), F32)
        m, level = 1, 0
        while m < rows:
            d = decay[level * rows : (level + 1) * rows, cols]
            right = (row & m) != 0
            rd = jnp.where(right, rf * d, 0.0).astype(BF16)
            kd = jnp.where(right, 0.0, kf * d).astype(BF16)
            kk, rr = block_rows(kd, head), block_rows(rd, head)
            near = apart < 2 * m
            a = mm(kd, rr, NT)
            scores_t = scores_t + jnp.where(near, a, 0.0)
            here = jnp.where(near, pairs, 0.0).astype(BF16)
            here_t = jnp.where(near, pairs_t, 0.0).astype(BF16)
            gr = gr + jnp.where(right, d * mm(here, kk), 0.0)
            gk = gk + jnp.where(right, 0.0, d * mm(here_t, rr))
            m, level = 2 * m, level + 1
        sh, sl = halves(dyf * vf)
        own = mm(jnp.concatenate([sh, sl], 1), ones)
        bh, bl = halves(rf * u[:, cols] * kf)
        bonus = mm(jnp.concatenate([bh, bl], 1), ones)
        gr_out[:, cols] = gr
        gk_out[:, cols] = gk
        gv_out[:, cols] = mm(scores_t.astype(BF16), dydy) + bonus * dyf
        self_out[:, cols] = own
        du_out[:, cols] = jnp.sum(rf * kf * own, 0, keepdims=True)
    if skip:

        @pl.when(at_last)
        def _():
            for copy in out:
                copy.wait()


def outer_kernel(
    head, ring, r, k, v, dy, u, gr0, gk0, gv0, own, eb, ee, st, end, far, *refs
):
    place = position()
    msgs = refs[: ring - 1]
    proj, r_gr, k_gk, at_end = refs[ring - 1 :]
    width = r.shape[1]
    late, z = place[0] == 1, place[1]
    zero = jnp.zeros((head, width), F32)
    nothing = jnp.zeros((1, width), F32)
    state, grad, past, future = zero, zero, nothing, nothing
    for d in range(1, ring):
        msg = msgs[d - 1]
        live = d <= z
        state = state + jnp.where(live, jnp.exp(past) * msg[:head].astype(F32), 0.0)
        past = past + jnp.where(live, joined(msg, head), 0.0)
    for d in range(ring - 1, 0, -1):
        msg = msgs[d - 1]
        live = d > z
        grad = grad + jnp.where(live, jnp.exp(future) * msg[:head].astype(F32), 0.0)
        future = future + jnp.where(live, joined(msg, head), 0.0)
    ef = jnp.exp(joined(far, 2 * head))
    st_in = jnp.where(late, far[:head].astype(F32) + ef * state, state)
    gt_in = jnp.where(late, grad, far[head : 2 * head].astype(F32) + ef * grad)
    at_end[...] = jnp.sum(gt_in * (jnp.exp(end[...]) * st_in + st[...]), 0, keepdims=True)
    sb, gb = st_in.astype(BF16), gt_in.astype(BF16)
    for p in range(width // PAIR):
        cols = slice(p * PAIR, (p + 1) * PAIR)
        grads = block_rows(gb[:, cols], head)
        rf, kf = r[:, cols].astype(F32), k[:, cols].astype(F32)
        after = ee[:, cols]
        gr = gr0[:, cols] + eb[:, cols] * mm(dy[:, cols], block_rows(sb[:, cols], head))
        gk = gk0[:, cols] + after * mm(v[:, cols], grads)
        gv = gv0[:, cols] + mm((kf * after).astype(BF16), grads, NT)
        s = own[:, cols] * u[:, cols]
        proj[0, :, cols] = (gr + kf * s).astype(BF16)
        proj[1, :, cols] = (gk + rf * s).astype(BF16)
        proj[2, :, cols] = gv.astype(BF16)
        r_gr[:, cols] = rf * gr
        k_gk[:, cols] = kf * gk


def decay_grad_kernel(w, r_gr, k_gk, at_end, up, lora_t, cums, up_grad, base_grad, mid_grad):
    ah, al = halves(r_gr[...])
    bh, bl = halves(k_gk[...])
    gp = (mm(cums[...], jnp.concatenate([ah, al, bh, bl], 0)) + at_end[...]) * w[...]
    gpb = gp.astype(BF16)
    up_grad[...] = mm(lora_t[...], gpb)
    base_grad[...] = jnp.sum(gp, 0, keepdims=True)
    mid_grad[...] = mm(gpb, up[...].astype(BF16), NT)


def middle_kernel(count, x, carried, mix, down, lora, *refs):
    mids, sides, (keep, send, grad_in) = refs[:count], refs[count:-3], refs[-3:]
    total = mids[0][...]
    for part in mids[1:]:
        total = total + part[...]
    mid = total * (1.0 - lora[...] * lora[...])
    grad_in[...] = mm3(mid, down[...], NT)
    down_grad = mm3(mid.T, mixed_input(x, carried, mix))
    rank, half = mid.shape[1], x.shape[1] // 2
    wide = (8, half)
    late = position()[0] == 1

    def choose(low, high, at, size):
        keep[at : at + size] = jnp.where(late, high, low).astype(BF16)
        send[at : at + size] = jnp.where(late, low, high).astype(BF16)

    up_low, up_high, base_low, base_high, du_low, du_high = [ref[...] for ref in sides]
    choose(up_low, up_high, 0, rank)
    choose(down_grad[:, :half], down_grad[:, half:], rank, rank)
    for at, low, high in ((0, base_low, base_high), (8, du_low, du_high)):
        choose(jnp.broadcast_to(low, wide), jnp.broadcast_to(high, wide), 2 * rank + at, 8)


def finish_kernel(rank, mine, theirs, up, down, base, du):
    late = position()[0] == 1
    half = mine.shape[1]
    a, b = mine[...].astype(F32), theirs[...].astype(F32)
    for at, value in ((0, jnp.where(late, b, a)), (half, jnp.where(late, a, b))):
        here = slice(at, at + half)
        up[:, here] = value[:rank]
        down[here] = value[rank : 2 * rank].T
        for ref, row in ((base, 2 * rank), (du, 2 * rank + 8)):
            size = ref.shape[1]
            for i in range(half // size):
                to = at // size + i
                ref[to : to + 1] = value[row : row + 1, i * size : (i + 1) * size]


def project_kernel(count, ring, final, *refs):
    place = position()
    lows, highs, given, mix = refs[:count], refs[count : 2 * count], refs[2 * count : 2 * count + 3], refs[2 * count + 3]
    rest, (low, high, weights, own, prior, sem) = refs[2 * count + 4 : -6], refs[-6:]
    done, outs = (rest[:-ring], rest[-ring:]) if final else ((), rest)
    rows, width = lows[0].shape[1:]
    n = weights.shape[2]
    copies = []

    def fetch(source, target):
        copy = pltpu.make_async_copy(source, target, sem.at[len(copies)])
        copy.start()
        copies.append(copy)
        return copy

    weight_copies, block_copies = [], []
    for i in range(2):
        for m in range(3):
            if i == 0:
                weight_copies.append([fetch(given[0].at[m], weights.at[0, m])])
            else:
                first, cut = given[1].at[m], given[1].shape[1]
                weight_copies.append(
                    [
                        fetch(first, weights.at[1, m, pl.ds(0, cut)]),
                        fetch(given[2].at[m], weights.at[1, m, pl.ds(cut, n - cut)]),
                    ]
                )
            if i == 0:
                places = [pl.ds(q * rows, rows) for q in range(count)]
                block_copies.append(
                    [fetch(lows[q].at[m], low.at[m, at]) for q, at in enumerate(places)]
                    + [fetch(highs[q].at[m], high.at[m, at]) for q, at in enumerate(places)]
                )

    for i in range(2):
        column = pl.ds(pl.multiple_of((place[0] if i == 0 else 1 - place[0]) * n, n), n)
        for m in range(3):
            for copy in (block_copies[m] if i == 0 else []) + weight_copies[i * 3 + m]:
                copy.wait()
            term = mm(low[m], weights[i, m, :, :width], NT) + mm(high[m], weights[i, m, :, width:], NT)
            later = mix[m : m + 1, column] * term
            own[...] = term - later if m == 0 else own[...] + (term - later)
            prior[...] = later if m == 0 else prior[...] + later
        last = lax.broadcasted_iota(jnp.int32, (rows, n), 0) == rows - 1
        top = lax.broadcasted_iota(jnp.int32, (16, n), 0) == 0

        def store(out, q):
            here = slice(q * rows, (q + 1) * rows)
            part = prior[here]
            moved = jnp.where(last, 0.0, pltpu.roll(part, rows - 1, 0))
            out[:rows, column] = (own[here] + moved).astype(BF16)
            out[rows:, column] = jnp.where(top, part[:16], 0.0).astype(BF16)

        if not final:
            for q in range(count):
                store(outs[q], q)
            continue
        for d in range(ring):
            wanted = lax.rem(place[1] - lax.bitwise_xor(place[2], d) + ring, ring)
            for q in range(ring):

                @pl.when(wanted == q)
                def _():
                    if q == ring - 1:
                        store(outs[d], 0)
                    else:
                        outs[d][:, column] = done[q][:, column]


def per_device(
    layer_input, receptance, key_act, value_act, attention_result_sensitivity, time_first,
    decay_exponent_base, decay_shift_mix, mix_rkv, decay_adapter_down, decay_adapter_up, proj_weights,
):
    rows, cols = layer_input.shape
    heads, head = time_first.shape
    rank = decay_adapter_down.shape[1]
    n_seq, n_head = lax.axis_size("seq"), lax.axis_size("head")
    inner = n_seq // n_head
    ring = n_seq // inner
    pairs = cols // PAIR
    parts = 2
    part_cols = cols // parts
    block = min(part_cols, 2 * PAIR)
    r, k, v, dy = receptance, key_act, value_act, attention_result_sensitivity
    params = pltpu.CompilerParams(vmem_limit_bytes=VMEM)

    def shape(s, t=F32):
        return jax.ShapeDtypeStruct(s, t)

    def work(us):
        return pl.CostEstimate(flops=0, transcendentals=0, bytes_accessed=int(us * 3.5e6))

    def shift(a, distance):
        return lax.ppermute(
            a, "seq", [(i - distance, i) for i in range(n_seq) if 0 <= i - distance < n_seq]
        )

    def around(a, step):
        return lax.ppermute(a, "seq", [(i, (i + inner * step) % n_seq) for i in range(n_seq)])

    def partner(a):
        return lax.ppermute(a, "seq", [(i, i ^ 1) for i in range(n_seq)])

    def head_shift(a, d):
        return lax.ppermute(a, "head", [(i, (i + d) % n_head) for i in range(n_head)])

    def head_parts(a):
        return [a] + [head_shift(a, d) for d in range(1, n_head)]

    def after_that(value, *others):
        return lax.optimization_barrier((value, *others))[0]

    weight_rows = proj_weights.shape[1]
    cut = max(weight_rows * 3 // 256, 1) * 16
    anywhere = pl.BlockSpec(memory_space=pl.ANY)
    vmem = pl.BlockSpec(memory_space=pltpu.VMEM)

    carried, piece = lax.optimization_barrier((shift(layer_input[rows - 1 :], 1), proj_weights[:, :cut]))
    fars = [partner(piece)]
    shift_mix = decay_shift_mix.reshape(1, cols)
    pre = pl.pallas_call(
        adapter_kernel,
        out_shape=shape((rows, rank)),
        compiler_params=params,
        cost_estimate=work(1.5),
        name="adapter_input",
    )(layer_input, carried, shift_mix, decay_adapter_down)
    pres = head_parts(pre)

    sums = jnp.asarray(sum_matrix(rows), BF16)
    levels = jnp.asarray(level_matrix(rows), BF16)
    cums = jnp.asarray(cumulative_matrix(rows), BF16)
    far_rows = 2 * head + 8

    lora, lora_t, w, end, st, msg = pl.pallas_call(
        lambda *refs: decay_kernel(head, n_head, *refs),
        out_shape=[
            shape((rows, rank)), shape((rank, rows), BF16), shape((rows, cols)), shape((1, cols)),
            shape((head, cols)), shape((far_rows, cols), BF16),
        ],
        compiler_params=params,
        cost_estimate=work(3),
        name="decay_and_states",
    )(*pres, decay_exponent_base.reshape(1, cols), decay_adapter_up, r, k, v, dy, sums)

    vmem = pl.BlockSpec(memory_space=pltpu.VMEM)
    u = after_that(time_first, msg).reshape(1, cols)

    def col_block(n, width=block, offset=0):
        return pl.BlockSpec((n, width), lambda p, *_: (0, p + offset))

    def whole(s):
        return pl.BlockSpec(s, lambda p, *_: (0,) * len(s))

    steps = part_cols // block
    here = col_block(rows)

    def inside(part):
        at = lambda n: col_block(n, block, part * steps)
        extra = part == 0
        return pl.pallas_call(
            lambda *refs: inner_kernel(head, cut if extra else 0, *refs),
            grid=(steps,),
            in_specs=[at(rows)] * 5 + [at(1), whole(levels.shape), whole(sums.shape)] + [anywhere] * extra,
            out_specs=[here] * 6 + [col_block(1)] + [anywhere] * extra,
            out_shape=[shape((rows, part_cols))] * 6 + [shape((1, part_cols))]
            + [shape((3, weight_rows - cut, cols), BF16)] * extra,
            scratch_shapes=[
                pltpu.VMEM((3, weight_rows - cut, cols), BF16), pltpu.SemaphoreType.DMA((6,)),
            ] * extra,
            compiler_params=params,
            cost_estimate=work(4),
            name="inside_chunk",
        )(r, k, v, dy, after_that(w, fars[0]) if extra else w, u, levels, sums, *[proj_weights] * extra)

    inner_parts = [inside(part) for part in range(parts)]
    far, piece, inner_parts[0] = lax.optimization_barrier(
        (partner(msg), inner_parts[0][7], inner_parts[0][:7])
    )
    fars.append(partner(piece))
    out_msgs = pl.pallas_call(
        lambda *refs: pair_kernel(head, ring, *refs),
                out_shape=[shape((head + 8, cols), BF16)] * (ring - 1),
        compiler_params=params,
        cost_estimate=work(1.5),
        name="pair_states",
    )(msg, far)
    msgs = [around(m, d + 1) for d, m in enumerate(out_msgs)]

    inner_parts[1], msgs = lax.optimization_barrier((inner_parts[1], msgs))
    outer = []
    for part in range(parts):
        at = lambda n: col_block(n, block, part * steps)
        outer.append(
            pl.pallas_call(
                lambda *refs: outer_kernel(head, ring, *refs),
                grid=(steps,),
                in_specs=[at(rows)] * 4 + [at(1)] + [here] * 6
                + [at(head), at(1), at(far_rows)] + [at(head + 8)] * (ring - 1),
                out_specs=[pl.BlockSpec((3, rows, block), lambda p: (0, 0, p)), here, here, col_block(1)],
                out_shape=[
                    shape((3, rows, part_cols), BF16), shape((rows, part_cols)),
                    shape((rows, part_cols)), shape((1, part_cols)),
                ],
                compiler_params=params,
                cost_estimate=work(3),
                name="across_chunks",
            )(r, k, v, dy, u, *inner_parts[part][:6], st, end, far, *msgs)
        )
    projs = [o[0] for o in outer]

    ups, bases, mid_parts = [], [], []
    for part in range(parts):
        at = lambda n: pl.BlockSpec((n, part_cols), lambda p: (0, part))
        up_grad, base_grad, mid_grad = pl.pallas_call(
            decay_grad_kernel,
            grid=(1,),
            in_specs=[at(rows), *[whole((rows, part_cols))] * 2, whole((1, part_cols)), at(rank)]
            + [whole((rank, rows)), whole(cums.shape)],
            out_specs=[whole((rank, part_cols)), whole((1, part_cols)), whole((rows, rank))],
            out_shape=[shape((rank, part_cols)), shape((1, part_cols)), shape((rows, rank))],
            compiler_params=params,
            cost_estimate=work(2),
            name="decay_gradient",
        )(w, *outer[part][1:], decay_adapter_up, lora_t, cums)
        ups.append(up_grad)
        bases.append(base_grad)
        mid_parts.append(mid_grad)
    mid_grad = sum(mid_parts)

    mids = head_parts(mid_grad)
    dus = [part[6] for part in inner_parts]
    keep, send, grad_in = pl.pallas_call(
        lambda *refs: middle_kernel(n_head, *refs),
        in_specs=[vmem] * (5 + n_head + 3 * parts),
        out_shape=[shape((2 * rank + 16, part_cols), BF16)] * 2 + [shape((rows, cols))],
        compiler_params=params,
        cost_estimate=work(3),
        name="adapter_grads",
    )(
        layer_input, carried, shift_mix, decay_adapter_down, lora, *mids, *ups, *bases, *dus
    )

    lows, highs = [projs[0]], [projs[1]]
    for step in range(ring - 1):
        low, high = lows[-1], highs[-1]
        lows.append(around(after_that(low, mid_grad) if step == 1 else low, 1))
        highs.append(around(after_that(high, keep) if step == 1 else high, 1))

    def add(a, b):
        return (a.astype(F32) + b.astype(F32)).astype(BF16)

    got = partner(after_that(send, lows[2]))

    mix_here = lax.dynamic_slice_in_dim(after_that(mix_rkv, *out_msgs), position()[1] * cols, cols, 1)

    tall = rows + 16

    def project(low, high, done=()):
        count, final = len(low), len(done) > 0
        return pl.pallas_call(
            lambda *refs: project_kernel(count, ring, final, *refs),
            in_specs=[anywhere] * (2 * count + 3) + [vmem] * (1 + len(done)),
            out_shape=[shape((tall, cols), BF16)] * (ring if final else count),
            scratch_shapes=[
                pltpu.VMEM((3, count * rows, part_cols), BF16),
                pltpu.VMEM((3, count * rows, part_cols), BF16),
                pltpu.VMEM((inner, 3, weight_rows, cols), BF16),
                pltpu.VMEM((count * rows, weight_rows), F32),
                pltpu.VMEM((count * rows, weight_rows), F32),
                pltpu.SemaphoreType.DMA((3 * (2 * count + 3),)),
            ],
            compiler_params=pltpu.CompilerParams(vmem_limit_bytes=24 * 2**20),
            cost_estimate=work(5),
            name="projections",
        )(*low, *high, proj_weights, *fars, mix_here, *done)

    done = project(lows[:-1], highs[:-1])
    sends = project(lows[-1:], highs[-1:], done)
    token_sums = add(keep, after_that(got, *done))
    def other_z(a, b):
        route = [(i, ((i // inner) ^ b) * inner + i % inner) for i in range(n_seq)]
        return lax.ppermute(a, "seq", route)

    token_sums = add(token_sums, after_that(other_z(token_sums, 1), sends))
    def across(a, bit):
        return lax.ppermute(a, "head", [(i, i ^ bit) for i in range(n_head)])

    left, bit = dict(enumerate(sends)), 1
    while bit < n_head:
        came = {e: across(left[e | bit], bit) for e in left if not e & bit}
        if bit == 1:
            came = {e: after_that(value, token_sums) for e, value in came.items()}
        left = {e: left[e].astype(F32) + came[e].astype(F32) for e in came}
        bit *= 2
        if bit < n_head:
            left = {e: value.astype(BF16) for e, value in left.items()}
    total = left[0]
    swap, back = [], []
    for h in range(n_head):
        for z in range(ring):
            for x in range(inner):
                source = h * n_seq + z * inner + x
                block_at = h * inner + x
                swap.append((source, z * n_seq + block_at))
                if block_at > 0:
                    back.append((source, z * n_seq + block_at - 1))
    summed = lax.ppermute(total[:rows].astype(BF16), ("head", "seq"), swap)
    edge = lax.ppermute(total[rows : rows + 1], ("head", "seq"), back)
    b = 2
    while b < ring:
        got = other_z(token_sums, b)
        token_sums = add(token_sums, after_that(got, edge) if b == 2 else got)
        b *= 2
    up_grad, down_grad, base_grad, du = pl.pallas_call(
        lambda *refs: finish_kernel(rank, *refs),
                out_shape=[shape((rank, cols)), shape((cols, rank)), shape((pairs, PAIR)), shape((heads, head))],
        compiler_params=pltpu.CompilerParams(vmem_limit_bytes=16 * 2**20),
        cost_estimate=work(2),
        name="token_sums",
    )(token_sums, partner(token_sums))

    base_grad = base_grad.reshape(cols)
    summed = after_that(summed, up_grad, base_grad, du)
    grad_next = jnp.concatenate([grad_in[1:], shift(grad_in[:1], -1)], 0)
    adapter_term = (1.0 - decay_shift_mix) * grad_in + decay_shift_mix * grad_next
    last = lax.broadcasted_iota(jnp.int32, (rows, 1), 0) == rows - 1
    result = (summed.astype(F32) + adapter_term + jnp.where(last, edge, 0.0)).astype(BF16)
    return (result, down_grad, up_grad, base_grad, du)


def solution(mesh):
    return jax.shard_map(
        per_device,
        mesh=mesh,
        in_specs=(
            P("seq", "head"), P("seq", "head"), P("seq", "head"), P("seq", "head"), P("seq", "head"),
            P("head", None), P("head"), P("head"), P(), P("head", None), P(None, "head"),
            P(None, "seq", "head"),
        ),
        out_specs=(P("seq", "head"), P("head", None), P(None, "head"), P("head"), P("head", None)),
        check_vma=False,
    )
```

```python
import jax
import jax.numpy as jnp
import numpy as np
from jax import lax
from jax.experimental import pallas as pl
from jax.experimental.pallas import tpu as pltpu
from jax.sharding import PartitionSpec as P

F32 = jnp.float32
BF16 = jnp.bfloat16
PAIR = 128
VMEM = 56 * 2**20
NN = (((1,), (0,)), ((), ()))
NT = (((1,), (1,)), ((), ()))
TN = (((0,), (0,)), ((), ()))


def position():
    seq, head = lax.axis_index("seq"), lax.axis_index("head")
    inner = lax.axis_size("seq") // lax.axis_size("head")
    return lax.rem(seq, inner), lax.div(seq, inner), head


def mm(a, b, dims=NN):
    return lax.dot_general(a, b, dims, preferred_element_type=F32)


def halves(a):
    hi = a.astype(BF16)
    return hi, (a - hi.astype(F32)).astype(BF16)


def low_lanes(shape, half):
    return lax.broadcasted_iota(jnp.int32, shape, len(shape) - 1) < half


def block_rows(a, half):
    low = low_lanes(a.shape, half)
    zero = jnp.zeros_like(a)
    return jnp.concatenate([jnp.where(low, a, zero), jnp.where(low, zero, a)], 0)


def fold(a, half):
    rows = a.shape[0] // 2
    return jnp.where(low_lanes((rows, a.shape[1]), half), a[:rows], a[rows:])


def sum_matrix(rows):
    t = np.arange(rows)
    both = np.concatenate([t[:, None] > t[None, :], t[:, None] < t[None, :]], 0)
    return np.concatenate([both, both], 1).astype(np.float32)


def level_matrix(rows):
    t = np.arange(rows)
    parts = []
    m = 1
    while m < rows:
        mid = (t // (2 * m)) * 2 * m + m
        right = t >= mid
        u = t[None, :]
        take_right = (u >= mid[:, None]) & (u < t[:, None])
        take_left = (u > t[:, None]) & (u < mid[:, None])
        parts.append(np.where(right[:, None], take_right, take_left))
        m *= 2
    both = np.concatenate(parts, 0)
    return np.concatenate([both, both], 1).astype(np.float32)


def cumulative_matrix(rows):
    t = np.arange(rows)
    strict = (t[:, None] < t[None, :]).astype(np.float32)
    full = (t[:, None] <= t[None, :]).astype(np.float32)
    return np.concatenate([strict, strict, -full, -full], 1)


def split_rows(a):
    hi, lo = halves(a)
    wide = (4, a.shape[1])
    return jnp.concatenate([jnp.broadcast_to(hi, wide), jnp.broadcast_to(lo, wide)], 0)


def joined(msg, at):
    return msg[at : at + 1].astype(F32) + msg[at + 4 : at + 5].astype(F32)


def mm3(a, b, dims=NN):
    ah, al = halves(a)
    bh, bl = halves(b)
    return mm(ah, bh, dims) + (mm(ah, bl, dims) + mm(al, bh, dims))


def mixed_input(x, carried, mix):
    features = x[...].astype(F32)
    row = lax.broadcasted_iota(jnp.int32, features.shape, 0)
    previous = jnp.where(row == 0, carried[...].astype(F32), pltpu.roll(features, 1, 0))
    return features + mix[...] * (previous - features)


def copy_rows(weights, piece, at, stage, sem):
    rows = pl.ds(at, piece.shape[1])
    into = [pltpu.make_async_copy(weights.at[m, rows], stage.at[m], sem.at[m]) for m in range(3)]
    out = [pltpu.make_async_copy(stage.at[m], piece.at[m], sem.at[3 + m]) for m in range(3)]
    return into, out


def adapter_kernel(x, carried, mix, down, pre):
    pre[...] = mm3(mixed_input(x, carried, mix), down[...])


def decay_kernel(head, count, *refs):
    pres = refs[:count]
    base, up, r, k, v, dy, sums, lora, lora_t, w_out, end, st, msg = refs[count:]
    rows = r.shape[0]
    total = pres[0][...]
    for pre in pres[1:]:
        total = total + pre[...]
    mid = jnp.tanh(total)
    lora[...] = mid
    lora_t[...] = mid.T.astype(BF16)
    w = -jnp.exp(base[...] + mm3(mid, up[...]))
    w_out[...] = w
    hi, lo = halves(w)
    args = mm(sums[...], jnp.concatenate([hi, lo], 0))
    before, after = args[:rows], args[rows:]
    final = before[rows - 1 :] + w[rows - 1 :]
    end[...] = final
    from_start, to_end = jnp.exp(before), jnp.exp(after)
    kf = (k[...].astype(F32) * to_end).astype(BF16)
    rb = (r[...].astype(F32) * from_start).astype(BF16)
    for p in range(r.shape[1] // PAIR):
        cols = slice(p * PAIR, (p + 1) * PAIR)
        state = fold(mm(v[:, cols], kf[:, cols], TN), head)
        st[:, cols] = state
        msg[:head, cols] = state.astype(BF16)
        msg[head : 2 * head, cols] = fold(mm(dy[:, cols], rb[:, cols], TN), head).astype(BF16)
    msg[2 * head :] = split_rows(final)


def pair_kernel(head, ring, own, far, *outs):
    place = position()
    late = place[0] == 1
    dec_own, dec_far = joined(own, 2 * head), joined(far, 2 * head)
    eo, ef = jnp.exp(dec_own), jnp.exp(dec_far)
    st_own, st_far = own[:head].astype(F32), far[:head].astype(F32)
    gt_own, gt_far = own[head : 2 * head].astype(F32), far[head : 2 * head].astype(F32)
    state = jnp.where(late, st_own + eo * st_far, st_far + ef * st_own).astype(BF16)
    grad = jnp.where(late, gt_far + ef * gt_own, gt_own + eo * gt_far).astype(BF16)
    decays = split_rows(dec_own + dec_far)
    for d in range(1, ring):
        out = outs[d - 1]
        ahead = place[1] + d < ring

        @pl.when(ahead)
        def _():
            out[:head] = state

        @pl.when(jnp.logical_not(ahead))
        def _():
            out[:head] = grad

        out[head:] = decays


def inner_kernel(head, skip, r, k, v, dy, w, u, levels, sums, *refs):
    if skip:
        weights, piece, stage, sem = refs[0], refs[8], refs[9], refs[10]
        refs = refs[1:8]
        into, out = copy_rows(weights, piece, skip, stage, sem)
        at_last = pl.program_id(0) == pl.num_programs(0) - 1

        @pl.when(pl.program_id(0) == 0)
        def _():
            for copy in into:
                copy.start()

        @pl.when(at_last)
        def _():
            for first, second in zip(into, out):
                first.wait()
                second.start()

    gr_out, gk_out, gv_out, self_out, eb_out, ee_out, du_out = refs
    rows, width = r.shape
    row = lax.broadcasted_iota(jnp.int32, (rows, PAIR), 0)
    row2 = lax.broadcasted_iota(jnp.int32, (rows, 2 * rows), 0)
    col2 = lax.broadcasted_iota(jnp.int32, (rows, 2 * rows), 1)
    apart = row2 ^ (col2 & (rows - 1))
    lane_r = lax.broadcasted_iota(jnp.int32, (2 * PAIR, PAIR), 0) & (PAIR - 1)
    lane_c = lax.broadcasted_iota(jnp.int32, (2 * PAIR, PAIR), 1)
    ones = jnp.where((lane_r < head) == (lane_c < head), 1.0, 0.0).astype(BF16)
    hi, lo = halves(w[...])
    both = jnp.concatenate([hi, lo], 0)
    decay = jnp.exp(mm(levels[...], both))
    ends = jnp.exp(mm(sums[...], both))
    eb_out[...], ee_out[...] = ends[:rows], ends[rows:]
    for p in range(width // PAIR):
        cols = slice(p * PAIR, (p + 1) * PAIR)
        rf, kf = r[:, cols].astype(F32), k[:, cols].astype(F32)
        vf, dyf = v[:, cols].astype(F32), dy[:, cols].astype(F32)
        dydy = block_rows(dy[:, cols], head)
        pairs = mm(dy[:, cols], block_rows(v[:, cols], head), NT)
        pairs_t = mm(v[:, cols], dydy, NT)
        gr = jnp.zeros((rows, PAIR), F32)
        gk = jnp.zeros((rows, PAIR), F32)
        scores_t = jnp.zeros((rows, 2 * rows), F32)
        m, level = 1, 0
        while m < rows:
            d = decay[level * rows : (level + 1) * rows, cols]
            right = (row & m) != 0
            rd = jnp.where(right, rf * d, 0.0).astype(BF16)
            kd = jnp.where(right, 0.0, kf * d).astype(BF16)
            kk, rr = block_rows(kd, head), block_rows(rd, head)
            near = apart < 2 * m
            a = mm(kd, rr, NT)
            scores_t = scores_t + jnp.where(near, a, 0.0)
            here = jnp.where(near, pairs, 0.0).astype(BF16)
            here_t = jnp.where(near, pairs_t, 0.0).astype(BF16)
            gr = gr + jnp.where(right, d * mm(here, kk), 0.0)
            gk = gk + jnp.where(right, 0.0, d * mm(here_t, rr))
            m, level = 2 * m, level + 1
        sh, sl = halves(dyf * vf)
        own = mm(jnp.concatenate([sh, sl], 1), ones)
        bh, bl = halves(rf * u[:, cols] * kf)
        bonus = mm(jnp.concatenate([bh, bl], 1), ones)
        gr_out[:, cols] = gr
        gk_out[:, cols] = gk
        gv_out[:, cols] = mm(scores_t.astype(BF16), dydy) + bonus * dyf
        self_out[:, cols] = own
        du_out[:, cols] = jnp.sum(rf * kf * own, 0, keepdims=True)
    if skip:

        @pl.when(at_last)
        def _():
            for copy in out:
                copy.wait()


def outer_kernel(
    head, ring, r, k, v, dy, u, gr0, gk0, gv0, own, eb, ee, st, end, far, *refs
):
    place = position()
    msgs = refs[: ring - 1]
    proj, r_gr, k_gk, at_end = refs[ring - 1 :]
    width = r.shape[1]
    late, z = place[0] == 1, place[1]
    zero = jnp.zeros((head, width), F32)
    nothing = jnp.zeros((1, width), F32)
    state, grad, past, future = zero, zero, nothing, nothing
    for d in range(1, ring):
        msg = msgs[d - 1]
        live = d <= z
        state = state + jnp.where(live, jnp.exp(past) * msg[:head].astype(F32), 0.0)
        past = past + jnp.where(live, joined(msg, head), 0.0)
    for d in range(ring - 1, 0, -1):
        msg = msgs[d - 1]
        live = d > z
        grad = grad + jnp.where(live, jnp.exp(future) * msg[:head].astype(F32), 0.0)
        future = future + jnp.where(live, joined(msg, head), 0.0)
    ef = jnp.exp(joined(far, 2 * head))
    st_in = jnp.where(late, far[:head].astype(F32) + ef * state, state)
    gt_in = jnp.where(late, grad, far[head : 2 * head].astype(F32) + ef * grad)
    at_end[...] = jnp.sum(gt_in * (jnp.exp(end[...]) * st_in + st[...]), 0, keepdims=True)
    sb, gb = st_in.astype(BF16), gt_in.astype(BF16)
    for p in range(width // PAIR):
        cols = slice(p * PAIR, (p + 1) * PAIR)
        grads = block_rows(gb[:, cols], head)
        rf, kf = r[:, cols].astype(F32), k[:, cols].astype(F32)
        after = ee[:, cols]
        gr = gr0[:, cols] + eb[:, cols] * mm(dy[:, cols], block_rows(sb[:, cols], head))
        gk = gk0[:, cols] + after * mm(v[:, cols], grads)
        gv = gv0[:, cols] + mm((kf * after).astype(BF16), grads, NT)
        s = own[:, cols] * u[:, cols]
        proj[0, :, cols] = (gr + kf * s).astype(BF16)
        proj[1, :, cols] = (gk + rf * s).astype(BF16)
        proj[2, :, cols] = gv.astype(BF16)
        r_gr[:, cols] = rf * gr
        k_gk[:, cols] = kf * gk


def decay_grad_kernel(w, r_gr, k_gk, at_end, up, lora_t, cums, up_grad, base_grad, mid_grad):
    ah, al = halves(r_gr[...])
    bh, bl = halves(k_gk[...])
    gp = (mm(cums[...], jnp.concatenate([ah, al, bh, bl], 0)) + at_end[...]) * w[...]
    gpb = gp.astype(BF16)
    up_grad[...] = mm(lora_t[...], gpb)
    base_grad[...] = jnp.sum(gp, 0, keepdims=True)
    mid_grad[...] = mm(gpb, up[...].astype(BF16), NT)


def middle_kernel(count, x, carried, mix, down, lora, *refs):
    mids, sides, (keep, send, grad_in) = refs[:count], refs[count:-3], refs[-3:]
    total = mids[0][...]
    for part in mids[1:]:
        total = total + part[...]
    mid = total * (1.0 - lora[...] * lora[...])
    grad_in[...] = mm3(mid, down[...], NT)
    down_grad = mm3(mid.T, mixed_input(x, carried, mix))
    rank, half = mid.shape[1], x.shape[1] // 2
    wide = (8, half)
    late = position()[0] == 1

    def choose(low, high, at, size):
        keep[at : at + size] = jnp.where(late, high, low).astype(BF16)
        send[at : at + size] = jnp.where(late, low, high).astype(BF16)

    up_low, up_high, base_low, base_high, du_low, du_high = [ref[...] for ref in sides]
    choose(up_low, up_high, 0, rank)
    choose(down_grad[:, :half], down_grad[:, half:], rank, rank)
    for at, low, high in ((0, base_low, base_high), (8, du_low, du_high)):
        choose(jnp.broadcast_to(low, wide), jnp.broadcast_to(high, wide), 2 * rank + at, 8)


def finish_kernel(rank, mine, theirs, up, down, base, du):
    late = position()[0] == 1
    half = mine.shape[1]
    a, b = mine[...].astype(F32), theirs[...].astype(F32)
    for at, value in ((0, jnp.where(late, b, a)), (half, jnp.where(late, a, b))):
        here = slice(at, at + half)
        up[:, here] = value[:rank]
        down[here] = value[rank : 2 * rank].T
        for ref, row in ((base, 2 * rank), (du, 2 * rank + 8)):
            size = ref.shape[1]
            for i in range(half // size):
                to = at // size + i
                ref[to : to + 1] = value[row : row + 1, i * size : (i + 1) * size]


def project_kernel(count, ring, final, *refs):
    place = position()
    lows, highs, given, mix = refs[:count], refs[count : 2 * count], refs[2 * count : 2 * count + 2], refs[2 * count + 2]
    rest, (low, high, weights, own, prior, sem) = refs[2 * count + 3 : -6], refs[-6:]
    done, outs = (rest[:-ring], rest[-ring:]) if final else ((), rest)
    rows, width = lows[0].shape[1:]
    n = weights.shape[2]
    copies = []

    def fetch(source, target):
        copy = pltpu.make_async_copy(source, target, sem.at[len(copies)])
        copy.start()
        copies.append(copy)
        return copy

    weight_copies, block_copies = [], []
    for i in range(2):
        for m in range(3):
            weight_copies.append([fetch(given[i].at[m], weights.at[i, m])])
            if i == 0:
                places = [pl.ds(q * rows, rows) for q in range(count)]
                block_copies.append(
                    [fetch(lows[q].at[m], low.at[m, at]) for q, at in enumerate(places)]
                    + [fetch(highs[q].at[m], high.at[m, at]) for q, at in enumerate(places)]
                )

    for i in range(2):
        column = pl.ds(pl.multiple_of((place[0] if i == 0 else 1 - place[0]) * n, n), n)
        for m in range(3):
            for copy in (block_copies[m] if i == 0 else []) + weight_copies[i * 3 + m]:
                copy.wait()
            term = mm(low[m], weights[i, m, :, :width], NT) + mm(high[m], weights[i, m, :, width:], NT)
            later = mix[m : m + 1, column] * term
            own[...] = term - later if m == 0 else own[...] + (term - later)
            prior[...] = later if m == 0 else prior[...] + later
        last = lax.broadcasted_iota(jnp.int32, (rows, n), 0) == rows - 1
        top = lax.broadcasted_iota(jnp.int32, (16, n), 0) == 0

        def store(out, q):
            here = slice(q * rows, (q + 1) * rows)
            part = prior[here]
            moved = jnp.where(last, 0.0, pltpu.roll(part, rows - 1, 0))
            out[:rows, column] = (own[here] + moved).astype(BF16)
            out[rows:, column] = jnp.where(top, part[:16], 0.0).astype(BF16)

        if not final:
            for q in range(count):
                store(outs[q], q)
            continue
        for d in range(ring):
            wanted = lax.rem(place[1] - lax.bitwise_xor(place[2], d) + ring, ring)
            for q in range(ring):

                @pl.when(wanted == q)
                def _():
                    if q == ring - 1:
                        store(outs[d], 0)
                    else:
                        outs[d][:, column] = done[q][:, column]


def per_device(
    layer_input, receptance, key_act, value_act, attention_result_sensitivity, time_first,
    decay_exponent_base, decay_shift_mix, mix_rkv, decay_adapter_down, decay_adapter_up, proj_weights,
):
    rows, cols = layer_input.shape
    heads, head = time_first.shape
    rank = decay_adapter_down.shape[1]
    n_seq, n_head = lax.axis_size("seq"), lax.axis_size("head")
    inner = n_seq // n_head
    ring = n_seq // inner
    pairs = cols // PAIR
    parts = 2
    part_cols = cols // parts
    block = min(part_cols, 2 * PAIR)
    r, k, v, dy = receptance, key_act, value_act, attention_result_sensitivity
    params = pltpu.CompilerParams(vmem_limit_bytes=VMEM)

    def shape(s, t=F32):
        return jax.ShapeDtypeStruct(s, t)

    def work(us):
        return pl.CostEstimate(flops=0, transcendentals=0, bytes_accessed=int(us * 3.5e6))

    def shift(a, distance):
        return lax.ppermute(
            a, "seq", [(i - distance, i) for i in range(n_seq) if 0 <= i - distance < n_seq]
        )

    def around(a, step):
        return lax.ppermute(a, "seq", [(i, (i + inner * step) % n_seq) for i in range(n_seq)])

    def partner(a):
        return lax.ppermute(a, "seq", [(i, i ^ 1) for i in range(n_seq)])

    def head_shift(a, d):
        return lax.ppermute(a, "head", [(i, (i + d) % n_head) for i in range(n_head)])

    def head_parts(a):
        return [a] + [head_shift(a, d) for d in range(1, n_head)]

    def after_that(value, *others):
        return lax.optimization_barrier((value, *others))[0]

    weight_rows = proj_weights.shape[1]
    cut = max(weight_rows * 3 // 256, 1) * 16
    anywhere = pl.BlockSpec(memory_space=pl.ANY)
    vmem = pl.BlockSpec(memory_space=pltpu.VMEM)

    carried = shift(layer_input[rows - 1 :], 1)
    shift_mix = decay_shift_mix.reshape(1, cols)
    pre = pl.pallas_call(
        adapter_kernel,
        out_shape=shape((rows, rank)),
        compiler_params=params,
        cost_estimate=work(1.5),
        name="adapter_input",
    )(layer_input, carried, shift_mix, decay_adapter_down)
    pres = head_parts(pre)

    sums = jnp.asarray(sum_matrix(rows), BF16)
    levels = jnp.asarray(level_matrix(rows), BF16)
    cums = jnp.asarray(cumulative_matrix(rows), BF16)
    far_rows = 2 * head + 8

    lora, lora_t, w, end, st, msg = pl.pallas_call(
        lambda *refs: decay_kernel(head, n_head, *refs),
        out_shape=[
            shape((rows, rank)), shape((rank, rows), BF16), shape((rows, cols)), shape((1, cols)),
            shape((head, cols)), shape((far_rows, cols), BF16),
        ],
        compiler_params=params,
        cost_estimate=work(3),
        name="decay_and_states",
    )(*pres, decay_exponent_base.reshape(1, cols), decay_adapter_up, r, k, v, dy, sums)

    vmem = pl.BlockSpec(memory_space=pltpu.VMEM)
    u = after_that(time_first, msg).reshape(1, cols)

    def col_block(n, width=block, offset=0):
        return pl.BlockSpec((n, width), lambda p, *_: (0, p + offset))

    def whole(s):
        return pl.BlockSpec(s, lambda p, *_: (0,) * len(s))

    steps = part_cols // block
    here = col_block(rows)

    def inside(part):
        at = lambda n: col_block(n, block, part * steps)
        extra = False
        return pl.pallas_call(
            lambda *refs: inner_kernel(head, cut if extra else 0, *refs),
            grid=(steps,),
            in_specs=[at(rows)] * 5 + [at(1), whole(levels.shape), whole(sums.shape)] + [anywhere] * extra,
            out_specs=[here] * 6 + [col_block(1)] + [anywhere] * extra,
            out_shape=[shape((rows, part_cols))] * 6 + [shape((1, part_cols))]
            + [shape((3, weight_rows - cut, cols), BF16)] * extra,
            scratch_shapes=[
                pltpu.VMEM((3, weight_rows - cut, cols), BF16), pltpu.SemaphoreType.DMA((6,)),
            ] * extra,
            compiler_params=params,
            cost_estimate=work(4),
            name="inside_chunk",
        )(r, k, v, dy, w, u, levels, sums, *[proj_weights] * extra)

    inner_parts = [inside(part) for part in range(parts)]
    far, weights, inner_parts[0] = lax.optimization_barrier((partner(msg), proj_weights, inner_parts[0]))
    fars = [partner(weights)]
    out_msgs = pl.pallas_call(
        lambda *refs: pair_kernel(head, ring, *refs),
                out_shape=[shape((head + 8, cols), BF16)] * (ring - 1),
        compiler_params=params,
        cost_estimate=work(1.5),
        name="pair_states",
    )(msg, far)
    msgs = [around(m, d + 1) for d, m in enumerate(out_msgs)]

    inner_parts[1], msgs = lax.optimization_barrier((inner_parts[1], msgs))
    outer = []
    for part in range(parts):
        at = lambda n: col_block(n, block, part * steps)
        outer.append(
            pl.pallas_call(
                lambda *refs: outer_kernel(head, ring, *refs),
                grid=(steps,),
                in_specs=[at(rows)] * 4 + [at(1)] + [here] * 6
                + [at(head), at(1), at(far_rows)] + [at(head + 8)] * (ring - 1),
                out_specs=[pl.BlockSpec((3, rows, block), lambda p: (0, 0, p)), here, here, col_block(1)],
                out_shape=[
                    shape((3, rows, part_cols), BF16), shape((rows, part_cols)),
                    shape((rows, part_cols)), shape((1, part_cols)),
                ],
                compiler_params=params,
                cost_estimate=work(3),
                name="across_chunks",
            )(r, k, v, dy, u, *inner_parts[part][:6], st, end, far, *msgs)
        )
    projs = [o[0] for o in outer]

    ups, bases, mid_parts = [], [], []
    for part in range(parts):
        at = lambda n: pl.BlockSpec((n, part_cols), lambda p: (0, part))
        up_grad, base_grad, mid_grad = pl.pallas_call(
            decay_grad_kernel,
            grid=(1,),
            in_specs=[at(rows), *[whole((rows, part_cols))] * 2, whole((1, part_cols)), at(rank)]
            + [whole((rank, rows)), whole(cums.shape)],
            out_specs=[whole((rank, part_cols)), whole((1, part_cols)), whole((rows, rank))],
            out_shape=[shape((rank, part_cols)), shape((1, part_cols)), shape((rows, rank))],
            compiler_params=params,
            cost_estimate=work(2),
            name="decay_gradient",
        )(w, *outer[part][1:], decay_adapter_up, lora_t, cums)
        ups.append(up_grad)
        bases.append(base_grad)
        mid_parts.append(mid_grad)
    mid_grad = sum(mid_parts)

    mids = head_parts(mid_grad)
    dus = [part[6] for part in inner_parts]
    keep, send, grad_in = pl.pallas_call(
        lambda *refs: middle_kernel(n_head, *refs),
        in_specs=[vmem] * (5 + n_head + 3 * parts),
        out_shape=[shape((2 * rank + 16, part_cols), BF16)] * 2 + [shape((rows, cols))],
        compiler_params=params,
        cost_estimate=work(3),
        name="adapter_grads",
    )(
        layer_input, carried, shift_mix, decay_adapter_down, lora, *mids, *ups, *bases, *dus
    )

    lows, highs = [projs[0]], [projs[1]]
    for step in range(ring - 1):
        low, high = lows[-1], highs[-1]
        lows.append(around(after_that(low, mid_grad) if step == 1 else low, 1))
        highs.append(around(after_that(high, keep) if step == 1 else high, 1))

    def add(a, b):
        return (a.astype(F32) + b.astype(F32)).astype(BF16)

    got = partner(after_that(send, lows[2]))

    mix_here = lax.dynamic_slice_in_dim(after_that(mix_rkv, *out_msgs), position()[1] * cols, cols, 1)

    tall = rows + 16

    def project(low, high, done=()):
        count, final = len(low), len(done) > 0
        return pl.pallas_call(
            lambda *refs: project_kernel(count, ring, final, *refs),
            in_specs=[anywhere] * (2 * count + 2) + [vmem] * (1 + len(done)),
            out_shape=[shape((tall, cols), BF16)] * (ring if final else count),
            scratch_shapes=[
                pltpu.VMEM((3, count * rows, part_cols), BF16),
                pltpu.VMEM((3, count * rows, part_cols), BF16),
                pltpu.VMEM((inner, 3, weight_rows, cols), BF16),
                pltpu.VMEM((count * rows, weight_rows), F32),
                pltpu.VMEM((count * rows, weight_rows), F32),
                pltpu.SemaphoreType.DMA((3 * (2 * count + 2),)),
            ],
            compiler_params=pltpu.CompilerParams(vmem_limit_bytes=24 * 2**20),
            cost_estimate=work(5),
            name="projections",
        )(*low, *high, proj_weights, *fars, mix_here, *done)

    done = project(lows[:-1], highs[:-1])
    sends = project(lows[-1:], highs[-1:], done)
    token_sums = add(keep, after_that(got, *done))
    def other_z(a, b):
        route = [(i, ((i // inner) ^ b) * inner + i % inner) for i in range(n_seq)]
        return lax.ppermute(a, "seq", route)

    token_sums = add(token_sums, after_that(other_z(token_sums, 1), sends))
    def across(a, bit):
        return lax.ppermute(a, "head", [(i, i ^ bit) for i in range(n_head)])

    left, bit = dict(enumerate(sends)), 1
    while bit < n_head:
        came = {e: across(left[e | bit], bit) for e in left if not e & bit}
        if bit == 1:
            came = {e: after_that(value, token_sums) for e, value in came.items()}
        left = {e: left[e].astype(F32) + came[e].astype(F32) for e in came}
        bit *= 2
        if bit < n_head:
            left = {e: value.astype(BF16) for e, value in left.items()}
    total = left[0]
    swap, back = [], []
    for h in range(n_head):
        for z in range(ring):
            for x in range(inner):
                source = h * n_seq + z * inner + x
                block_at = h * inner + x
                swap.append((source, z * n_seq + block_at))
                if block_at > 0:
                    back.append((source, z * n_seq + block_at - 1))
    summed = lax.ppermute(total[:rows].astype(BF16), ("head", "seq"), swap)
    edge = lax.ppermute(total[rows : rows + 1], ("head", "seq"), back)
    b = 2
    while b < ring:
        got = other_z(token_sums, b)
        token_sums = add(token_sums, after_that(got, edge) if b == 2 else got)
        b *= 2
    up_grad, down_grad, base_grad, du = pl.pallas_call(
        lambda *refs: finish_kernel(rank, *refs),
                out_shape=[shape((rank, cols)), shape((cols, rank)), shape((pairs, PAIR)), shape((heads, head))],
        compiler_params=pltpu.CompilerParams(vmem_limit_bytes=16 * 2**20),
        cost_estimate=work(2),
        name="token_sums",
    )(token_sums, partner(token_sums))

    base_grad = base_grad.reshape(cols)
    summed = after_that(summed, up_grad, base_grad, du)
    grad_next = jnp.concatenate([grad_in[1:], shift(grad_in[:1], -1)], 0)
    adapter_term = (1.0 - decay_shift_mix) * grad_in + decay_shift_mix * grad_next
    last = lax.broadcasted_iota(jnp.int32, (rows, 1), 0) == rows - 1
    result = (summed.astype(F32) + adapter_term + jnp.where(last, edge, 0.0)).astype(BF16)
    return (result, down_grad, up_grad, base_grad, du)


def solution(mesh):
    return jax.shard_map(
        per_device,
        mesh=mesh,
        in_specs=(
            P("seq", "head"), P("seq", "head"), P("seq", "head"), P("seq", "head"), P("seq", "head"),
            P("head", None), P("head"), P("head"), P(), P("head", None), P(None, "head"),
            P(None, "seq", "head"),
        ),
        out_specs=(P("seq", "head"), P("head", None), P(None, "head"), P("head"), P("head", None)),
        check_vma=False,
    )
```
